768 devices in a mesh: row: 16 (over x_lo, y), col: 48 (over x_hi, z, core).
Axes of the slice: x: 4 (x_hi: 2, x_lo: 2; x = x_hi * 2 + x_lo), y: 8, z: 12, core: 2. Of those that a mesh axis runs over, the one named last changes fastest.
Arguments:
- a_own_values: bfloat16 [16, 48, 16, 1, 128, 128], P('row', 'col'), may hold values from -1.5 to 1.5
- a_own_code: int32 [16, 48, 16, 1], P('row', 'col'), may hold values from -1 to 2303, as said below
- b_own_values: bfloat16 [16, 48, 16, 1, 128, 128], P('row', 'col'), may hold values from -0.5 to 0.5
- b_own_code: int32 [16, 48, 16, 1], P('row', 'col'), may hold values from -1 to 767, as said below
- c_code: int32 [16, 48, 12], P('row', 'col'), may hold values from 0 to 767, as said below
Outputs:
- product: bfloat16 [16, 48, 12, 128, 128], P('row', 'col')
The draws below stay inside these ranges and needn't reach their ends.
Inputs may be any that keep to these rules, and one draw needn't show every extreme that they name: `a_own_code`: entry [r, c, s, q] is the code of the q-th block that owner c of block row group r holds for panel (r, s) of A: i * 48 + k for block (i, k), or -1 for an unused entry. Live codes of one panel are distinct. In every draw some panel has all 48 entries live. `b_own_code`: entry [r, c, s, q] is the code of the q-th block that owner r holds for panel (s, c) of B: k * 16 + j for block (k, j), or -1 for an unused entry. Live codes of one panel are distinct. No block row of a panel holds more than 2 live blocks; in every draw some panel has all 16 entries live and some block row holds exactly 2. `c_code`: each grid position keeps 12 distinct blocks (i, j), coded i * 16 + j, with i < 48. Every product of a live block (i, k) of A's panel (r, s) with a live block (k, j) of B's panel (s, c), for the panels that meet at (r, c) within the window, falls on a kept block.
All inputs are finite; a program needn't handle non-finite values.
Results may differ from the reference program's by a relative error of at most 0.001.
Values may be sent and summed in bfloat16 or wider, within the bound.
No kernel may reach another device: no remote copies, remote signals or barrier semaphores. Data moves between devices by JAX's collectives and lax.ppermute only.
A program may use at most 64 MiB of HBM per device.

```python
import jax
import jax.numpy as jnp
from jax import lax

BLK = 128
BC = 16
STEPS = 3
BROW = 2
ACAP = 48
BCAP = 16
CS = 12
BR = 48
BK = 48
SA = 1
SB = 1
N_ROW = 16
N_COL = 48


def thin_out(key, candidates):
    count_panels = candidates.shape[0]
    capacity = candidates.shape[1]
    key_mix, key_count, key_full, key_place = jax.random.split(key, 4)
    mixed = jax.vmap(lambda sub_key, line: jax.random.permutation(sub_key, line))(jax.random.split(key_mix, count_panels), candidates)
    target = jax.random.randint(key_count, (count_panels,), (capacity + 2) // 3, capacity + 1)
    fullest = jax.random.randint(key_full, (), 0, count_panels)
    target = target.at[fullest].set(capacity)
    positions = jnp.arange(capacity, dtype=jnp.int32)[None, :]
    codes = jnp.where(positions < target[:, None], mixed, -1).astype(jnp.int32)
    placing = jax.vmap(lambda sub_key: jax.random.permutation(sub_key, capacity))(jax.random.split(key_place, count_panels))
    return jnp.take_along_axis(codes, placing, axis=1).astype(jnp.int32)


def patterns(key):
    inner_count = BCAP // BROW
    row_count_set = ACAP // inner_count
    key_rows, key_inner, key_cols, key_left, key_right, key_keep = jax.random.split(key, 6)
    row_sets = jax.vmap(lambda sub_key: jax.random.permutation(sub_key, BR)[:row_count_set])(jax.random.split(key_rows, N_ROW)).astype(jnp.int32)
    inner_sets = jax.vmap(lambda sub_key: jax.random.permutation(sub_key, BK)[:inner_count])(jax.random.split(key_inner, N_ROW)).astype(jnp.int32)
    col_sets = jax.vmap(lambda sub_key: jax.random.permutation(sub_key, BC)[:BROW])(jax.random.split(key_cols, N_COL)).astype(jnp.int32)
    left_cand = (row_sets[:, None, :, None] * BK + inner_sets[None, :, None, :]).reshape(N_ROW * N_ROW, ACAP)
    right_cand = (inner_sets[:, None, :, None] * BC + col_sets[None, :, None, :]).reshape(N_ROW * N_COL, BCAP)
    kept = (row_sets[:, None, :, None] * BC + col_sets[None, :, None, :]).reshape(N_ROW * N_COL, CS)
    kept = jax.vmap(lambda sub_key, line: jax.random.permutation(sub_key, line))(jax.random.split(key_keep, N_ROW * N_COL), kept)
    kept = kept.reshape(N_ROW, N_COL, CS).astype(jnp.int32)
    left_lists = thin_out(key_left, left_cand)
    right_lists = thin_out(key_right, right_cand)
    left_owned = left_lists.reshape(N_ROW, N_ROW, N_COL, ACAP // N_COL).transpose(0, 2, 1, 3)
    right_owned = right_lists.reshape(N_ROW, N_COL, N_ROW, BCAP // N_ROW).transpose(2, 1, 0, 3)
    return (left_owned, right_owned, kept)


def draw_a_own_code(key, part):
    shared = patterns(key)
    return shared[0]


def draw_b_own_code(key, part):
    shared = patterns(key)
    return shared[1]


def draw_c_code(key, part):
    shared = patterns(key)
    return shared[2]


def steps_of(stream_key, extent, shards, smallest, largest):
    def one(dim, shards_of):
        steps = jax.random.uniform(jax.random.fold_in(jax.random.fold_in(stream_key, 6), dim), (shards_of,), jnp.float32, smallest / len(shards), largest / len(shards))
        return jnp.repeat(jnp.exp(steps), extent[dim] // shards_of).reshape((-1,) + (1,) * (len(extent) - dim - 1))

    gain = one(*shards[0])
    for cut in shards[1:]:
        gain = gain * one(*cut)
    return gain


def noise(own_key, extent, deviation, limit, cuts=(), held_as=jnp.bfloat16):
    values = jax.random.normal(own_key, extent, jnp.float32) * deviation
    if len(cuts) > 0:
        values = steps_of(own_key, extent, cuts, -0.22, 0.18) * values
    return jnp.clip(values, min=-limit, max=limit).astype(held_as)


def setup_inputs(seed: int = 0) -> dict:
    streams_of = jax.random.split(jax.random.key(seed), 6)
    a_own_values = noise(streams_of[0], (N_ROW, N_COL, N_ROW, SA, BLK, BLK), 0.25, 1.5, ((0, 16), (1, 48)))
    a_own_code = draw_a_own_code(jax.random.fold_in(streams_of[5], 71), 0)
    b_own_values = noise(streams_of[2], (N_ROW, N_COL, N_ROW, SB, BLK, BLK), BLK ** -0.5, 0.5, ((0, 16), (1, 48)))
    b_own_code = draw_b_own_code(jax.random.fold_in(streams_of[5], 71), 0)
    c_code = draw_c_code(jax.random.fold_in(streams_of[5], 71), 0)
    return dict(a_own_values=a_own_values, a_own_code=a_own_code, b_own_values=b_own_values, b_own_code=b_own_code, c_code=c_code)


def reference(a_own_values, a_own_code, b_own_values, b_own_code, c_code):
    col_ratio = N_COL // N_ROW
    panel_width = BC * col_ratio

    def one_device(device_number):
        grid_row = device_number // N_COL
        grid_col = device_number % N_COL
        slot_codes = c_code[grid_row, grid_col]
        running = jnp.zeros((CS, BLK, BLK), jnp.float32)
        for step_number in range(STEPS):
            slab_number = (grid_row + grid_col + step_number) % N_ROW
            left_blocks = a_own_values[grid_row, :, slab_number].reshape(ACAP, BLK, BLK).astype(jnp.float32)
            left_codes = a_own_code[grid_row, :, slab_number].reshape(ACAP)
            right_blocks = b_own_values[:, grid_col, slab_number].reshape(BCAP, BLK, BLK).astype(jnp.float32)
            right_codes = b_own_code[:, grid_col, slab_number].reshape(BCAP)
            left_live = left_codes >= 0
            right_live = right_codes >= 0
            left_rows = left_codes // panel_width
            left_inner = left_codes % panel_width
            right_inner = right_codes // BC
            right_cols = right_codes % BC
            matching = left_live[:, None] & right_live[None, :] & (left_inner[:, None] == right_inner[None, :])
            ranking = jnp.cumsum(matching.astype(jnp.int32), axis=1) - 1
            target = left_rows[:, None] * BC + right_cols[None, :]
            kept_hit = (target[:, :, None] == slot_codes[None, None, :]).astype(jnp.float32)
            for rank_number in range(BROW):
                select = (matching & (ranking == rank_number)).astype(jnp.float32)
                partner = jnp.einsum("ab,bjk->ajk", select, right_blocks, precision=lax.Precision.HIGHEST)
                pieces = jnp.einsum("aij,ajk->aik", left_blocks, partner, precision=lax.Precision.HIGHEST)
                landing = jnp.einsum("ab,abp->ap", select, kept_hit, precision=lax.Precision.HIGHEST)
                running = running + jnp.einsum("ap,aik->pik", landing, pieces, precision=lax.Precision.HIGHEST)
        return running

    result = lax.map(one_device, jnp.arange(N_ROW * N_COL, dtype=jnp.int32))
    return result.reshape(N_ROW, N_COL, CS, BLK, BLK).astype(jnp.bfloat16)
```

```python
import functools

import jax
import jax.numpy as jnp
from jax import lax
from jax.experimental import pallas as pl
from jax.experimental.pallas import tpu as pltpu
from jax.sharding import Mesh
from jax.sharding import PartitionSpec as P

AXES = ("xl", "y", "xh", "z", "core")
ROW = ("xl", "y")
COL = ("xh", "z", "core")
SIZES = (2, 8, 2, 12, 2)
NZ = 12
BC = 16
PANEL = 48
STEPS = 3
KEPT = 12
BLK = 128

GROUPS = (
    (((0, 0), (1, 1), (3, -1), (2, -2)), ((1, 0), (2, 1), (3, 2), (0, -1))),
    (((2, 2), (3, 3), (1, -3)), ((0, 3), (3, -2), (2, -3))),
    (((0, -4), (3, -5)), ((1, 4), (2, 5))),
    (((1, 5), (2, 6), (0, 4)), ((1, -4), (3, -6), (0, -5))),
)


def rot(distance):
    return [(i, (i + distance) % NZ) for i in range(NZ)]


def shifted(block, distance):
    return lax.ppermute(block, "z", rot(distance))


def shifted_across(block, distance):
    route = [
        (h * NZ + i, (1 - h) * NZ + (i + distance) % NZ) for h in range(2) for i in range(NZ)
    ]
    return lax.ppermute(block, ("xh", "z"), route)


def copy_blocks_kernel(order, outs_of, index_ref, src_ref, *rest):
    outs, sems = rest[: len(outs_of)], rest[len(outs_of)]
    copies = []
    at = 0
    for out, count in zip(outs, outs_of, strict=True):
        for n in range(count):
            copies.append(
                pltpu.make_async_copy(
                    src_ref.at[pl.ds(index_ref[order[at]], 1)], out.at[pl.ds(n, 1)], sems.at[at]
                )
            )
            at += 1
    for copy in copies:
        copy.start()
    for copy in copies:
        copy.wait()


def copy_blocks(src, index, order, outs_of):
    total = sum(outs_of)
    return pl.pallas_call(
        functools.partial(copy_blocks_kernel, order, outs_of),
        out_shape=[jax.ShapeDtypeStruct((n, BLK, BLK), src.dtype) for n in outs_of],
        in_specs=[
            pl.BlockSpec(memory_space=pltpu.SMEM),
            pl.BlockSpec(memory_space=pl.ANY),
        ],
        out_specs=[pl.BlockSpec(memory_space=pl.ANY) for _ in outs_of],
        scratch_shapes=[pltpu.SemaphoreType.DMA((total,))],
        cost_estimate=pl.CostEstimate(
            flops=0, bytes_accessed=2 * total * BLK * BLK * 2, transcendentals=0
        ),
    )(index, src)


def product_kernel(counts, table_ref, b_ref, *rest):
    lefts, out_ref, acc = rest[: len(counts)], rest[len(counts)], rest[len(counts) + 1]
    acc[...] = jnp.zeros_like(acc)
    base = 0
    for left, count in zip(lefts, counts, strict=True):

        def body(n, carry, left=left, base=base):
            block = left[n]
            for rank in range(2):
                place = table_ref[2 * rank + 1, base + n]
                right = b_ref[table_ref[2 * rank, base + n]]
                acc[place] += jnp.dot(block, right, preferred_element_type=jnp.float32)
            return carry

        lax.fori_loop(0, count, body, 0, unroll=6)
        base += count
    out_ref[...] = acc[:KEPT].astype(out_ref.dtype)


def product(table, right, lefts):
    counts = tuple(left.shape[0] for left in lefts)
    total = sum(counts)
    return pl.pallas_call(
        functools.partial(product_kernel, counts),
        out_shape=jax.ShapeDtypeStruct((KEPT, BLK, BLK), jnp.bfloat16),
        in_specs=[pl.BlockSpec(memory_space=pltpu.SMEM)]
        + [pl.BlockSpec(memory_space=pltpu.VMEM)] * (1 + len(lefts)),
        out_specs=pl.BlockSpec(memory_space=pltpu.VMEM),
        scratch_shapes=[pltpu.VMEM((KEPT + 1, BLK, BLK), jnp.float32)],
        compiler_params=pltpu.CompilerParams(vmem_limit_bytes=32 << 20),
        cost_estimate=pl.CostEstimate(
            flops=total * 4 * BLK**3, bytes_accessed=total * BLK * BLK * 2, transcendentals=0
        ),
    )(table, right, *lefts)


def tables(a_code, b_code, c_code, r, z, h, core):
    a_all = lax.all_gather(a_code, COL).reshape(2, NZ, 2, 16)
    b_all = lax.all_gather(b_code, ROW)
    c = 24 * h + 2 * z + core
    a_cyc = jnp.concatenate([a_all, a_all], axis=3)
    mine = lax.dynamic_slice_in_dim(a_cyc, (r + 24 * h + 2 * z) % 16, 4, 3)
    mine = jnp.concatenate([mine, mine], axis=1)[:, ::-1]
    mine = lax.dynamic_slice_in_dim(mine, NZ - 1 - z, NZ, 1)
    mine = jnp.where(h == 0, mine, mine[::-1])
    mine = jnp.where(core == 0, mine, mine[:, :, ::-1])
    b_cyc = jnp.concatenate([b_all, b_all], axis=1)
    right = lax.dynamic_slice_in_dim(b_cyc, (r + c) % 16, STEPS, 1).T
    is0 = core == 0
    steps = jnp.stack(
        [jnp.where(is0, 1, 0), jnp.where(is0, 2, 1), jnp.where(is0, 0, 2)]
    )
    right = jnp.stack(
        [
            jnp.where(is0, right[1], right[0]),
            jnp.where(is0, right[2], right[1]),
            jnp.where(is0, right[0], right[2]),
        ]
    )
    codes, slots = [], []
    for low, high in GROUPS:
        for other in range(2):
            for half in range(2):

                def pick(items, panel):
                    return [mine[half, d % NZ, other, panel] for _, d in items]

                codes += pick(low, 1) + pick(high, 2)
                codes += [
                    jnp.where(is0, x, y) for x, y in zip(pick(low, 0), pick(high, 3), strict=True)
                ]
                slots += [0] * len(low) + [1] * len(low) + [2] * len(low)
    codes = jnp.stack(codes)
    count = codes.shape[0]
    which = jnp.array(slots, jnp.int32)
    one_hot = which[:, None] == jnp.arange(3)[None, :]
    right_live = right >= 0
    right_inner = jnp.where(right_live, right // BC, -1)
    right_col = right % BC
    owners = jnp.arange(16, dtype=jnp.int32)
    earlier = owners[None, :] < owners[:, None]
    rank = jnp.sum(
        ((right_inner[:, :, None] == right_inner[:, None, :]) & earlier[None]).astype(jnp.int32),
        axis=2,
    )
    packed = right_inner * 1024 + rank * 32 + right_col
    packed = jnp.where(right_live, packed, -1)

    def of_slot(x):
        return jnp.sum(jnp.where(one_hot[:, :, None], x[None], 0), axis=1)

    right_n = of_slot(packed)
    live_n = right_n >= 0
    step_n = jnp.sum(jnp.where(one_hot, steps[None, :], 0), axis=1)
    left_live = codes >= 0
    left_row = codes // PANEL
    left_inner = codes % PANEL
    match = live_n & left_live[:, None] & ((right_n // 1024) == left_inner[:, None])
    rows = []
    for rank_number in range(2):
        hit = match & ((right_n // 32) % 32 == rank_number)
        valid = jnp.any(hit, axis=1)
        owner = jnp.sum(jnp.where(hit, owners[None, :], 0), axis=1)
        column = jnp.sum(jnp.where(hit, right_n % 32, 0), axis=1)
        target = left_row * BC + column
        found = (target[:, None] == c_code[None, :]) & valid[:, None]
        place = jnp.sum(jnp.where(found, jnp.arange(KEPT)[None, :] - KEPT, 0), axis=1) + KEPT
        rows += [owner * STEPS + step_n, place]
    return jnp.stack(rows).astype(jnp.int32).reshape(4, count)


def local(a_own_values, a_own_code, b_own_values, b_own_code, c_code):
    r = lax.axis_index(ROW)
    h = lax.axis_index("xh")
    z = lax.axis_index("z")
    core = lax.axis_index("core")
    is0 = core == 0
    c = 24 * h + 2 * z + core
    a_own = a_own_values.reshape(16, BLK, BLK)
    b_own = b_own_values.reshape(16, BLK, BLK)

    cyc = (r + 2 * z + jnp.arange(8, dtype=jnp.int32)) % 8
    a_index = jnp.concatenate([cyc, cyc + 8])
    order = tuple(e * 8 + 2 * a + b for a in (1, 2, 3, 0) for b in range(2) for e in range(2))
    first, second = copy_blocks(a_own, a_index, order, (8, 8))
    b_index = (c + jnp.arange(18, dtype=jnp.int32)) % 16
    b_order = tuple(n + t for n in range(16) for t in range(STEPS))
    (b_send,) = copy_blocks(b_own, b_index, b_order, (48,))

    items = {}

    def keep(moved, names):
        moved = moved.reshape(len(names), 2, 2, BLK, BLK)
        for n, name in enumerate(names):
            items[name] = moved[n]

    def joined(names):
        return jnp.stack([items[name] for name in names])

    keep(first, ((1, 0), (2, 0)))
    keep(second, ((3, 0), (0, 0)))
    up1 = shifted(first, 1)
    down1 = shifted(second, -1)
    up2 = shifted(second, 2)
    down2 = shifted(first, -2)
    right = lax.all_to_all(b_send.reshape(16, STEPS, BLK, BLK), ROW, 0, 0, tiled=True)
    right = right.reshape(48, BLK, BLK)
    keep(up1, ((1, 1), (2, 1)))
    keep(down1, ((3, -1), (0, -1)))
    keep(up2, ((3, 2), (0, 2)))
    keep(down2, ((1, -2), (2, -2)))
    keep(shifted(joined(((2, 1), (3, 2), (0, 2))), 1), ((2, 2), (3, 3), (0, 3)))
    keep(shifted(joined(((3, -1), (2, -2), (1, -2))), -1), ((3, -2), (2, -3), (1, -3)))
    keep(shifted(joined(((1, 1), (2, 2))), 3), ((1, 4), (2, 5)))
    keep(shifted(joined(((0, -1), (3, -2))), -3), ((0, -4), (3, -5)))

    def half_of(place):
        return [(r + 24 * h + 2 * (place % NZ) + w) % 16 // 8 for w in range(4)]

    def chosen(names, e):
        return jnp.stack(
            [jnp.where(e[b] == 0, items[name][b, 0], items[name][b, 1]) for name in names for b in range(2)]
        )

    def flipped(e):
        return [1 - x for x in e]

    lefts = []
    for number, (low, high) in enumerate(GROUPS):
        n = len(low)
        if number < 3:
            e = half_of(z)
            own = jnp.concatenate([chosen(low, e[:2]), chosen(high, e[2:])])
            out = jnp.concatenate(
                [chosen(low, flipped(e[:2])), chosen(high, flipped(e[2:]))]
            )
            other = lax.ppermute(out, "xh", [(0, 1), (1, 0)])
        else:
            e = half_of(z + 1)[:2]
            before = ((1, 4), (2, 5), (0, 3))
            own_low = shifted(chosen(before, e), 1)
            other_low = shifted_across(chosen(before, flipped(e)), 1)
            e = half_of(z - 1)[2:]
            before = ((1, -3), (3, -5), (0, -4))
            own_high = shifted(chosen(before, e), -1)
            other_high = shifted_across(chosen(before, flipped(e)), -1)
            own = jnp.concatenate([own_low, own_high])
            other = jnp.concatenate([other_low, other_high])
        kept, sent = [], []
        for part in (own, other):
            part = part.reshape(2, n, 2, BLK, BLK)
            low0, low1, high2, high3 = part[0, :, 0], part[0, :, 1], part[1, :, 0], part[1, :, 1]
            kept += [low1, high2, jnp.where(is0, low0, high3)]
            sent += [low1, high2, jnp.where(is0, high3, low0)]
        kept, sent = jnp.concatenate(kept), jnp.concatenate(sent)
        lefts += [kept, lax.ppermute(sent, "core", [(0, 1), (1, 0)])]

    table = tables(a_own_code.reshape(16), b_own_code.reshape(16), c_code.reshape(KEPT), r, z, h, core)
    return product(table, right, lefts)[None, None]


def solution(mesh):
    fine = Mesh(mesh.devices.reshape(SIZES), AXES)
    return jax.shard_map(
        local,
        mesh=fine,
        in_specs=(
            P(ROW, COL, None, None, None, None),
            P(ROW, COL, None, None),
            P(ROW, COL, None, None, None, None),
            P(ROW, COL, None, None),
            P(ROW, COL, None),
        ),
        out_specs=P(ROW, COL, None, None, None),
        check_vma=False,
    )
```

```python
import functools

import jax
import jax.numpy as jnp
import numpy as np
from jax import lax
from jax.experimental import pallas as pl
from jax.experimental.pallas import tpu as pltpu
from jax.sharding import Mesh
from jax.sharding import PartitionSpec as P

AXES = ("xl", "y", "xh", "z", "core")
ROW = ("xl", "y")
COL = ("xh", "z", "core")
SIZES = (2, 8, 2, 12, 2)
NZ = 12
BC = 16
PANEL = 48
STEPS = 3
KEPT = 12
BLK = 128

GROUPS = (
    (((0, 0), (1, 1), (3, -1), (2, -2)), ((1, 0), (2, 1), (3, 2), (0, -1))),
    (((2, 2), (3, 3), (1, -3)), ((0, 3), (3, -2), (2, -3))),
    (((0, -4), (3, -5)), ((1, 4), (2, 5))),
    (((1, 5), (2, 6), (0, 4)), ((1, -4), (3, -6), (0, -5))),
)


def rot(distance):
    return [(i, (i + distance) % NZ) for i in range(NZ)]


def shifted(block, distance):
    return lax.ppermute(block, "z", rot(distance))


def shifted_across(block, distance):
    route = [
        (h * NZ + i, (1 - h) * NZ + (i + distance) % NZ) for h in range(2) for i in range(NZ)
    ]
    return lax.ppermute(block, ("xh", "z"), route)


VMEM = pltpu.VMEM
SMEM_SPEC = pl.BlockSpec(memory_space=pltpu.SMEM)
VMEM_SPEC = pl.BlockSpec(memory_space=pltpu.VMEM)
LIMIT = pltpu.CompilerParams(vmem_limit_bytes=40 << 20)


def moves(blocks):
    return pl.CostEstimate(flops=0, bytes_accessed=2 * blocks * BLK * BLK * 2, transcendentals=0)


def block_shape(blocks):
    return jax.ShapeDtypeStruct((blocks, BLK, BLK), jnp.bfloat16)


def ordered_kernel(orders, index_ref, src_ref, *outs):
    for out, order in zip(outs, orders, strict=True):
        for n, place in enumerate(order):
            out[n] = src_ref[index_ref[place]]


def ordered(src, index, orders):
    return pl.pallas_call(
        functools.partial(ordered_kernel, orders),
        out_shape=[block_shape(len(order)) for order in orders],
        in_specs=[SMEM_SPEC, VMEM_SPEC],
        out_specs=[VMEM_SPEC for _ in orders],
        compiler_params=LIMIT,
        cost_estimate=moves(sum(len(order) for order in orders)),
    )(index, src)


def right_kernel(index_ref, src_ref, code_ref, out):
    for n in range(16):
        for t in range(STEPS):
            out[n, pl.ds(t * BLK, BLK), :] = src_ref[index_ref[n + t]]
        out[n, pl.ds(STEPS * BLK, 16), :] = code_ref[n]


def right_packed(src, index, codes):
    return pl.pallas_call(
        right_kernel,
        out_shape=jax.ShapeDtypeStruct((16, STEPS * BLK + 16, BLK), jnp.bfloat16),
        in_specs=[SMEM_SPEC, VMEM_SPEC, VMEM_SPEC],
        out_specs=VMEM_SPEC,
        compiler_params=LIMIT,
        cost_estimate=moves(48),
    )(index, src, codes)


def pack_kernel(spec, count, pick_ref, *refs):
    sources, outs = refs[:count], refs[count:]

    def copy(out, n, entry):
        source, block, pick, sign = entry
        place = block if pick is None else block + sign * pick_ref[pick]
        out[n] = sources[source][place]

    for out, entries in zip(outs, spec, strict=True):
        for n, (zero, one) in enumerate(entries):
            if zero == one:
                copy(out, n, zero)
    differ = any(zero != one for entries in spec for zero, one in entries)
    if differ:
        for core in range(2):

            @pl.when(pick_ref[4] == core)
            def _(core=core):
                for out, entries in zip(outs, spec, strict=True):
                    for n, pair in enumerate(entries):
                        if pair[0] != pair[1]:
                            copy(out, n, pair[core])


def pack(pick, sources, spec):
    return pl.pallas_call(
        functools.partial(pack_kernel, spec, len(sources)),
        out_shape=[block_shape(len(entries)) for entries in spec],
        in_specs=[SMEM_SPEC] + [VMEM_SPEC] * len(sources),
        out_specs=[VMEM_SPEC for _ in spec],
        compiler_params=LIMIT,
        cost_estimate=moves(sum(len(entries) for entries in spec)),
    )(pick, *sources)


def product_kernel(counts, base, first, last, table_ref, right_ref, *rest):
    lefts, rest = rest[: len(counts)], rest[len(counts) :]
    if last:
        before, out_ref, acc = rest
        acc[...] = before[...]
    elif first:
        (acc,) = rest
        acc[...] = jnp.zeros_like(acc)
    else:
        before, acc = rest
        acc[...] = before[...]
    for left, count in zip(lefts, counts, strict=True):

        def body(n, carry, left=left, base=base):
            block = left[n]
            for rank in range(2):
                owner = table_ref[3 * rank, base + n]
                row = pl.multiple_of(table_ref[3 * rank + 1, base + n], BLK)
                place = table_ref[3 * rank + 2, base + n]
                right = right_ref[owner, pl.ds(row, BLK), :]
                acc[place] += jnp.dot(block, right, preferred_element_type=jnp.float32)
            return carry

        lax.fori_loop(0, count, body, 0, unroll=6)
        base += count
    if last:
        out_ref[...] = acc[:KEPT].astype(out_ref.dtype)


def product(table, right, lefts, base, before=None, last=False):
    counts = tuple(left.shape[0] for left in lefts)
    total = sum(counts)
    sums = jax.ShapeDtypeStruct((KEPT + 1, BLK, BLK), jnp.float32)
    return pl.pallas_call(
        functools.partial(product_kernel, counts, base, before is None, last),
        out_shape=block_shape(KEPT) if last else sums,
        in_specs=[SMEM_SPEC] + [VMEM_SPEC] * (1 + len(lefts) + (before is not None)),
        out_specs=VMEM_SPEC,
        scratch_shapes=[VMEM(sums.shape, jnp.float32)] if last else [],
        compiler_params=LIMIT,
        cost_estimate=pl.CostEstimate(
            flops=total * 16 * BLK**3, bytes_accessed=total * BLK * BLK * 2, transcendentals=0
        ),
    )(table, right, *lefts, *(() if before is None else (before,)))


def left_order():
    found = []
    for core in range(2):
        rows = []
        for low, high in GROUPS:
            for other_core in range(2):
                for other_half in range(2):
                    rows += [(other_half, other_core, d, 1) for _, d in low]
                    rows += [(other_half, other_core, d, 2) for _, d in high]
                    rows += [
                        (other_half, other_core, d, 3 * core) for _, d in (high if core else low)
                    ]
        found.append(rows)
    return np.array(found, np.int32)


def tables(a_all, right_codes, c_code, r, z, h, core):
    order = left_order()
    order = jnp.where(core == 0, order[0], order[1])
    other_half, other_core, distance, panel = (order[:, n] for n in range(4))
    count = order.shape[0]
    owner = 24 * (h ^ other_half) + 2 * ((z - distance) % NZ) + (core ^ other_core)
    place = owner * 16 + (r + 24 * h + 2 * z + panel) % 16
    flat = a_all.reshape(1, 768)
    codes = jnp.sum(jnp.where(place[:, None] == jnp.arange(768)[None, :], flat, 0), axis=1)
    step = panel - core
    right_live = right_codes >= 0
    right_inner = jnp.where(right_live, right_codes // BC, -1)
    owners = jnp.arange(16, dtype=jnp.int32)
    earlier = owners[None, :] < owners[:, None]
    rank = jnp.sum(
        ((right_inner[:, None, :] == right_inner[None, :, :]) & earlier[:, :, None]).astype(jnp.int32),
        axis=1,
    )
    packed = jnp.where(right_live, right_inner * 1024 + rank * 32 + right_codes % BC, -1)
    right_n = jnp.where(
        (step == 0)[:, None],
        packed[None, :, 0],
        jnp.where((step == 1)[:, None], packed[None, :, 1], packed[None, :, 2]),
    )
    match = (right_n >= 0) & (codes >= 0)[:, None] & ((right_n // 1024) == (codes % PANEL)[:, None])
    rows = []
    for rank_number in range(2):
        hit = match & ((right_n // 32) % 32 == rank_number)
        found = jnp.sum(jnp.where(hit, owners[None, :] * 32 + right_n % 32 + 1, 0), axis=1)
        partner = jnp.maximum(found - 1, 0)
        target = (codes // PANEL) * BC + partner % 32
        there = (target[:, None] == c_code[None, :]) & (found > 0)[:, None]
        slot = jnp.sum(jnp.where(there, jnp.arange(KEPT)[None, :] - KEPT, 0), axis=1) + KEPT
        rows += [partner // 32, step * BLK, slot]
    return jnp.stack(rows).astype(jnp.int32).reshape(6, count)


def local(a_own_values, a_own_code, b_own_values, b_own_code, c_code):
    r = lax.axis_index(ROW)
    h = lax.axis_index("xh")
    z = lax.axis_index("z")
    core = lax.axis_index("core")
    c = 24 * h + 2 * z + core
    a_own = a_own_values.reshape(16, BLK, BLK)
    b_own = b_own_values.reshape(16, BLK, BLK)

    cyc = (r + 2 * z + jnp.arange(8, dtype=jnp.int32)) % 8
    a_index = jnp.concatenate([cyc, cyc + 8])

    def class_order(classes):
        return tuple(e * 8 + 2 * a + b for a in classes for b in range(2) for e in range(2))

    first, second = ordered(a_own, a_index, (class_order((1, 2)), class_order((3, 0))))
    up1 = shifted(first, 1)
    down1 = shifted(second, -1)
    up2 = shifted(second, 2)
    down2 = shifted(first, -2)

    shift = (c + jnp.arange(16, dtype=jnp.int32)) % 16
    b_index = jnp.concatenate([shift, shift[:2]])
    b_code = b_own_code.reshape(16) + 1
    b_code = jnp.sum(jnp.where(b_index[:, None] == jnp.arange(16)[None, :], b_code[None, :], 0), axis=1)
    b_code = jnp.stack([b_code[t : t + 16] for t in range(STEPS)], axis=1)
    b_code = jnp.concatenate([b_code // 16, b_code % 16], axis=1).astype(jnp.bfloat16)
    b_code = jnp.broadcast_to(jnp.pad(b_code, ((0, 0), (0, BLK - 6)))[:, None, :], (16, 16, BLK))
    right = lax.all_to_all(right_packed(b_own, b_index, b_code), ROW, 0, 0, tiled=True)
    a_all = lax.all_to_all(
        jnp.broadcast_to(a_own_code.reshape(1, 16), (48, 16)), COL, 0, 0, tiled=True
    )

    here = [(r + 24 * h + 2 * z + w) % 16 // 8 for w in range(4)]
    above = [(r + 24 * h + 2 * ((z + 1) % NZ) + w) % 16 // 8 for w in range(2)]
    below = [(r + 24 * h + 2 * ((z + NZ - 1) % NZ) + w) % 16 // 8 for w in range(2, 4)]
    pick = jnp.stack(here + [core] + above + below).astype(jnp.int32)

    sources, at = [], {}

    def keep(array, names):
        for n, name in enumerate(names):
            at[name] = (len(sources), 4 * n)
        sources.append(array)

    def packed(spec):
        used = sorted({entry[0] for entries in spec for pair in entries for entry in pair})
        where = {source: n for n, source in enumerate(used)}
        spec = tuple(
            tuple(tuple((where[entry[0]],) + entry[1:] for entry in pair) for pair in entries)
            for entries in spec
        )
        return pack(pick, [sources[source] for source in used], spec)

    def same(entry):
        return (entry, entry)

    def whole(names):
        return [
            same((at[name][0], at[name][1] + n, None, 1)) for name in names for n in range(4)
        ]

    def wanted(name, b, picked, other=False):
        source, block = at[name]
        return (source, block + 2 * b + (1 if other else 0), picked, -1 if other else 1)

    keep(first, ((1, 0), (2, 0)))
    keep(second, ((3, 0), (0, 0)))
    keep(up1, ((1, 1), (2, 1)))
    keep(down1, ((3, -1), (0, -1)))
    keep(up2, ((3, 2), (0, 2)))
    keep(down2, ((1, -2), (2, -2)))
    up_in, down_in = packed(
        [whole(((2, 1), (3, 2), (0, 2))), whole(((3, -1), (2, -2), (1, -2)))]
    )
    keep(shifted(up_in, 1), ((2, 2), (3, 3), (0, 3)))
    keep(shifted(down_in, -1), ((3, -2), (2, -3), (1, -3)))
    up_in, down_in = packed([whole(((1, 1), (2, 2))), whole(((0, -1), (3, -2)))])
    keep(shifted(up_in, 3), ((1, 4), (2, 5)))
    keep(shifted(down_in, -3), ((0, -4), (3, -5)))
    low_from, high_from = ((1, 4), (2, 5), (0, 3)), ((1, -3), (3, -5), (0, -4))
    last_low, last_low_other, last_high, last_high_other = packed(
        [
            [
                same(wanted(name, b, start + b, other))
                for name in names
                for b in range(2)
            ]
            for names, start in ((low_from, 5), (high_from, 7))
            for other in (False, True)
        ]
    )
    last = (
        shifted(last_low, 1),
        shifted_across(last_low_other, 1),
        shifted(last_high, -1),
        shifted_across(last_high_other, -1),
    )

    lefts = []
    for number, (low, high) in enumerate(GROUPS):
        n = len(low)
        if number < 3:
            (out,) = packed(
                [
                    [same(wanted(name, b, b, True)) for name in low for b in range(2)]
                    + [same(wanted(name, b, 2 + b, True)) for name in high for b in range(2)]
                ]
            )
            sources.append(lax.ppermute(out, "xh", [(0, 1), (1, 0)]))
            crossed = len(sources) - 1

            def own_block(i, panel, low=low, high=high):
                return wanted((low if panel < 2 else high)[i], panel % 2, panel)

            def other_block(i, panel, n=n, crossed=crossed):
                return (crossed, (n if panel >= 2 else 0) * 2 + 2 * i + panel % 2, None, 1)
        else:
            sources.extend(last)
            base = len(sources) - 4

            def own_block(i, panel, base=base):
                return (base + (2 if panel >= 2 else 0), 2 * i + panel % 2, None, 1)

            def other_block(i, panel, base=base):
                return (base + 1 + (2 if panel >= 2 else 0), 2 * i + panel % 2, None, 1)

        spec = []
        for for_other_core in range(2):
            entries = []
            for block in (own_block, other_block):
                for panel in (1, 2):
                    entries += [same(block(i, panel)) for i in range(n)]
                pair = (3, 0) if for_other_core else (0, 3)
                entries += [(block(i, pair[0]), block(i, pair[1])) for i in range(n)]
            spec.append(entries)
        kept, sent = packed(spec)
        lefts.append((kept, lax.ppermute(sent, "core", [(0, 1), (1, 0)])))

    right_codes = right[:, STEPS * BLK, :6].astype(jnp.int32)
    right_codes = right_codes[:, :3] * 16 + right_codes[:, 3:] - 1
    table = tables(a_all, right_codes, c_code.reshape(KEPT), r, z, h, core)
    sums = product(table, right, lefts[0], 0)
    sums = product(table, right, lefts[1] + lefts[2], 48, sums)
    return product(table, right, lefts[3], 108, sums, last=True)[None, None]


def solution(mesh):
    fine = Mesh(mesh.devices.reshape(SIZES), AXES)
    return jax.shard_map(
        local,
        mesh=fine,
        in_specs=(
            P(ROW, COL, None, None, None, None),
            P(ROW, COL, None, None),
            P(ROW, COL, None, None, None, None),
            P(ROW, COL, None, None),
            P(ROW, COL, None),
        ),
        out_specs=P(ROW, COL, None, None, None),
        check_vma=False,
    )
```

```python
import functools

import jax
import jax.numpy as jnp
import numpy as np
from jax import lax
from jax.experimental import pallas as pl
from jax.experimental.pallas import tpu as pltpu
from jax.sharding import Mesh
from jax.sharding import PartitionSpec as P

AXES = ("xl", "y", "xh", "z", "core")
ROW = ("xl", "y")
COL = ("xh", "z", "core")
RING = ("xh", "z")
SIZES = (2, 8, 2, 12, 2)
NQ = 24
BC = 16
PANEL = 48
STEPS = 3
KEPT = 12
BLK = 128

GROUPS = (
    (
        ((0, 0), (4, 12), (1, 1), (5, 13), (7, 23), (3, 11), (6, 22), (2, 10)),
        ((1, 0), (5, 12), (2, 1), (6, 13), (3, 2), (7, 14), (0, 23), (4, 11)),
    ),
    (
        ((2, 2), (6, 14), (3, 3), (7, 15), (1, 9), (5, 21), (0, 8), (4, 20), (3, 19), (7, 7)),
        ((0, 15), (4, 3), (3, 10), (7, 22), (2, 9), (6, 21), (1, 16), (5, 4), (2, 17), (6, 5)),
    ),
    (
        ((1, 17), (5, 5), (2, 18), (6, 6), (0, 16), (4, 4)),
        ((0, 7), (4, 19), (3, 18), (7, 6), (1, 8), (5, 20)),
    ),
)

VMEM = pltpu.VMEM
SMEM_SPEC = pl.BlockSpec(memory_space=pltpu.SMEM)
VMEM_SPEC = pl.BlockSpec(memory_space=pltpu.VMEM)
ANY_SPEC = pl.BlockSpec(memory_space=pl.ANY)
LIMIT = pltpu.CompilerParams(vmem_limit_bytes=40 << 20)


def moves(blocks):
    return pl.CostEstimate(flops=0, bytes_accessed=2 * blocks * BLK * BLK * 2, transcendentals=0)


def rows_shape(rows):
    return jax.ShapeDtypeStruct((rows, BLK), jnp.bfloat16)


def blk(n):
    return pl.ds(n * BLK, BLK)


def ordered_kernel(orders, index_ref, src_ref, note_ref, *outs):
    for out, order in zip(outs, orders, strict=True):
        for n, place in enumerate(order):
            out[blk(n), :] = src_ref[index_ref[place]]
        out[pl.ds(len(order) * BLK, 16), :] = note_ref[...]


def ordered(src, index, note, orders):
    return pl.pallas_call(
        functools.partial(ordered_kernel, orders),
        out_shape=[rows_shape(len(order) * BLK + 16) for order in orders],
        in_specs=[SMEM_SPEC, VMEM_SPEC, VMEM_SPEC],
        out_specs=[VMEM_SPEC for _ in orders],
        compiler_params=LIMIT,
        cost_estimate=moves(sum(len(order) for order in orders)),
    )(index, src, note)


def right_kernel(index_ref, src_ref, code_ref, after_ref, out):
    del after_ref
    for n in range(16):
        for t in range(STEPS):
            out[n, pl.ds(t * BLK, BLK), :] = src_ref[index_ref[n + t]]
        out[n, pl.ds(STEPS * BLK, 16), :] = code_ref[n]


def right_packed(src, index, codes, after):
    return pl.pallas_call(
        right_kernel,
        out_shape=jax.ShapeDtypeStruct((16, STEPS * BLK + 16, BLK), jnp.bfloat16),
        in_specs=[SMEM_SPEC, VMEM_SPEC, VMEM_SPEC, ANY_SPEC],
        out_specs=VMEM_SPEC,
        compiler_params=LIMIT,
        cost_estimate=moves(48),
    )(index, src, codes, after)


def pack_kernel(spec, notes, count, core_ref, *refs):
    sources, outs = refs[:count], refs[count:]
    if notes:
        merged = None
        for source, row, rows, turn in notes:
            note = sources[source][pl.ds(row, rows), :].astype(jnp.float32)
            if rows == 16:
                note = jnp.concatenate([note, jnp.zeros((8, BLK), jnp.float32)])
            else:
                note = note[:NQ]
            if turn:
                note = pltpu.roll(note, turn, 0)
            merged = note if merged is None else jnp.maximum(merged, note)
        merged = jnp.concatenate([merged, jnp.zeros((8, BLK), jnp.float32)]).astype(jnp.bfloat16)

    def copy(out, n, entry):
        out[blk(n), :] = sources[entry[0]][blk(entry[1]), :]

    for out, (entries, noted) in zip(outs, spec, strict=True):
        for n, (zero, one) in enumerate(entries):
            if zero == one:
                copy(out, n, zero)
        if noted:
            out[pl.ds(len(entries) * BLK, 32), :] = merged
    if any(zero != one for entries, _ in spec for zero, one in entries):
        for core in range(2):

            @pl.when(core_ref[0] == core)
            def _(core=core):
                for out, (entries, _) in zip(outs, spec, strict=True):
                    for n, pair in enumerate(entries):
                        if pair[0] != pair[1]:
                            copy(out, n, pair[core])


def pack(core, sources, spec, notes):
    used = sorted({e[0] for entries, _ in spec for pair in entries for e in pair} | {n[0] for n in notes})
    where = {source: n for n, source in enumerate(used)}
    spec = tuple(
        (tuple(tuple((where[e[0]], e[1]) for e in pair) for pair in entries), noted)
        for entries, noted in spec
    )
    notes = tuple((where[n[0]],) + tuple(n[1:]) for n in notes)
    return pl.pallas_call(
        functools.partial(pack_kernel, spec, notes, len(used)),
        out_shape=[rows_shape(len(entries) * BLK + 32 * noted) for entries, noted in spec],
        in_specs=[SMEM_SPEC] + [VMEM_SPEC] * len(used),
        out_specs=[VMEM_SPEC for _ in spec],
        compiler_params=LIMIT,
        cost_estimate=moves(sum(len(entries) for entries, _ in spec)),
    )(core, *[sources[source] for source in used])


def product_kernel(counts, base, first, last, table_ref, right_ref, *rest):
    lefts, rest = rest[: len(counts)], rest[len(counts) :]
    if last:
        before, out_ref, acc = rest
        acc[...] = before[...]
    elif first:
        (acc,) = rest
        acc[...] = jnp.zeros_like(acc)
    else:
        before, acc = rest
        acc[...] = before[...]
    for left, count in zip(lefts, counts, strict=True):

        def body(n, carry, left=left, base=base):
            block = left[pl.ds(pl.multiple_of(n * BLK, BLK), BLK), :]
            for rank in range(2):
                owner = table_ref[3 * rank, base + n]
                row = pl.multiple_of(table_ref[3 * rank + 1, base + n], BLK)
                place = table_ref[3 * rank + 2, base + n]
                right = right_ref[owner, pl.ds(row, BLK), :]
                acc[place] += jnp.dot(block, right, preferred_element_type=jnp.float32)
            return carry

        lax.fori_loop(0, count, body, 0, unroll=6)
        base += count
    if last:
        out_ref[...] = acc[:KEPT].astype(out_ref.dtype)


def product(table, right, lefts, base, before=None, last=False):
    counts = tuple(left.shape[0] // BLK for left in lefts)
    total = sum(counts)
    sums = jax.ShapeDtypeStruct((KEPT + 1, BLK, BLK), jnp.float32)
    return pl.pallas_call(
        functools.partial(product_kernel, counts, base, before is None, last),
        out_shape=jax.ShapeDtypeStruct((KEPT, BLK, BLK), jnp.bfloat16) if last else sums,
        in_specs=[SMEM_SPEC] + [VMEM_SPEC] * (1 + len(lefts) + (before is not None)),
        out_specs=VMEM_SPEC,
        scratch_shapes=[VMEM(sums.shape, jnp.float32)] if last else [],
        compiler_params=LIMIT,
        cost_estimate=pl.CostEstimate(
            flops=total * 16 * BLK**3, bytes_accessed=total * BLK * BLK * 2, transcendentals=0
        ),
    )(table, right, *lefts, *(() if before is None else (before,)))


def left_order(groups):
    found = []
    for core in range(2):
        rows = []
        for low, high in groups:
            for other_core in range(2):
                rows += [(other_core, d, 1) for _, d in low]
                rows += [(other_core, d, 2) for _, d in high]
                rows += [(other_core, d, 3 * core) for _, d in (high if core else low)]
        found.append(rows)
    return np.array(found, np.int32)


def tables(groups, notes, right_codes, c_code, start, core):
    order = left_order(groups)
    order = jnp.where(core == 0, order[0], order[1])
    other_core, distance, panel = (order[:, n] for n in range(3))
    count = order.shape[0]
    notes = jnp.stack(notes)[:, :NQ, :32].astype(jnp.int32)
    flat = (notes[:, :, :16] * 64 + notes[:, :, 16:] - 1).reshape(1, 2 * NQ * 16)
    place = (other_core * NQ + distance) * 16 + (start + panel) % 16
    codes = jnp.sum(jnp.where(place[:, None] == jnp.arange(2 * NQ * 16)[None, :], flat, 0), axis=1)
    step = panel - core
    right_live = right_codes >= 0
    right_inner = jnp.where(right_live, right_codes // BC, -1)
    owners = jnp.arange(16, dtype=jnp.int32)
    earlier = owners[None, :] < owners[:, None]
    rank = jnp.sum(
        ((right_inner[:, None, :] == right_inner[None, :, :]) & earlier[:, :, None]).astype(jnp.int32),
        axis=1,
    )
    packed = jnp.where(right_live, right_inner * 1024 + rank * 32 + right_codes % BC, -1)
    right_n = jnp.where(
        (step == 0)[:, None],
        packed[None, :, 0],
        jnp.where((step == 1)[:, None], packed[None, :, 1], packed[None, :, 2]),
    )
    match = (right_n >= 0) & (codes >= 0)[:, None] & ((right_n // 1024) == (codes % PANEL)[:, None])
    rows = []
    for rank_number in range(2):
        hit = match & ((right_n // 32) % 32 == rank_number)
        found = jnp.sum(jnp.where(hit, owners[None, :] * 32 + right_n % 32 + 1, 0), axis=1)
        partner = jnp.maximum(found - 1, 0)
        target = (codes // PANEL) * BC + partner % 32
        there = (target[:, None] == c_code[None, :]) & (found > 0)[:, None]
        slot = jnp.sum(jnp.where(there, jnp.arange(KEPT)[None, :] - KEPT, 0), axis=1) + KEPT
        rows += [partner // 32, step * BLK, slot]
    return jnp.stack(rows).astype(jnp.int32).reshape(6, count)


def moved(array, distance):
    route = [(i, (i + distance) % NQ) for i in range(NQ)]
    return lax.ppermute(array, RING, route)


def local(a_own_values, a_own_code, b_own_values, b_own_code, c_code):
    r = lax.axis_index(ROW)
    q = lax.axis_index(RING)
    core = lax.axis_index("core")
    start = (r + 2 * q) % 16
    a_own = a_own_values.reshape(16, BLK, BLK)
    b_own = b_own_values.reshape(16, BLK, BLK)
    core_1d = core.astype(jnp.int32).reshape(1)

    sources, at = [], {}

    def keep(array, names):
        for n, name in enumerate(names):
            at[name] = (len(sources), 2 * n)
        sources.append(array)
        return len(sources) - 1

    def send(array, names, distance):
        return keep(moved(array, distance), [(a, (d + distance) % NQ) for a, d in names])

    def both(entry):
        return (entry, entry)

    def blocks(names):
        return [both((at[name][0], at[name][1] + b)) for name in names for b in range(2)]

    def packed(spec, notes=()):
        return pack(core_1d, sources, spec, notes)

    def core_blocks(group):
        low, high = group

        def block(name, b):
            return (at[name][0], at[name][1] + b)

        spec = []
        for turned in (False, True):
            entries = [both(block(name, 1)) for name in low]
            entries += [both(block(name, 0)) for name in high]
            for x, y in zip(low, high, strict=True):
                pair = (block(x, 0), block(y, 1))
                entries.append(pair[::-1] if turned else pair)
            spec.append((entries, turned))
        return spec

    code = a_own_code.reshape(16) + 1
    note = jnp.concatenate([code // 64, code % 64]).astype(jnp.bfloat16).reshape(1, 32)
    note = jnp.pad(note, ((0, 15), (0, BLK - 32)))
    a_index = (start + jnp.arange(16, dtype=jnp.int32)) % 16

    def class_order(classes):
        return tuple(2 * a + b for a in classes for b in range(2))

    one, two = (1, 2, 5, 6), (3, 0, 7, 4)
    first, second = ordered(a_own, a_index, note, (class_order(one), class_order(two)))
    ones, twos = [(a, 0) for a in one], [(a, 0) for a in two]
    own = keep(first, ones)
    keep(second, twos)
    up2 = send(second, twos, 2)
    down2 = send(first, ones, -2)
    up1 = send(first, ones, 1)
    down1 = send(second, twos, -1)

    shift = (2 * q + core + jnp.arange(18, dtype=jnp.int32)) % 16
    b_code = b_own_code.reshape(16) + 1
    b_code = jnp.sum(jnp.where(shift[:, None] == jnp.arange(16)[None, :], b_code[None, :], 0), axis=1)
    b_code = jnp.stack([b_code[t : t + 16] for t in range(STEPS)], axis=1)
    b_code = jnp.concatenate([b_code // 16, b_code % 16], axis=1).astype(jnp.bfloat16)
    b_code = jnp.broadcast_to(jnp.pad(b_code, ((0, 0), (0, BLK - 6)))[:, None, :], (16, 16, BLK))
    right = right_packed(b_own, shift, b_code, sources[up1])
    right = lax.all_to_all(right, ROW, 0, 0, tiled=True)

    near = [(own, 8 * BLK, 16, 0)]
    near += [(up1, 8 * BLK, 16, 1), (up2, 8 * BLK, 16, 2), (down1, 8 * BLK, 16, 23), (down2, 8 * BLK, 16, 22)]
    up_names = [(2, 1), (6, 1), (3, 2), (7, 2), (0, 2), (4, 2)]
    down_names = [(3, 23), (7, 23), (2, 22), (6, 22), (1, 22), (5, 22)]
    up_in, down_in = packed([(blocks(up_names), True), (blocks(down_names), True)], near)
    mine = len(sources)
    sources.append(up_in)
    up3 = send(up_in, up_names, 1)
    down3 = send(down_in, down_names, -1)

    cross_names = [(5, 1), (6, 1), (7, 2), (4, 0), (5, 0), (4, 23), (3, 23), (2, 22)]
    (cross_in,) = packed([(blocks(cross_names), True)], near)
    sources.append(cross_in)
    crossed = send(cross_in, cross_names, 12)
    around = [(crossed - 1, 16 * BLK, 32, 0), (crossed, 16 * BLK, 32, 12)]

    near = [(mine, 12 * BLK, 32, 0), (up3, 12 * BLK, 32, 1), (down3, 12 * BLK, 32, 23)]
    plans = (([(1, 1), (2, 2)], 15), ([(5, 1), (6, 2)], 3), ([(0, 23), (7, 22)], 9), ([(4, 23), (3, 22)], -3))
    inputs = packed([(blocks(names), True) for names, _ in plans], near)
    far = [(len(sources), 4 * BLK, 32, 0)]
    sources.append(inputs[0])
    for array, (names, distance) in zip(inputs, plans, strict=True):
        far.append((send(array, names, distance), 4 * BLK, 32, distance % NQ))

    cross_names = [(6, 2), (7, 3), (0, 3), (3, 22), (2, 21), (1, 21)]
    (cross_in,) = packed([(blocks(cross_names), False)])
    send(cross_in, cross_names, 12)

    up_names = [(1, 16), (5, 4), (2, 17), (6, 5), (0, 15), (4, 3)]
    down_names = [(0, 8), (4, 20), (3, 19), (7, 7), (1, 9), (5, 21)]
    up_in, down_in = packed([(blocks(up_names), False), (blocks(down_names), False)])
    send(up_in, up_names, 1)
    send(down_in, down_names, -1)

    lefts, notes = [], []
    for number, group in enumerate(GROUPS):
        spec = core_blocks(group)
        if number == 2:
            spec = [(entries, False) for entries, _ in spec]
        kept, sent = packed(spec, (around, far, ())[number])
        received = lax.ppermute(sent, "core", [(0, 1), (1, 0)])
        count = len(spec[0][0])
        lefts.append((kept, received))
        notes.append((sent[count * BLK :], received[count * BLK :]))

    right_codes = right[:, STEPS * BLK, :6].astype(jnp.int32)
    right_codes = right_codes[:, :3] * 16 + right_codes[:, 3:] - 1
    c_code = c_code.reshape(KEPT)
    table = tables(GROUPS[:1], notes[0], right_codes, c_code, start, core)
    sums = product(table, right, lefts[0], 0)
    table = tables(GROUPS[1:], notes[1], right_codes, c_code, start, core)
    sums = product(table, right, lefts[1], 0, sums)
    return product(table, right, lefts[2], 60, sums, last=True)[None, None]


def solution(mesh):
    fine = Mesh(mesh.devices.reshape(SIZES), AXES)
    return jax.shard_map(
        local,
        mesh=fine,
        in_specs=(
            P(ROW, COL, None, None, None, None),
            P(ROW, COL, None, None),
            P(ROW, COL, None, None, None, None),
            P(ROW, COL, None, None),
            P(ROW, COL, None),
        ),
        out_specs=P(ROW, COL, None, None, None),
        check_vma=False,
    )
```

```python
import functools

import jax
import jax.numpy as jnp
import numpy as np
from jax import lax
from jax.experimental import pallas as pl
from jax.experimental.pallas import tpu as pltpu
from jax.sharding import Mesh
from jax.sharding import PartitionSpec as P

AXES = ("xl", "y", "xh", "z", "core")
ROW = ("xl", "y")
COL = ("xh", "z", "core")
SIZES = (2, 8, 2, 12, 2)
NQ = 24
NOTE = 2 * NQ
BC = 16
PANEL = 48
STEPS = 3
KEPT = 12
BLK = 128


def items(pairs):
    return [(a, d, k) for a, d in pairs for k in range(2)]


def wanted(name):
    a, d, _ = name
    return [(0, 0), (1, 1)] if (d - a) % 8 == 0 else [(0, 2)]


def passed_on(name):
    a, d, _ = name
    return [(1, 2)] if (d - a) % 8 == 0 else [(0, 1), (1, 0)]


VMEM = pltpu.VMEM
SMEM_SPEC = pl.BlockSpec(memory_space=pltpu.SMEM)
VMEM_SPEC = pl.BlockSpec(memory_space=pltpu.VMEM)
ANY_SPEC = pl.BlockSpec(memory_space=pl.ANY)
LIMIT = pltpu.CompilerParams(vmem_limit_bytes=40 << 20)


def moves(blocks):
    return pl.CostEstimate(flops=0, bytes_accessed=2 * blocks * BLK * BLK * 2, transcendentals=0)


def rows_shape(rows):
    return jax.ShapeDtypeStruct((rows, BLK), jnp.bfloat16)


def blk(n):
    return pl.ds(n * BLK, BLK)


def first_kernel(orders, index_ref, own_ref, other_ref, own_note, other_note, *outs):
    empty = jnp.zeros((8, BLK), jnp.float32)
    note = jnp.concatenate(
        [own_note[...].astype(jnp.float32), empty, other_note[...].astype(jnp.float32), empty]
    ).astype(jnp.bfloat16)
    for out, order in zip(outs, orders, strict=True):
        for n, (other, place) in enumerate(order):
            out[blk(n), :] = (other_ref if other else own_ref)[index_ref[place]]
        out[pl.ds(len(order) * BLK, NOTE), :] = note


def first_packed(index, own, other, own_note, other_note, orders):
    return pl.pallas_call(
        functools.partial(first_kernel, orders),
        out_shape=[rows_shape(len(order) * BLK + NOTE) for order in orders],
        in_specs=[SMEM_SPEC] + [VMEM_SPEC] * 4,
        out_specs=[VMEM_SPEC for _ in orders],
        compiler_params=LIMIT,
        cost_estimate=moves(sum(len(order) for order in orders)),
    )(index, own, other, own_note, other_note)


def right_kernel(index_ref, src_ref, code_ref, after_ref, out):
    del after_ref
    for n in range(16):
        for t in range(STEPS):
            out[n, pl.ds(t * BLK, BLK), :] = src_ref[index_ref[n + t]]
        out[n, pl.ds(STEPS * BLK, 16), :] = code_ref[n]


def right_packed(src, index, codes, after):
    return pl.pallas_call(
        right_kernel,
        out_shape=jax.ShapeDtypeStruct((16, STEPS * BLK + 16, BLK), jnp.bfloat16),
        in_specs=[SMEM_SPEC, VMEM_SPEC, VMEM_SPEC, ANY_SPEC],
        out_specs=VMEM_SPEC,
        compiler_params=LIMIT,
        cost_estimate=moves(48),
    )(index, src, codes, after)


def turned(note, distance):
    if distance == 0:
        return note
    return jnp.concatenate([pltpu.roll(note[n : n + NQ], distance, 0) for n in (0, NQ)])


def pack_kernel(spec, notes, count, *refs):
    sources, outs = refs[:count], refs[-len(spec) :]
    if notes:
        merged = None
        for source, row, distance in notes:
            note = sources[source][pl.ds(row, NOTE), :].astype(jnp.float32)
            note = turned(note, distance)
            merged = note if merged is None else jnp.maximum(merged, note)
        merged = merged.astype(jnp.bfloat16)
    for out, (entries, noted) in zip(outs, spec, strict=True):
        for n, (source, place) in enumerate(entries):
            out[blk(n), :] = sources[source][blk(place), :]
        if noted:
            out[pl.ds(len(entries) * BLK, NOTE), :] = merged


def pack(sources, spec, notes, after):
    used = sorted({e[0] for entries, _ in spec for e in entries} | {n[0] for n in notes})
    where = {source: n for n, source in enumerate(used)}
    spec = tuple((tuple((where[s], n) for s, n in entries), noted) for entries, noted in spec)
    notes = tuple((where[n[0]],) + tuple(n[1:]) for n in notes)
    return pl.pallas_call(
        functools.partial(pack_kernel, spec, notes, len(used)),
        out_shape=[rows_shape(len(entries) * BLK + NOTE * noted) for entries, noted in spec],
        in_specs=[VMEM_SPEC] * len(used) + [ANY_SPEC] * len(after),
        out_specs=[VMEM_SPEC for _ in spec],
        compiler_params=LIMIT,
        cost_estimate=moves(sum(len(entries) for entries, _ in spec)),
    )(*[sources[source] for source in used], *after)


def product_kernel(counts, base, first, last, table_ref, right_ref, *rest):
    lefts, rest = rest[: len(counts)], rest[len(counts) :]
    if last:
        before, out_ref, acc = rest
        acc[...] = before[...]
    elif first:
        (acc,) = rest
        acc[...] = jnp.zeros_like(acc)
    else:
        before, acc = rest
        acc[...] = before[...]
    for left, count in zip(lefts, counts, strict=True):

        def body(n, carry, left=left, base=base):
            block = left[pl.ds(pl.multiple_of(table_ref[6, base + n], BLK), BLK), :]
            for rank in range(2):
                owner = table_ref[3 * rank, base + n]
                row = pl.multiple_of(table_ref[3 * rank + 1, base + n], BLK)
                place = table_ref[3 * rank + 2, base + n]
                right = right_ref[owner, pl.ds(row, BLK), :]
                acc[place] += jnp.dot(block, right, preferred_element_type=jnp.float32)
            return carry

        unroll = max(n for n in (7, 6, 5, 4, 3, 2, 1) if count % n == 0)
        lax.fori_loop(0, count, body, 0, unroll=unroll)
        base += count
    if last:
        out_ref[...] = acc[:KEPT].astype(out_ref.dtype)


def product(table, right, lefts, counts, base, before=None, last=False):
    total = sum(counts)
    sums = jax.ShapeDtypeStruct((KEPT + 1, BLK, BLK), jnp.float32)
    return pl.pallas_call(
        functools.partial(product_kernel, counts, base, before is None, last),
        out_shape=jax.ShapeDtypeStruct((KEPT, BLK, BLK), jnp.bfloat16) if last else sums,
        in_specs=[SMEM_SPEC] + [VMEM_SPEC] * (1 + len(lefts) + (before is not None)),
        out_specs=VMEM_SPEC,
        scratch_shapes=[VMEM(sums.shape, jnp.float32)] if last else [],
        compiler_params=LIMIT,
        cost_estimate=pl.CostEstimate(
            flops=total * 16 * BLK**3, bytes_accessed=total * BLK * BLK * 2, transcendentals=0
        ),
    )(table, right, *lefts, *(() if before is None else (before,)))


def tables(order, notes, right_codes, c_code, start, core):
    order = np.array(order, np.int32)
    count = order.shape[0]
    row, other, k, distance, panel = (order[:, n] for n in range(5))
    notes = jnp.stack(notes)[:, :, :32].astype(jnp.int32)
    flat = (notes[:, :, :16] * 64 + notes[:, :, 16:] - 1).reshape(1, 2 * NOTE * 16)
    of = (start + panel + core * (3 - 2 * panel)) % 16
    place = (other * NOTE + k * NQ + distance) * 16 + of
    codes = jnp.sum(jnp.where(place[:, None] == jnp.arange(2 * NOTE * 16)[None, :], flat, 0), axis=1)
    step = panel + core * (2 - 2 * panel)
    right_live = right_codes >= 0
    right_inner = jnp.where(right_live, right_codes // BC, -1)
    owners = jnp.arange(16, dtype=jnp.int32)
    earlier = owners[None, :] < owners[:, None]
    rank = jnp.sum(
        ((right_inner[:, None, :] == right_inner[None, :, :]) & earlier[:, :, None]).astype(jnp.int32),
        axis=1,
    )
    packed = jnp.where(right_live, right_inner * 1024 + rank * 32 + right_codes % BC, -1)
    right_n = jnp.where(
        (step == 0)[:, None],
        packed[None, :, 0],
        jnp.where((step == 1)[:, None], packed[None, :, 1], packed[None, :, 2]),
    )
    match = (right_n >= 0) & (codes >= 0)[:, None] & ((right_n // 1024) == (codes % PANEL)[:, None])
    rows = []
    for rank_number in range(2):
        hit = match & ((right_n // 32) % 32 == rank_number)
        found = jnp.sum(jnp.where(hit, owners[None, :] * 32 + right_n % 32 + 1, 0), axis=1)
        partner = jnp.maximum(found - 1, 0)
        target = (codes // PANEL) * BC + partner % 32
        there = (target[:, None] == c_code[None, :]) & (found > 0)[:, None]
        slot = jnp.sum(jnp.where(there, jnp.arange(KEPT)[None, :] - KEPT, 0), axis=1) + KEPT
        rows += [partner // 32, step * BLK, slot]
    return jnp.stack(rows + [jnp.array(row)]).astype(jnp.int32).reshape(7, count)


def moved(array, distance):
    route = []
    for i in range(NQ):
        route.append((2 * i, 2 * ((i + distance) % NQ)))
        route.append((2 * i + 1, 2 * ((i - distance) % NQ) + 1))
    return lax.ppermute(array, COL, route)


def from_other_core(array):
    return lax.ppermute(array, "core", [(0, 1), (1, 0)])


def local(a_own_values, a_own_code, b_own_values, b_own_code, c_code):
    r = lax.axis_index(ROW)
    q = lax.axis_index(("xh", "z"))
    core = lax.axis_index("core")
    start = (r + 2 * q) % 16
    a_own = a_own_values.reshape(16, BLK, BLK)
    b_own = b_own_values.reshape(16, BLK, BLK)

    sources, at = [], {}

    def keep(array, names):
        for n, name in enumerate(names):
            at[name] = (len(sources), 2 * n)
        sources.append(array)
        return len(sources) - 1

    def send(array, names, distance):
        return keep(moved(array, distance), [(a, (d + distance) % NQ, k) for a, d, k in names])

    def blocks(names):
        return [(at[name][0], at[name][1] + b) for name in names for b in range(2)]

    def packed(spec, notes=(), after=()):
        return pack(sources, spec, notes, after)

    code = a_own_code.reshape(16) + 1
    note = jnp.concatenate([code // 64, code % 64]).astype(jnp.bfloat16).reshape(1, 32)
    note = jnp.pad(note, ((0, 15), (0, BLK - 32)))
    a_other, note_other = from_other_core(a_own), from_other_core(note)
    a_index = jnp.arange(16, dtype=jnp.int32)
    a_index = (start + jnp.where(core == 0, a_index, 3 - a_index)) % 16

    ones, twos = (items((a, 0) for a in classes) for classes in ((1, 2, 5, 6), (3, 0, 7, 4)))
    orders = tuple(
        tuple((k, 2 * a + b) for a, _, k in names for b in range(2)) for names in (ones, twos)
    )
    first, second = first_packed(a_index, a_own, a_other, note, note_other, orders)
    own = keep(first, ones)
    keep(second, twos)
    up2 = send(second, twos, 2)
    up1 = send(first, ones, 1)

    shift = (2 * q + core + jnp.arange(18, dtype=jnp.int32)) % 16
    b_code = b_own_code.reshape(16) + 1
    b_code = jnp.sum(jnp.where(shift[:, None] == jnp.arange(16)[None, :], b_code[None, :], 0), axis=1)
    b_code = jnp.stack([b_code[t : t + 16] for t in range(STEPS)], axis=1)
    b_code = jnp.concatenate([b_code // 16, b_code % 16], axis=1).astype(jnp.bfloat16)
    b_code = jnp.broadcast_to(jnp.pad(b_code, ((0, 0), (0, BLK - 6)))[:, None, :], (16, 16, BLK))
    right = right_packed(b_own, shift, b_code, sources[up2])
    right = lax.all_to_all(right, ROW, 0, 0, tiled=True)

    near = [(own, 16 * BLK, 0), (up1, 16 * BLK, 1), (up2, 16 * BLK, 2)]
    names = items([(2, 1), (6, 1), (3, 2), (7, 2), (0, 2), (4, 2)])
    (up_in,) = packed([(blocks(names), True)], near)
    sources.append(up_in)
    up3 = send(up_in, names, 1)

    names = items([(5, 1), (6, 1), (7, 2)]) + [(4, 0, 0), (5, 0, 0)]
    (cross_in,) = packed([(blocks(names), True)], near, (up_in,))
    crossed = send(cross_in, names, 12)
    far = [(crossed, 16 * BLK, 12)]

    near = [(up3 - 1, 24 * BLK, 0), (up3, 24 * BLK, 1)]
    plans = ((items([(1, 1), (2, 2)]), 15), (items([(5, 1), (6, 2)]), 3))
    inputs = packed([(blocks(names), True) for names, _ in plans], near)
    far.append((len(sources), 8 * BLK, 0))
    sources.append(inputs[0])
    for array, (names, distance) in zip(inputs, plans, strict=True):
        far.append((send(array, names, distance), 8 * BLK, distance))

    names = items([(6, 2), (7, 3), (0, 3)])
    (cross_in,) = packed([(blocks(names), False)], (), (inputs[0],))
    send(cross_in, names, 12)

    early = items([(1, 1), (5, 13), (2, 2), (6, 14), (3, 3), (7, 15)]) + [(4, 12, 0)]
    early += items([(2, 1), (6, 13), (3, 2), (7, 14), (0, 15), (4, 3)]) + [(5, 12, 0)]

    def pass_on(names, after=()):
        entries = [(at[name][0], at[name][1] + b) for name in names for b, _ in passed_on(name)]
        (array,) = packed([(entries, False)], (), after)
        return from_other_core(array)

    early_other = pass_on(early)

    names = items([(1, 16), (5, 4), (2, 17), (6, 5), (0, 15), (4, 3)])
    up_in, notes = packed([(blocks(names), False), ((), True)], far)
    send(up_in, names, 1)
    notes = (notes, from_other_core(notes))

    late = items([(1, 16), (5, 4), (2, 17), (6, 5)])
    late += items([(1, 17), (5, 5), (2, 18), (6, 6), (0, 16), (4, 4)])


    def part_of(names):
        by_source = {}
        for name in names:
            source, place = at[name]
            for b, panel in wanted(name):
                by_source.setdefault(source, []).append(((place + b) * BLK, 0, name[2], name[1], panel))
        found = sorted(by_source.items())
        return [(sources[source], rows) for source, rows in found]

    def received_of(array, names):
        rows = []
        for name in names:
            for _, panel in passed_on(name):
                rows.append((len(rows) * BLK, 1, name[2], name[1], panel))
        return [(array, rows)]

    parts = [
        part_of(items([(0, 0), (1, 0)]) + early) + received_of(early_other, early),
        part_of(late),
        received_of(None, late),
    ]
    order = [row for part in parts for _, rows in part for row in rows]
    right_codes = right[:, STEPS * BLK, :6].astype(jnp.int32)
    right_codes = right_codes[:, :3] * 16 + right_codes[:, 3:] - 1
    table = tables(order, notes, right_codes, c_code.reshape(KEPT), start, core)

    def product_of(part, base, before=None, last=False):
        lefts, counts = [array for array, _ in part], tuple(len(rows) for _, rows in part)
        return product(table, right, lefts, counts, base, before, last), base + sum(counts)

    sums, base = product_of(parts[0], 0)
    late_other = pass_on(late, (sums,))
    sums, base = product_of(parts[1], base, sums)
    parts[2] = received_of(late_other, late)
    out, base = product_of(parts[2], base, sums, last=True)
    return out[None, None]


def solution(mesh):
    fine = Mesh(mesh.devices.reshape(SIZES), AXES)
    return jax.shard_map(
        local,
        mesh=fine,
        in_specs=(
            P(ROW, COL, None, None, None, None),
            P(ROW, COL, None, None),
            P(ROW, COL, None, None, None, None),
            P(ROW, COL, None, None),
            P(ROW, COL, None),
        ),
        out_specs=P(ROW, COL, None, None, None),
        check_vma=False,
    )
```

```python
import functools

import jax
import jax.numpy as jnp
import numpy as np
from jax import lax
from jax.experimental import pallas as pl
from jax.experimental.pallas import tpu as pltpu
from jax.sharding import Mesh
from jax.sharding import PartitionSpec as P

AXES = ("xl", "y", "xh", "z", "core")
ROW = ("xl", "y")
COL = ("xh", "z", "core")
SIZES = (2, 8, 2, 12, 2)
NQ = 24
NOTE = 2 * NQ
BC = 16
PANEL = 48
STEPS = 3
KEPT = 12
BLK = 128


def items(pairs):
    return [(a, d, k) for a, d in pairs for k in range(2)]


def wanted(name):
    a, d, _ = name
    return [(0, 0), (1, 1)] if (d - a) % 8 == 0 else [(0, 2)]


def passed_on(name):
    a, d, _ = name
    return [(1, 2)] if (d - a) % 8 == 0 else [(0, 1), (1, 0)]


VMEM = pltpu.VMEM
SMEM_SPEC = pl.BlockSpec(memory_space=pltpu.SMEM)
VMEM_SPEC = pl.BlockSpec(memory_space=pltpu.VMEM)
ANY_SPEC = pl.BlockSpec(memory_space=pl.ANY)
LIMIT = pltpu.CompilerParams(vmem_limit_bytes=16 << 20)


def moves(blocks):
    return pl.CostEstimate(flops=0, bytes_accessed=2 * blocks * BLK * BLK * 2, transcendentals=0)


def rows_shape(rows):
    return jax.ShapeDtypeStruct((rows, BLK), jnp.bfloat16)


def blk(n):
    return pl.ds(n * BLK, BLK)


def first_kernel(orders, index_ref, own_ref, other_ref, note_ref, *outs):
    for out, order in zip(outs, orders, strict=True):
        for n, (other, place) in enumerate(order):
            out[blk(n), :] = (other_ref if other else own_ref)[index_ref[place]]
        out[pl.ds(len(order) * BLK, 16), :] = note_ref[...]


def first_packed(index, own, other, note, orders):
    return pl.pallas_call(
        functools.partial(first_kernel, orders),
        out_shape=[rows_shape(len(order) * BLK + 16) for order in orders],
        in_specs=[SMEM_SPEC] + [VMEM_SPEC] * 3,
        out_specs=[VMEM_SPEC for _ in orders],
        compiler_params=LIMIT,
        cost_estimate=moves(sum(len(order) for order in orders)),
    )(index, own, other, note)


def right_kernel(index_ref, src_ref, code_ref, out):
    for n in range(16):
        for t in range(STEPS):
            out[n, pl.ds(t * BLK, BLK), :] = src_ref[index_ref[n + t]]
        out[n, pl.ds(STEPS * BLK, 16), :] = code_ref[n]


def right_packed(src, index, codes):
    return pl.pallas_call(
        right_kernel,
        out_shape=jax.ShapeDtypeStruct((16, STEPS * BLK + 16, BLK), jnp.bfloat16),
        in_specs=[SMEM_SPEC, VMEM_SPEC, VMEM_SPEC],
        out_specs=VMEM_SPEC,
        compiler_params=LIMIT,
        cost_estimate=moves(48),
    )(index, src, codes)


def turned(note, distance):
    if distance == 0:
        return note
    return jnp.concatenate([pltpu.roll(note[n : n + NQ], distance, 0) for n in (0, NQ)])


def pack_kernel(spec, notes, count, *refs):
    sources, outs = refs[:count], refs[-len(spec) :]
    if notes:
        merged = None
        rows = lax.broadcasted_iota(jnp.int32, (NOTE, BLK), 0)
        for source, row, distance, small in notes:
            if small:
                note = sources[source][pl.ds(row, 16), :].astype(jnp.float32)
                other = jnp.where(rows == NQ + distance, note[1:2], 0.0)
                note = jnp.where(rows == distance, note[0:1], other)
            else:
                note = turned(sources[source][pl.ds(row, NOTE), :].astype(jnp.float32), distance)
            merged = note if merged is None else jnp.maximum(merged, note)
        merged = merged.astype(jnp.bfloat16)
    for out, (entries, noted) in zip(outs, spec, strict=True):
        for n, (source, place) in enumerate(entries):
            out[blk(n), :] = sources[source][blk(place), :]
        if noted:
            out[pl.ds(len(entries) * BLK, NOTE), :] = merged


def pack(sources, spec, notes, after):
    used = sorted({e[0] for entries, _ in spec for e in entries} | {n[0] for n in notes})
    where = {source: n for n, source in enumerate(used)}
    spec = tuple((tuple((where[s], n) for s, n in entries), noted) for entries, noted in spec)
    notes = tuple((where[n[0]],) + tuple(n[1:]) for n in notes)
    return pl.pallas_call(
        functools.partial(pack_kernel, spec, notes, len(used)),
        out_shape=[rows_shape(len(entries) * BLK + NOTE * noted) for entries, noted in spec],
        in_specs=[VMEM_SPEC] * len(used) + [ANY_SPEC] * len(after),
        out_specs=[VMEM_SPEC for _ in spec],
        compiler_params=LIMIT,
        cost_estimate=moves(sum(len(entries) for entries, _ in spec)),
    )(*[sources[source] for source in used], *after)


def product_kernel(counts, base, first, last, table_ref, right_ref, *rest):
    lefts, rest = rest[: len(counts)], rest[len(counts) :]
    if last:
        before, out_ref, acc = rest
        acc[...] = before[...]
    elif first:
        (acc,) = rest
        acc[...] = jnp.zeros_like(acc)
    else:
        before, acc = rest
        acc[...] = before[...]
    for left, count in zip(lefts, counts, strict=True):

        def body(n, carry, left=left, base=base):
            block = left[pl.ds(pl.multiple_of(table_ref[6, base + n], BLK), BLK), :]
            pair = []
            for rank in range(2):
                owner = table_ref[3 * rank, base + n]
                row = pl.multiple_of(table_ref[3 * rank + 1, base + n], BLK)
                pair.append(right_ref[owner, pl.ds(row, BLK), :])
            both = jnp.dot(block, jnp.concatenate(pair, axis=1), preferred_element_type=jnp.float32)
            acc[table_ref[2, base + n]] += both[:, :BLK]
            acc[table_ref[5, base + n]] += both[:, BLK:]
            return carry

        unroll = max(n for n in (7, 6, 5, 4, 3, 2, 1) if count % n == 0)
        lax.fori_loop(0, count, body, 0, unroll=unroll)
        base += count
    if last:
        out_ref[...] = acc[:KEPT].astype(out_ref.dtype)


def product(table, right, lefts, counts, base, before=None, last=False):
    total = sum(counts)
    sums = jax.ShapeDtypeStruct((KEPT + 1, BLK, BLK), jnp.float32)
    return pl.pallas_call(
        functools.partial(product_kernel, counts, base, before is None, last),
        out_shape=jax.ShapeDtypeStruct((KEPT, BLK, BLK), jnp.bfloat16) if last else sums,
        in_specs=[SMEM_SPEC] + [VMEM_SPEC] * (1 + len(lefts) + (before is not None)),
        out_specs=VMEM_SPEC,
        scratch_shapes=[VMEM(sums.shape, jnp.float32)] if last else [],
        compiler_params=LIMIT,
        cost_estimate=pl.CostEstimate(
            flops=total * 16 * BLK**3, bytes_accessed=total * BLK * BLK * 2, transcendentals=0
        ),
    )(table, right, *lefts, *(() if before is None else (before,)))


def tables(order, notes, right_codes, c_code, start, core):
    order = np.array(order, np.int32)
    count = order.shape[0]
    row, other, k, distance, panel = (order[:, n] for n in range(5))
    notes = jnp.stack(notes)[:, :, :32].astype(jnp.int32)
    flat = (notes[:, :, :16] * 64 + notes[:, :, 16:] - 1).reshape(1, 2 * NOTE * 16)
    of = (start + panel + core * (3 - 2 * panel)) % 16
    place = (other * NOTE + k * NQ + distance) * 16 + of
    codes = jnp.sum(jnp.where(place[:, None] == jnp.arange(2 * NOTE * 16)[None, :], flat, 0), axis=1)
    step = panel + core * (2 - 2 * panel)
    right_live = right_codes >= 0
    right_inner = jnp.where(right_live, right_codes // BC, -1)
    owners = jnp.arange(16, dtype=jnp.int32)
    earlier = owners[None, :] < owners[:, None]
    rank = jnp.sum(
        ((right_inner[:, None, :] == right_inner[None, :, :]) & earlier[:, :, None]).astype(jnp.int32),
        axis=1,
    )
    packed = jnp.where(right_live, right_inner * 1024 + rank * 32 + right_codes % BC, -1)
    right_n = jnp.where(
        (step == 0)[:, None],
        packed[None, :, 0],
        jnp.where((step == 1)[:, None], packed[None, :, 1], packed[None, :, 2]),
    )
    match = (right_n >= 0) & (codes >= 0)[:, None] & ((right_n // 1024) == (codes % PANEL)[:, None])
    rows = []
    for rank_number in range(2):
        hit = match & ((right_n // 32) % 32 == rank_number)
        found = jnp.sum(jnp.where(hit, owners[None, :] * 32 + right_n % 32 + 1, 0), axis=1)
        partner = jnp.maximum(found - 1, 0)
        target = (codes // PANEL) * BC + partner % 32
        there = (target[:, None] == c_code[None, :]) & (found > 0)[:, None]
        slot = jnp.sum(jnp.where(there, jnp.arange(KEPT)[None, :] - KEPT, 0), axis=1) + KEPT
        rows += [partner // 32, step * BLK, slot]
    return jnp.stack(rows + [jnp.array(row)]).astype(jnp.int32).reshape(7, count)


def moved(array, distance):
    route = []
    for i in range(NQ):
        route.append((2 * i, 2 * ((i + distance) % NQ)))
        route.append((2 * i + 1, 2 * ((i - distance) % NQ) + 1))
    return lax.ppermute(array, COL, route)


def from_other_core(array):
    return lax.ppermute(array, "core", [(0, 1), (1, 0)])


def local(a_own_values, a_own_code, b_own_values, b_own_code, c_code):
    r = lax.axis_index(ROW)
    q = lax.axis_index(("xh", "z"))
    core = lax.axis_index("core")
    start = (r + 2 * q) % 16
    a_own = a_own_values.reshape(16, BLK, BLK)
    b_own = b_own_values.reshape(16, BLK, BLK)

    sources, at = [], {}

    def keep(array, names):
        for n, name in enumerate(names):
            at[name] = (len(sources), 2 * n)
        sources.append(array)
        return len(sources) - 1

    def send(array, names, distance):
        return keep(moved(array, distance), [(a, (d + distance) % NQ, k) for a, d, k in names])

    def blocks(names):
        return [(at[name][0], at[name][1] + b) for name in names for b in range(2)]

    def packed(spec, notes=(), after=()):
        return pack(sources, spec, notes, after)

    code = a_own_code.reshape(16) + 1
    note = jnp.concatenate([code // 64, code % 64]).astype(jnp.bfloat16).reshape(1, 32)
    note = jnp.pad(note, ((0, 15), (0, BLK - 32)))
    a_other, note_other = from_other_core(a_own), from_other_core(note)
    note = jnp.concatenate([note[:1], note_other[:1], note[2:]])
    a_index = jnp.arange(16, dtype=jnp.int32)
    a_index = (start + jnp.where(core == 0, a_index, 3 - a_index)) % 16

    starts = [
        (items([(3, 0), (4, 0)]), 2),
        (items([(7, 0), (0, 0)]), 14),
        (items([(1, 0), (2, 0)]), 1),
        (items([(5, 0), (6, 0)]), 13),
        ([(4, 0, 0), (5, 0, 0)], 12),
    ]
    orders = tuple(
        tuple((k, 2 * a + b) for a, _, k in names for b in range(2)) for names, _ in starts
    )
    arrays = first_packed(a_index, a_own, a_other, note, orders)
    near = []
    for array, (names, _) in zip(arrays[:4], starts[:4], strict=True):
        own = keep(array, names)
    near.append((own, 8 * BLK, 0, True))
    for array, (names, distance) in zip(arrays, starts, strict=True):
        near.append((send(array, names, distance), 2 * len(names) * BLK, distance, True))
    crossed = near.pop()

    shift = (2 * q + core + jnp.arange(18, dtype=jnp.int32)) % 16
    b_code = b_own_code.reshape(16) + 1
    b_code = jnp.sum(jnp.where(shift[:, None] == jnp.arange(16)[None, :], b_code[None, :], 0), axis=1)
    b_code = jnp.stack([b_code[t : t + 16] for t in range(STEPS)], axis=1)
    b_code = jnp.concatenate([b_code // 16, b_code % 16], axis=1).astype(jnp.bfloat16)
    b_code = jnp.broadcast_to(jnp.pad(b_code, ((0, 0), (0, BLK - 6)))[:, None, :], (16, 16, BLK))
    right = right_packed(b_own, shift, b_code)
    right = lax.all_to_all(right, ROW, 0, 0, tiled=True)

    names = items([(2, 1), (6, 13), (3, 2), (7, 14), (0, 14), (4, 2)])
    (up_in,) = packed([(blocks(names), True)], near)
    sources.append(up_in)
    up3 = send(up_in, names, 1)
    middle = [(up3 - 1, 24 * BLK, 0, False), (up3, 24 * BLK, 1, False)]

    names = items([(1, 1), (5, 13), (2, 2), (6, 14)])
    (up_in,) = packed([(blocks(names), True)], middle)
    up6 = send(up_in, names, 15)
    middle.append(crossed)
    far = middle + [(up6, 16 * BLK, 15, False)]

    early = items([(1, 1), (5, 13), (2, 2), (6, 14), (3, 3), (7, 15)]) + [(4, 12, 0)]
    early += items([(2, 1), (6, 13), (3, 2), (7, 14), (0, 15), (4, 3)]) + [(5, 12, 0)]

    def pass_on(names, noted, notes=(), after=()):
        entries = [(at[name][0], at[name][1] + b) for name in names for b, _ in passed_on(name)]
        (array,) = packed([(entries, noted)], notes, after)
        received = from_other_core(array)
        end = len(entries) * BLK
        return received, (array[end:], received[end:])

    early_other, early_notes = pass_on(early, True, middle, (up_in,))

    names = items([(1, 16), (5, 4), (2, 17), (6, 5), (0, 15), (4, 3)])
    up_in, notes = packed([(blocks(names), False), ((), True)], far)
    send(up_in, names, 1)
    notes = (notes, from_other_core(notes))

    late = items([(1, 16), (5, 4), (2, 17), (6, 5)])
    late += items([(1, 17), (5, 5), (2, 18), (6, 6), (0, 16), (4, 4)])

    def part_of(names):
        by_source = {}
        for name in names:
            source, place = at[name]
            for b, panel in wanted(name):
                by_source.setdefault(source, []).append(((place + b) * BLK, 0, name[2], name[1], panel))
        return [(sources[source], rows) for source, rows in sorted(by_source.items())]

    def received_of(array, names):
        rows = []
        for name in names:
            for _, panel in passed_on(name):
                rows.append((len(rows) * BLK, 1, name[2], name[1], panel))
        return [(array, rows)]

    right_codes = right[:, STEPS * BLK, :6].astype(jnp.int32)
    right_codes = right_codes[:, :3] * 16 + right_codes[:, 3:] - 1
    c_code = c_code.reshape(KEPT)

    def table_of(parts, notes):
        order = [row for part in parts for _, rows in part for row in rows]
        return tables(order, notes, right_codes, c_code, start, core)

    def product_of(table, part, base, before=None, last=False):
        lefts, counts = [array for array, _ in part], tuple(len(rows) for _, rows in part)
        return product(table, right, lefts, counts, base, before, last), base + sum(counts)

    part = part_of(items([(0, 0), (1, 0)]) + early) + received_of(early_other, early)
    sums, _ = product_of(table_of((part,), early_notes), part, 0)
    parts = [part_of(late), received_of(None, late)]
    table = table_of(parts, notes)
    late_other, _ = pass_on(late, False, (), (sums,))
    sums, base = product_of(table, parts[0], 0, sums)
    out, _ = product_of(table, received_of(late_other, late), base, sums, last=True)
    return out[None, None]


def solution(mesh):
    fine = Mesh(mesh.devices.reshape(SIZES), AXES)
    return jax.shard_map(
        local,
        mesh=fine,
        in_specs=(
            P(ROW, COL, None, None, None, None),
            P(ROW, COL, None, None),
            P(ROW, COL, None, None, None, None),
            P(ROW, COL, None, None),
            P(ROW, COL, None),
        ),
        out_specs=P(ROW, COL, None, None, None),
        check_vma=False,
    )
```

```python
import functools

import jax
import jax.numpy as jnp
import numpy as np
from jax import lax
from jax.experimental import pallas as pl
from jax.experimental.pallas import tpu as pltpu
from jax.sharding import Mesh
from jax.sharding import PartitionSpec as P

AXES = ("xl", "y", "xh", "z", "core")
ROW = ("xl", "y")
COL = ("xh", "z", "core")
SIZES = (2, 8, 2, 12, 2)
NQ = 24
NOTE = 2 * NQ
BC = 16
PANEL = 48
STEPS = 3
KEPT = 12
SPAN = 8 + STEPS - 1
BLK = 128


def items(pairs):
    return [(a, d, k) for a, d in pairs for k in range(2)]


def wanted(name):
    a, d, _ = name
    return [(0, 0), (1, 1)] if (d - a) % 8 == 0 else [(0, 2)]


def passed_on(name):
    a, d, _ = name
    return [(1, 2)] if (d - a) % 8 == 0 else [(0, 1), (1, 0)]


VMEM = pltpu.VMEM
SMEM_SPEC = pl.BlockSpec(memory_space=pltpu.SMEM)
VMEM_SPEC = pl.BlockSpec(memory_space=pltpu.VMEM)
ANY_SPEC = pl.BlockSpec(memory_space=pl.ANY)
LIMIT = pltpu.CompilerParams(vmem_limit_bytes=16 << 20)


def moves(blocks):
    return pl.CostEstimate(flops=0, bytes_accessed=2 * blocks * BLK * BLK * 2, transcendentals=0)


def rows_shape(rows):
    return jax.ShapeDtypeStruct((rows, BLK), jnp.bfloat16)


def blk(n):
    return pl.ds(n * BLK, BLK)


def first_kernel(orders, index_ref, own_ref, other_ref, note_ref, *outs):
    for out, order in zip(outs, orders, strict=True):
        for n, (other, place) in enumerate(order):
            out[blk(n), :] = (other_ref if other else own_ref)[index_ref[place]]
        out[pl.ds(len(order) * BLK, 16), :] = note_ref[...]


def first_packed(index, own, other, note, orders):
    return pl.pallas_call(
        functools.partial(first_kernel, orders),
        out_shape=[rows_shape(len(order) * BLK + 16) for order in orders],
        in_specs=[SMEM_SPEC] + [VMEM_SPEC] * 3,
        out_specs=[VMEM_SPEC for _ in orders],
        compiler_params=LIMIT,
        cost_estimate=moves(sum(len(order) for order in orders)),
    )(index, own, other, note)


def split_kernel(index_ref, src_ref, note_ref, *outs):
    for half, out in enumerate(outs):
        for n in range(SPAN):
            out[blk(n), :] = src_ref[index_ref[SPAN * half + n]]
        out[pl.ds(SPAN * BLK, 16), :] = note_ref[...]


def split(index, src, note):
    return pl.pallas_call(
        split_kernel,
        out_shape=[rows_shape(SPAN * BLK + 16)] * 2,
        in_specs=[SMEM_SPEC, VMEM_SPEC, VMEM_SPEC],
        out_specs=[VMEM_SPEC] * 2,
        compiler_params=LIMIT,
        cost_estimate=moves(2 * SPAN),
    )(index, src, note)


def chosen_kernel(index_ref, *rest):
    sources, out, sems = rest[:2], rest[2], rest[3]
    copies = []
    for half, src in enumerate(sources):
        for n in range(8):
            for t in range(STEPS):
                row = pl.multiple_of(index_ref[t] * BLK, BLK)
                place = blk((half * STEPS + t) * 8 + n)
                copies.append((src.at[n, pl.ds(row, BLK)], out.at[place]))
            tail = pl.ds(STEPS * 16 * BLK + 16 * (8 * half + n), 16)
            copies.append((src.at[n, pl.ds(SPAN * BLK, 16)], out.at[tail]))
    copies = [pltpu.make_async_copy(a, b, sems.at[n]) for n, (a, b) in enumerate(copies)]
    for copy in copies:
        copy.start()
    for copy in copies:
        copy.wait()


def chosen(index, sources):
    return pl.pallas_call(
        chosen_kernel,
        out_shape=rows_shape(STEPS * 16 * BLK + 16 * 16),
        in_specs=[SMEM_SPEC, ANY_SPEC, ANY_SPEC],
        out_specs=VMEM_SPEC,
        scratch_shapes=[pltpu.SemaphoreType.DMA((2 * 8 * (STEPS + 1),))],
        compiler_params=LIMIT,
        cost_estimate=moves(48),
    )(index, *sources)


def turned(note, distance):
    if distance == 0:
        return note
    return jnp.concatenate([pltpu.roll(note[n : n + NQ], distance, 0) for n in (0, NQ)])


def pack_kernel(spec, notes, count, *refs):
    sources, outs = refs[:count], refs[-len(spec) :]
    if notes:
        merged = None
        rows = lax.broadcasted_iota(jnp.int32, (NOTE, BLK), 0)
        for source, row, distance, small in notes:
            if small:
                note = sources[source][pl.ds(row, 16), :].astype(jnp.float32)
                other = jnp.where(rows == NQ + distance, note[1:2], 0.0)
                note = jnp.where(rows == distance, note[0:1], other)
            else:
                note = turned(sources[source][pl.ds(row, NOTE), :].astype(jnp.float32), distance)
            merged = note if merged is None else jnp.maximum(merged, note)
        merged = merged.astype(jnp.bfloat16)
    for out, (entries, noted) in zip(outs, spec, strict=True):
        for n, (source, place) in enumerate(entries):
            out[blk(n), :] = sources[source][blk(place), :]
        if noted:
            out[pl.ds(len(entries) * BLK, NOTE), :] = merged


def pack(sources, spec, notes, after):
    used = sorted({e[0] for entries, _ in spec for e in entries} | {n[0] for n in notes})
    where = {source: n for n, source in enumerate(used)}
    spec = tuple((tuple((where[s], n) for s, n in entries), noted) for entries, noted in spec)
    notes = tuple((where[n[0]],) + tuple(n[1:]) for n in notes)
    return pl.pallas_call(
        functools.partial(pack_kernel, spec, notes, len(used)),
        out_shape=[rows_shape(len(entries) * BLK + NOTE * noted) for entries, noted in spec],
        in_specs=[VMEM_SPEC] * len(used) + [ANY_SPEC] * len(after),
        out_specs=[VMEM_SPEC for _ in spec],
        compiler_params=LIMIT,
        cost_estimate=moves(sum(len(entries) for entries, _ in spec)),
    )(*[sources[source] for source in used], *after)


def product_kernel(counts, base, first, last, table_ref, right_ref, *rest):
    lefts, rest = rest[: len(counts)], rest[len(counts) :]
    if last:
        before, out_ref, acc = rest
        acc[...] = before[...]
    elif first:
        (acc,) = rest
        acc[...] = jnp.zeros_like(acc)
    else:
        before, acc = rest
        acc[...] = before[...]
    for left, count in zip(lefts, counts, strict=True):

        def body(n, carry, left=left, base=base):
            block = left[pl.ds(pl.multiple_of(table_ref[4, base + n], BLK), BLK), :]
            pair = []
            for rank in range(2):
                row = pl.multiple_of(table_ref[2 * rank, base + n], BLK)
                pair.append(right_ref[pl.ds(row, BLK), :])
            both = jnp.dot(block, jnp.concatenate(pair, axis=1), preferred_element_type=jnp.float32)
            acc[table_ref[1, base + n]] += both[:, :BLK]
            acc[table_ref[3, base + n]] += both[:, BLK:]
            return carry

        unroll = max(n for n in (7, 6, 5, 4, 3, 2, 1) if count % n == 0)
        lax.fori_loop(0, count, body, 0, unroll=unroll)
        base += count
    if last:
        out_ref[...] = acc[:KEPT].astype(out_ref.dtype)


def product(table, right, lefts, counts, base, before=None, last=False):
    total = sum(counts)
    sums = jax.ShapeDtypeStruct((KEPT + 1, BLK, BLK), jnp.float32)
    return pl.pallas_call(
        functools.partial(product_kernel, counts, base, before is None, last),
        out_shape=jax.ShapeDtypeStruct((KEPT, BLK, BLK), jnp.bfloat16) if last else sums,
        in_specs=[SMEM_SPEC] + [VMEM_SPEC] * (1 + len(lefts) + (before is not None)),
        out_specs=VMEM_SPEC,
        scratch_shapes=[VMEM(sums.shape, jnp.float32)] if last else [],
        compiler_params=LIMIT,
        cost_estimate=pl.CostEstimate(
            flops=total * 16 * BLK**3, bytes_accessed=total * BLK * BLK * 2, transcendentals=0
        ),
    )(table, right, *lefts, *(() if before is None else (before,)))


def tables(order, notes, right_codes, c_code, start, core):
    order = np.array(order, np.int32)
    count = order.shape[0]
    row, other, k, distance, panel = (order[:, n] for n in range(5))
    notes = jnp.stack(notes)[:, :, :32].astype(jnp.int32)
    flat = (notes[:, :, :16] * 64 + notes[:, :, 16:] - 1).reshape(1, 2 * NOTE * 16)
    of = (start + panel + core * (3 - 2 * panel)) % 16
    place = (other * NOTE + k * NQ + distance) * 16 + of
    codes = jnp.sum(jnp.where(place[:, None] == jnp.arange(2 * NOTE * 16)[None, :], flat, 0), axis=1)
    step = panel + core * (2 - 2 * panel)
    right_live = right_codes >= 0
    right_inner = jnp.where(right_live, right_codes // BC, -1)
    owners = jnp.arange(16, dtype=jnp.int32)
    earlier = owners[None, :] < owners[:, None]
    rank = jnp.sum(
        ((right_inner[:, None, :] == right_inner[None, :, :]) & earlier[:, :, None]).astype(jnp.int32),
        axis=1,
    )
    packed = jnp.where(right_live, right_inner * 1024 + rank * 32 + right_codes % BC, -1)
    right_n = jnp.where(
        (step == 0)[:, None],
        packed[None, :, 0],
        jnp.where((step == 1)[:, None], packed[None, :, 1], packed[None, :, 2]),
    )
    match = (right_n >= 0) & (codes >= 0)[:, None] & ((right_n // 1024) == (codes % PANEL)[:, None])
    rows = []
    for rank_number in range(2):
        hit = match & ((right_n // 32) % 32 == rank_number)
        found = jnp.sum(jnp.where(hit, owners[None, :] * 32 + right_n % 32 + 1, 0), axis=1)
        partner = jnp.maximum(found - 1, 0)
        target = (codes // PANEL) * BC + partner % 32
        there = (target[:, None] == c_code[None, :]) & (found > 0)[:, None]
        slot = jnp.sum(jnp.where(there, jnp.arange(KEPT)[None, :] - KEPT, 0), axis=1) + KEPT
        owner = partner // 32
        rows += [(owner // 8 * (8 * STEPS) + step * 8 + owner % 8) * BLK, slot]
    return jnp.stack(rows + [jnp.array(row)]).astype(jnp.int32).reshape(5, count)


def moved(array, distance):
    route = []
    for i in range(NQ):
        route.append((2 * i, 2 * ((i + distance) % NQ)))
        route.append((2 * i + 1, 2 * ((i - distance) % NQ) + 1))
    return lax.ppermute(array, COL, route)


def from_other_core(array):
    return lax.ppermute(array, "core", [(0, 1), (1, 0)])


def local(a_own_values, a_own_code, b_own_values, b_own_code, c_code):
    r = lax.axis_index(ROW)
    q = lax.axis_index(("xh", "z"))
    core = lax.axis_index("core")
    start = (r + 2 * q) % 16
    a_own = a_own_values.reshape(16, BLK, BLK)
    b_own = b_own_values.reshape(16, BLK, BLK)

    def note_of(code):
        code = code.reshape(16) + 1
        digits = jnp.concatenate([code // 64, code % 64]).astype(jnp.bfloat16).reshape(1, 32)
        return jnp.pad(digits, ((0, 15), (0, BLK - 32)))

    spans = 2 * q + core + 8 * lax.axis_index("xl") + jnp.arange(SPAN, dtype=jnp.int32)
    spans = jnp.concatenate([spans, spans + 8]) % 16
    b_kept, b_sent = split(spans, b_own, note_of(b_own_code))
    b_all = [lax.all_gather(b_kept, "y")]
    b_other = lax.ppermute(b_sent, "xl", [(0, 1), (1, 0)])

    sources, at = [], {}

    def keep(array, names):
        for n, name in enumerate(names):
            at[name] = (len(sources), 2 * n)
        sources.append(array)
        return len(sources) - 1

    def send(array, names, distance):
        return keep(moved(array, distance), [(a, (d + distance) % NQ, k) for a, d, k in names])

    def blocks(names):
        return [(at[name][0], at[name][1] + b) for name in names for b in range(2)]

    def packed(spec, notes=(), after=()):
        return pack(sources, spec, notes, after)

    note = note_of(a_own_code)
    a_other, note_other = from_other_core(a_own), from_other_core(note)
    note = jnp.concatenate([note[:1], note_other[:1], note[2:]])
    a_index = jnp.arange(16, dtype=jnp.int32)
    a_index = (start + jnp.where(core == 0, a_index, 3 - a_index)) % 16

    starts = [
        (items([(3, 0), (4, 0)]), 2),
        (items([(7, 0), (0, 0)]), 14),
        (items([(1, 0), (2, 0)]), 1),
        (items([(5, 0), (6, 0)]), 13),
        ([(4, 0, 0), (5, 0, 0)], 12),
    ]
    orders = tuple(
        tuple((k, 2 * a + b) for a, _, k in names for b in range(2)) for names, _ in starts
    )
    arrays = first_packed(a_index, a_own, a_other, note, orders)
    near = []
    for array, (names, _) in zip(arrays[:4], starts[:4], strict=True):
        own = keep(array, names)
    near.append((own, 8 * BLK, 0, True))
    for array, (names, distance) in zip(arrays, starts, strict=True):
        near.append((send(array, names, distance), 2 * len(names) * BLK, distance, True))

    b_other, _ = lax.optimization_barrier((b_other, sources[near[1][0]]))
    b_all.append(lax.all_gather(b_other, "y"))

    names = items([(2, 1), (6, 13), (3, 2), (7, 14), (0, 14), (4, 2)])
    (up_in,) = packed([(blocks(names), True)], near)
    sources.append(up_in)
    up3 = send(up_in, names, 1)
    middle = [(up3 - 1, 24 * BLK, 0, False), (up3, 24 * BLK, 1, False)]

    names = items([(1, 1), (5, 13), (2, 2), (6, 14)])
    (up_in,) = packed([(blocks(names), True)], middle)
    up6 = send(up_in, names, 15)
    far = middle + [(up6, 16 * BLK, 15, False)]

    early = items([(1, 1), (5, 13), (2, 2), (6, 14), (3, 3), (7, 15)]) + [(4, 12, 0)]
    early += items([(2, 1), (6, 13), (3, 2), (7, 14), (0, 15), (4, 3)]) + [(5, 12, 0)]

    def pass_on(names, kept=None, notes=(), after=()):
        entries = [(at[name][0], at[name][1] + b) for name in names for b, _ in passed_on(name)]
        spec = [(entries, bool(notes))]
        if kept:
            spec.append(([(at[name][0], at[name][1] + b) for name in kept for b, _ in wanted(name)], False))
        array, *own_part = packed(spec, notes, after)
        received = from_other_core(array)
        end = len(entries) * BLK
        return received, own_part, (array[end:], received[end:])

    mine = items([(0, 0), (1, 0)]) + early
    early_other, early_own, early_notes = pass_on(early, mine, middle, (up_in,))

    names = items([(1, 16), (5, 4), (2, 17), (6, 5), (0, 15), (4, 3)])
    up_in, notes = packed([(blocks(names), False), ((), True)], far)
    send(up_in, names, 1)
    notes = (notes, from_other_core(notes))

    late = items([(1, 16), (5, 4), (2, 17), (6, 5)])
    late += items([(1, 17), (5, 5), (2, 18), (6, 6), (0, 16), (4, 4)])

    def part_of(names):
        by_source = {}
        for name in names:
            source, place = at[name]
            for b, panel in wanted(name):
                by_source.setdefault(source, []).append(((place + b) * BLK, 0, name[2], name[1], panel))
        return [(sources[source], rows) for source, rows in sorted(by_source.items())]

    def received_of(array, names):
        rows = []
        for name in names:
            for _, panel in passed_on(name):
                rows.append((len(rows) * BLK, 1, name[2], name[1], panel))
        return [(array, rows)]

    panels = (start + core + jnp.arange(STEPS, dtype=jnp.int32)) % 16
    right = chosen(lax.axis_index("y") + jnp.arange(STEPS, dtype=jnp.int32), b_all)
    digits = right[STEPS * 16 * BLK :].reshape(16, 16, BLK)[:, 0, :32].astype(jnp.int32)
    right_codes = (digits[:, :16] * 64 + digits[:, 16:] - 1)[:, None, :]
    right_codes = jnp.sum(
        jnp.where(panels[:, None] == jnp.arange(16)[None, :], right_codes, 0), axis=2
    )
    c_code = c_code.reshape(KEPT)

    def table_of(parts, notes):
        order = [row for part in parts for _, rows in part for row in rows]
        return tables(order, notes, right_codes, c_code, start, core)

    def product_of(table, part, base, before=None, last=False):
        lefts, counts = [array for array, _ in part], tuple(len(rows) for _, rows in part)
        return product(table, right, lefts, counts, base, before, last), base + sum(counts)

    rows = []
    for name in mine:
        rows += [(len(rows) * BLK + n * BLK, 0, name[2], name[1], w) for n, (_, w) in enumerate(wanted(name))]
    part = [(early_own[0], rows)] + received_of(early_other, early)
    sums, _ = product_of(table_of((part,), early_notes), part, 0)
    parts = [part_of(late), received_of(None, late)]
    table = table_of(parts, notes)
    late_other, _, _ = pass_on(late, None, (), (sums,))
    sums, base = product_of(table, parts[0], 0, sums)
    out, _ = product_of(table, received_of(late_other, late), base, sums, last=True)
    return out[None, None]


def solution(mesh):
    fine = Mesh(mesh.devices.reshape(SIZES), AXES)
    return jax.shard_map(
        local,
        mesh=fine,
        in_specs=(
            P(ROW, COL, None, None, None, None),
            P(ROW, COL, None, None),
            P(ROW, COL, None, None, None, None),
            P(ROW, COL, None, None),
            P(ROW, COL, None),
        ),
        out_specs=P(ROW, COL, None, None, None),
        check_vma=False,
    )
```

```python
import functools

import jax
import jax.numpy as jnp
import numpy as np
from jax import lax
from jax.experimental import pallas as pl
from jax.experimental.pallas import tpu as pltpu
from jax.sharding import Mesh
from jax.sharding import PartitionSpec as P

AXES = ("xl", "y", "xh", "z", "core")
ROW = ("xl", "y")
COL = ("xh", "z", "core")
SIZES = (2, 8, 2, 12, 2)
NQ = 24
NOTE = 2 * NQ
BC = 16
PANEL = 48
STEPS = 3
KEPT = 12
BLK = 128


def items(pairs):
    return [(a, d, k) for a, d in pairs for k in range(2)]


def wanted(name):
    a, d, _ = name
    return [(0, 0), (1, 1)] if (d - a) % 8 == 0 else [(0, 2)]


def passed_on(name):
    a, d, _ = name
    return [(1, 2)] if (d - a) % 8 == 0 else [(0, 1), (1, 0)]


VMEM = pltpu.VMEM
SMEM_SPEC = pl.BlockSpec(memory_space=pltpu.SMEM)
VMEM_SPEC = pl.BlockSpec(memory_space=pltpu.VMEM)
ANY_SPEC = pl.BlockSpec(memory_space=pl.ANY)
LIMIT = pltpu.CompilerParams(vmem_limit_bytes=16 << 20)


def moves(blocks):
    return pl.CostEstimate(flops=0, bytes_accessed=2 * blocks * BLK * BLK * 2, transcendentals=0)


def rows_shape(rows):
    return jax.ShapeDtypeStruct((rows, BLK), jnp.bfloat16)


def blk(n):
    return pl.ds(n * BLK, BLK)


def first_kernel(orders, index_ref, own_ref, other_ref, note_ref, *outs):
    for out, order in zip(outs, orders, strict=True):
        for n, (other, place) in enumerate(order):
            out[blk(n), :] = (other_ref if other else own_ref)[index_ref[place]]
        out[pl.ds(len(order) * BLK, 16), :] = note_ref[...]


def first_packed(index, own, other, note, orders):
    return pl.pallas_call(
        functools.partial(first_kernel, orders),
        out_shape=[rows_shape(len(order) * BLK + 16) for order in orders],
        in_specs=[SMEM_SPEC] + [VMEM_SPEC] * 3,
        out_specs=[VMEM_SPEC for _ in orders],
        compiler_params=LIMIT,
        cost_estimate=moves(sum(len(order) for order in orders)),
    )(index, own, other, note)


def right_kernel(index_ref, src_ref, code_ref, out):
    for n in range(16):
        for t in range(STEPS):
            out[n, pl.ds(t * BLK, BLK), :] = src_ref[index_ref[n + t]]
        out[n, pl.ds(STEPS * BLK, 16), :] = code_ref[n]


def right_packed(src, index, codes):
    return pl.pallas_call(
        right_kernel,
        out_shape=jax.ShapeDtypeStruct((16, STEPS * BLK + 16, BLK), jnp.bfloat16),
        in_specs=[SMEM_SPEC, VMEM_SPEC, VMEM_SPEC],
        out_specs=VMEM_SPEC,
        compiler_params=LIMIT,
        cost_estimate=moves(48),
    )(index, src, codes)


def turned(note, distance):
    if distance == 0:
        return note
    return jnp.concatenate([pltpu.roll(note[n : n + NQ], distance, 0) for n in (0, NQ)])


def pack_kernel(spec, notes, count, *refs):
    sources, outs = refs[:count], refs[-len(spec) :]
    if notes:
        merged = None
        rows = lax.broadcasted_iota(jnp.int32, (NOTE, BLK), 0)
        for source, row, distance, small in notes:
            if small:
                note = sources[source][pl.ds(row, 16), :].astype(jnp.float32)
                other = jnp.where(rows == NQ + distance, note[1:2], 0.0)
                note = jnp.where(rows == distance, note[0:1], other)
            else:
                note = turned(sources[source][pl.ds(row, NOTE), :].astype(jnp.float32), distance)
            merged = note if merged is None else jnp.maximum(merged, note)
        merged = merged.astype(jnp.bfloat16)
    for out, (entries, noted) in zip(outs, spec, strict=True):
        for n, (source, place) in enumerate(entries):
            out[blk(n), :] = sources[source][blk(place), :]
        if noted:
            out[pl.ds(len(entries) * BLK, NOTE), :] = merged


def pack(sources, spec, notes, after):
    used = sorted({e[0] for entries, _ in spec for e in entries} | {n[0] for n in notes})
    where = {source: n for n, source in enumerate(used)}
    spec = tuple((tuple((where[s], n) for s, n in entries), noted) for entries, noted in spec)
    notes = tuple((where[n[0]],) + tuple(n[1:]) for n in notes)
    return pl.pallas_call(
        functools.partial(pack_kernel, spec, notes, len(used)),
        out_shape=[rows_shape(len(entries) * BLK + NOTE * noted) for entries, noted in spec],
        in_specs=[VMEM_SPEC] * len(used) + [ANY_SPEC] * len(after),
        out_specs=[VMEM_SPEC for _ in spec],
        compiler_params=LIMIT,
        cost_estimate=moves(sum(len(entries) for entries, _ in spec)),
    )(*[sources[source] for source in used], *after)


def product_kernel(counts, base, first, last, table_ref, right_ref, *rest):
    lefts, rest = rest[: len(counts)], rest[len(counts) :]
    if last:
        before, out_ref, acc = rest
        acc[...] = before[...]
    elif first:
        (acc,) = rest
        acc[...] = jnp.zeros_like(acc)
    else:
        before, acc = rest
        acc[...] = before[...]
    for left, count in zip(lefts, counts, strict=True):

        def body(n, carry, left=left, base=base):
            block = left[pl.ds(pl.multiple_of(table_ref[6, base + n], BLK), BLK), :]
            pair = []
            for rank in range(2):
                owner = table_ref[3 * rank, base + n]
                row = pl.multiple_of(table_ref[3 * rank + 1, base + n], BLK)
                pair.append(right_ref[owner, pl.ds(row, BLK), :])
            both = jnp.dot(block, jnp.concatenate(pair, axis=1), preferred_element_type=jnp.float32)
            acc[table_ref[2, base + n]] += both[:, :BLK]
            acc[table_ref[5, base + n]] += both[:, BLK:]
            return carry

        unroll = max(n for n in (7, 6, 5, 4, 3, 2, 1) if count % n == 0)
        lax.fori_loop(0, count, body, 0, unroll=unroll)
        base += count
    if last:
        out_ref[...] = acc[:KEPT].astype(out_ref.dtype)


def product(table, right, lefts, counts, base, before=None, last=False):
    total = sum(counts)
    sums = jax.ShapeDtypeStruct((KEPT + 1, BLK, BLK), jnp.float32)
    return pl.pallas_call(
        functools.partial(product_kernel, counts, base, before is None, last),
        out_shape=jax.ShapeDtypeStruct((KEPT, BLK, BLK), jnp.bfloat16) if last else sums,
        in_specs=[SMEM_SPEC] + [VMEM_SPEC] * (1 + len(lefts) + (before is not None)),
        out_specs=VMEM_SPEC,
        scratch_shapes=[VMEM(sums.shape, jnp.float32)] if last else [],
        compiler_params=LIMIT,
        cost_estimate=pl.CostEstimate(
            flops=total * 16 * BLK**3, bytes_accessed=total * BLK * BLK * 2, transcendentals=0
        ),
    )(table, right, *lefts, *(() if before is None else (before,)))


def tables(order, notes, right_codes, c_code, start, core):
    order = np.array(order, np.int32)
    count = order.shape[0]
    row, other, k, distance, panel = (order[:, n] for n in range(5))
    notes = jnp.stack(notes)[:, :, :32].astype(jnp.int32)
    flat = (notes[:, :, :16] * 64 + notes[:, :, 16:] - 1).reshape(1, 2 * NOTE * 16)
    of = (start + panel + core * (3 - 2 * panel)) % 16
    place = (other * NOTE + k * NQ + distance) * 16 + of
    codes = jnp.sum(jnp.where(place[:, None] == jnp.arange(2 * NOTE * 16)[None, :], flat, 0), axis=1)
    step = panel + core * (2 - 2 * panel)
    right_live = right_codes >= 0
    right_inner = jnp.where(right_live, right_codes // BC, -1)
    owners = jnp.arange(16, dtype=jnp.int32)
    earlier = owners[None, :] < owners[:, None]
    rank = jnp.sum(
        ((right_inner[:, None, :] == right_inner[None, :, :]) & earlier[:, :, None]).astype(jnp.int32),
        axis=1,
    )
    packed = jnp.where(right_live, right_inner * 1024 + rank * 32 + right_codes % BC, -1)
    right_n = jnp.where(
        (step == 0)[:, None],
        packed[None, :, 0],
        jnp.where((step == 1)[:, None], packed[None, :, 1], packed[None, :, 2]),
    )
    match = (right_n >= 0) & (codes >= 0)[:, None] & ((right_n // 1024) == (codes % PANEL)[:, None])
    rows = []
    for rank_number in range(2):
        hit = match & ((right_n // 32) % 32 == rank_number)
        found = jnp.sum(jnp.where(hit, owners[None, :] * 32 + right_n % 32 + 1, 0), axis=1)
        partner = jnp.maximum(found - 1, 0)
        target = (codes // PANEL) * BC + partner % 32
        there = (target[:, None] == c_code[None, :]) & (found > 0)[:, None]
        slot = jnp.sum(jnp.where(there, jnp.arange(KEPT)[None, :] - KEPT, 0), axis=1) + KEPT
        rows += [partner // 32, step * BLK, slot]
    return jnp.stack(rows + [jnp.array(row)]).astype(jnp.int32).reshape(7, count)


def moved(array, distance):
    route = []
    for i in range(NQ):
        route.append((2 * i, 2 * ((i + distance) % NQ)))
        route.append((2 * i + 1, 2 * ((i - distance) % NQ) + 1))
    return lax.ppermute(array, COL, route)


def from_other_core(array):
    return lax.ppermute(array, "core", [(0, 1), (1, 0)])


def local(a_own_values, a_own_code, b_own_values, b_own_code, c_code):
    r = lax.axis_index(ROW)
    q = lax.axis_index(("xh", "z"))
    core = lax.axis_index("core")
    start = (r + 2 * q) % 16
    a_own = a_own_values.reshape(16, BLK, BLK)
    b_own = b_own_values.reshape(16, BLK, BLK)

    sources, at = [], {}

    def keep(array, names):
        for n, name in enumerate(names):
            at[name] = (len(sources), 2 * n)
        sources.append(array)
        return len(sources) - 1

    def send(array, names, distance):
        return keep(moved(array, distance), [(a, (d + distance) % NQ, k) for a, d, k in names])

    def blocks(names):
        return [(at[name][0], at[name][1] + b) for name in names for b in range(2)]

    def packed(spec, notes=(), after=()):
        return pack(sources, spec, notes, after)

    code = a_own_code.reshape(16) + 1
    note = jnp.concatenate([code // 64, code % 64]).astype(jnp.bfloat16).reshape(1, 32)
    note = jnp.pad(note, ((0, 15), (0, BLK - 32)))
    a_other, note_other = from_other_core(a_own), from_other_core(note)
    note = jnp.concatenate([note[:1], note_other[:1], note[2:]])
    a_index = jnp.arange(16, dtype=jnp.int32)
    a_index = (start + jnp.where(core == 0, a_index, 3 - a_index)) % 16

    starts = [
        (items([(3, 0), (4, 0)]), 2),
        (items([(7, 0), (0, 0)]), 14),
        (items([(1, 0), (2, 0)]), 1),
        (items([(5, 0), (6, 0)]), 13),
        ([(4, 0, 0), (5, 0, 0)], 12),
    ]
    orders = tuple(
        tuple((k, 2 * a + b) for a, _, k in names for b in range(2)) for names, _ in starts
    )
    arrays = first_packed(a_index, a_own, a_other, note, orders)
    near = []
    for array, (names, _) in zip(arrays[:4], starts[:4], strict=True):
        own = keep(array, names)
    near.append((own, 8 * BLK, 0, True))
    for array, (names, distance) in zip(arrays, starts, strict=True):
        near.append((send(array, names, distance), 2 * len(names) * BLK, distance, True))

    shift = (2 * q + core + jnp.arange(18, dtype=jnp.int32)) % 16
    b_code = b_own_code.reshape(16) + 1
    b_code = jnp.sum(jnp.where(shift[:, None] == jnp.arange(16)[None, :], b_code[None, :], 0), axis=1)
    b_code = jnp.stack([b_code[t : t + 16] for t in range(STEPS)], axis=1)
    b_code = jnp.concatenate([b_code // 16, b_code % 16], axis=1).astype(jnp.bfloat16)
    b_code = jnp.broadcast_to(jnp.pad(b_code, ((0, 0), (0, BLK - 6)))[:, None, :], (16, 16, BLK))
    right = right_packed(b_own, shift, b_code)
    right = lax.all_to_all(right, ROW, 0, 0, tiled=True)

    names = items([(2, 1), (6, 13), (3, 2), (7, 14), (0, 14), (4, 2)])
    long_names = items([(1, 1), (5, 13)])
    up_in, long_in = packed([(blocks(names), True), (blocks(long_names), False)], near)
    sources.append(up_in)
    up3 = send(up_in, names, 1)
    send(long_in, long_names, 15)
    middle = [(up3 - 1, 24 * BLK, 0, False), (up3, 24 * BLK, 1, False)]

    names = items([(0, 15), (4, 3), (1, 16), (5, 4)])
    long_names = items([(2, 2), (6, 14)])
    long_in, up_in = packed([(blocks(long_names), True), (blocks(names), False)], middle)
    long = send(long_in, long_names, 15)
    far = middle + [(long, 8 * BLK, 15, False)]
    up7 = send(up_in, names, 1)
    send(sources[long], items([(2, 17), (6, 5)]), 1)

    early = items([(1, 1), (5, 13), (2, 2), (6, 14), (3, 3), (7, 15)]) + [(4, 12, 0)]
    early += items([(2, 1), (6, 13), (3, 2), (7, 14), (0, 15), (4, 3)]) + [(5, 12, 0)]
    mine = items([(0, 0), (1, 0)]) + early
    late = items([(1, 16), (5, 4), (2, 17), (6, 5), (0, 16), (4, 4), (1, 17), (5, 5)])
    last = items([(2, 18), (6, 6)])

    def pass_on(names, kept=None, notes=(), after=()):
        entries = [(at[name][0], at[name][1] + b) for name in names for b, _ in passed_on(name)]
        spec = [(entries, bool(notes))]
        if kept:
            spec.append(([(at[name][0], at[name][1] + b) for name in kept for b, _ in wanted(name)], False))
        array, *own_part = packed(spec, notes, after)
        received = from_other_core(array)
        end = len(entries) * BLK
        return received, own_part, (array[end:], received[end:])

    early_other, early_own, early_notes = pass_on(early, mine, middle, (sources[up7],))
    late_other, _, notes = pass_on(late, None, far)
    last_other, _, _ = pass_on(last)

    def part_of(names):
        by_source = {}
        for name in names:
            source, place = at[name]
            for b, panel in wanted(name):
                by_source.setdefault(source, []).append(((place + b) * BLK, 0, name[2], name[1], panel))
        return [(sources[source], rows) for source, rows in sorted(by_source.items())]

    def received_of(array, names):
        rows = []
        for name in names:
            for _, panel in passed_on(name):
                rows.append((len(rows) * BLK, 1, name[2], name[1], panel))
        return [(array, rows)]

    right_codes = right[:, STEPS * BLK, :6].astype(jnp.int32)
    right_codes = right_codes[:, :3] * 16 + right_codes[:, 3:] - 1
    c_code = c_code.reshape(KEPT)

    def table_of(parts, notes):
        order = [row for part in parts for _, rows in part for row in rows]
        return tables(order, notes, right_codes, c_code, start, core)

    def product_of(table, part, base, before=None, last=False):
        lefts, counts = [array for array, _ in part], tuple(len(rows) for _, rows in part)
        return product(table, right, lefts, counts, base, before, last), base + sum(counts)

    rows = []
    for name in mine:
        rows += [(len(rows) * BLK + n * BLK, 0, name[2], name[1], w) for n, (_, w) in enumerate(wanted(name))]
    part = [(early_own[0], rows)] + received_of(early_other, early)
    sums, _ = product_of(table_of((part,), early_notes), part, 0)
    part = part_of(late + last) + received_of(late_other, late) + received_of(last_other, last)
    out, _ = product_of(table_of((part,), notes), part, 0, sums, last=True)
    return out[None, None]


def solution(mesh):
    fine = Mesh(mesh.devices.reshape(SIZES), AXES)
    return jax.shard_map(
        local,
        mesh=fine,
        in_specs=(
            P(ROW, COL, None, None, None, None),
            P(ROW, COL, None, None),
            P(ROW, COL, None, None, None, None),
            P(ROW, COL, None, None),
            P(ROW, COL, None),
        ),
        out_specs=P(ROW, COL, None, None, None),
        check_vma=False,
    )
```

```python
import functools

import jax
import jax.numpy as jnp
import numpy as np
from jax import lax
from jax.experimental import pallas as pl
from jax.experimental.pallas import tpu as pltpu
from jax.sharding import Mesh
from jax.sharding import PartitionSpec as P

AXES = ("xl", "y", "xh", "z", "core")
ROW = ("xl", "y")
COL = ("xh", "z", "core")
SIZES = (2, 8, 2, 12, 2)
NQ = 24
NOTE = 2 * NQ
BC = 16
PANEL = 48
STEPS = 3
KEPT = 12
SPAN = 8 + STEPS - 1
HALF = STEPS * 128 + 16
BLK = 128


def items(pairs):
    return [(a, d, k) for a, d in pairs for k in range(2)]


def wanted(name):
    a, d, _ = name
    return [(0, 0), (1, 1)] if (d - a) % 8 == 0 else [(0, 2)]


def passed_on(name):
    a, d, _ = name
    return [(1, 2)] if (d - a) % 8 == 0 else [(0, 1), (1, 0)]


VMEM = pltpu.VMEM
SMEM_SPEC = pl.BlockSpec(memory_space=pltpu.SMEM)
VMEM_SPEC = pl.BlockSpec(memory_space=pltpu.VMEM)
ANY_SPEC = pl.BlockSpec(memory_space=pl.ANY)
LIMIT = pltpu.CompilerParams(vmem_limit_bytes=16 << 20)


def moves(blocks):
    return pl.CostEstimate(flops=0, bytes_accessed=2 * blocks * BLK * BLK * 2, transcendentals=0)


def rows_shape(rows):
    return jax.ShapeDtypeStruct((rows, BLK), jnp.bfloat16)


def blk(n):
    return pl.ds(n * BLK, BLK)


def first_kernel(orders, index_ref, own_ref, other_ref, note_ref, *outs):
    for out, order in zip(outs, orders, strict=True):
        for n, (other, place) in enumerate(order):
            out[blk(n), :] = (other_ref if other else own_ref)[index_ref[place]]
        out[pl.ds(len(order) * BLK, 16), :] = note_ref[...]


def first_packed(index, own, other, note, orders):
    return pl.pallas_call(
        functools.partial(first_kernel, orders),
        out_shape=[rows_shape(len(order) * BLK + 16) for order in orders],
        in_specs=[SMEM_SPEC] + [VMEM_SPEC] * 3,
        out_specs=[VMEM_SPEC for _ in orders],
        compiler_params=LIMIT,
        cost_estimate=moves(sum(len(order) for order in orders)),
    )(index, own, other, note)


def split_kernel(index_ref, src_ref, note_ref, *outs):
    for half, out in enumerate(outs):
        for n in range(SPAN):
            out[blk(n), :] = src_ref[index_ref[SPAN * half + n]]
        out[pl.ds(SPAN * BLK, 16), :] = note_ref[...]


def split(index, src, note):
    return pl.pallas_call(
        split_kernel,
        out_shape=[rows_shape(SPAN * BLK + 16)] * 2,
        in_specs=[SMEM_SPEC, VMEM_SPEC, VMEM_SPEC],
        out_specs=[VMEM_SPEC] * 2,
        compiler_params=LIMIT,
        cost_estimate=moves(2 * SPAN),
    )(index, src, note)


def right_kernel(*refs):
    sources, out = refs[:2], refs[-1]
    for n in range(8):
        for half, source in enumerate(sources):
            out[n, pl.ds(half * HALF, STEPS * BLK), :] = source[pl.ds(n * BLK, STEPS * BLK), :]
            note = source[pl.ds(SPAN * BLK, 16), :]
            out[n, pl.ds(half * HALF + STEPS * BLK, 16), :] = note


def right_packed(kept, other, after):
    return pl.pallas_call(
        right_kernel,
        out_shape=jax.ShapeDtypeStruct((8, 2 * HALF, BLK), jnp.bfloat16),
        in_specs=[VMEM_SPEC, VMEM_SPEC, ANY_SPEC],
        out_specs=VMEM_SPEC,
        compiler_params=LIMIT,
        cost_estimate=moves(48),
    )(kept, other, after)


def turned(note, distance):
    if distance == 0:
        return note
    return jnp.concatenate([pltpu.roll(note[n : n + NQ], distance, 0) for n in (0, NQ)])


def pack_kernel(spec, notes, count, *refs):
    sources, outs = refs[:count], refs[-len(spec) :]
    if notes:
        merged = None
        rows = lax.broadcasted_iota(jnp.int32, (NOTE, BLK), 0)
        for source, row, distance, small in notes:
            if small:
                note = sources[source][pl.ds(row, 16), :].astype(jnp.float32)
                other = jnp.where(rows == NQ + distance, note[1:2], 0.0)
                note = jnp.where(rows == distance, note[0:1], other)
            else:
                note = turned(sources[source][pl.ds(row, NOTE), :].astype(jnp.float32), distance)
            merged = note if merged is None else jnp.maximum(merged, note)
        merged = merged.astype(jnp.bfloat16)
    for out, (entries, noted) in zip(outs, spec, strict=True):
        for n, (source, place) in enumerate(entries):
            out[blk(n), :] = sources[source][blk(place), :]
        if noted:
            out[pl.ds(len(entries) * BLK, NOTE), :] = merged


def pack(sources, spec, notes, after):
    used = sorted({e[0] for entries, _ in spec for e in entries} | {n[0] for n in notes})
    where = {source: n for n, source in enumerate(used)}
    spec = tuple((tuple((where[s], n) for s, n in entries), noted) for entries, noted in spec)
    notes = tuple((where[n[0]],) + tuple(n[1:]) for n in notes)
    return pl.pallas_call(
        functools.partial(pack_kernel, spec, notes, len(used)),
        out_shape=[rows_shape(len(entries) * BLK + NOTE * noted) for entries, noted in spec],
        in_specs=[VMEM_SPEC] * len(used) + [ANY_SPEC] * len(after),
        out_specs=[VMEM_SPEC for _ in spec],
        compiler_params=LIMIT,
        cost_estimate=moves(sum(len(entries) for entries, _ in spec)),
    )(*[sources[source] for source in used], *after)


def product_kernel(counts, base, first, last, table_ref, right_ref, *rest):
    lefts, rest = rest[: len(counts)], rest[len(counts) :]
    if last:
        before, out_ref, acc = rest
        acc[...] = before[...]
    elif first:
        (acc,) = rest
        acc[...] = jnp.zeros_like(acc)
    else:
        before, acc = rest
        acc[...] = before[...]
    for left, count in zip(lefts, counts, strict=True):

        def body(n, carry, left=left, base=base):
            block = left[pl.ds(pl.multiple_of(table_ref[4, base + n], BLK), BLK), :]
            pair = []
            for rank in range(2):
                row = pl.multiple_of(table_ref[2 * rank, base + n], 16)
                pair.append(right_ref[pl.ds(row, BLK), :])
            both = jnp.dot(block, jnp.concatenate(pair, axis=1), preferred_element_type=jnp.float32)
            acc[table_ref[1, base + n]] += both[:, :BLK]
            acc[table_ref[3, base + n]] += both[:, BLK:]
            return carry

        unroll = max(n for n in (7, 6, 5, 4, 3, 2, 1) if count % n == 0)
        lax.fori_loop(0, count, body, 0, unroll=unroll)
        base += count
    if last:
        out_ref[...] = acc[:KEPT].astype(out_ref.dtype)


def product(table, right, lefts, counts, base, before=None, last=False):
    total = sum(counts)
    sums = jax.ShapeDtypeStruct((KEPT + 1, BLK, BLK), jnp.float32)
    return pl.pallas_call(
        functools.partial(product_kernel, counts, base, before is None, last),
        out_shape=jax.ShapeDtypeStruct((KEPT, BLK, BLK), jnp.bfloat16) if last else sums,
        in_specs=[SMEM_SPEC] + [VMEM_SPEC] * (1 + len(lefts) + (before is not None)),
        out_specs=VMEM_SPEC,
        scratch_shapes=[VMEM(sums.shape, jnp.float32)] if last else [],
        compiler_params=LIMIT,
        cost_estimate=pl.CostEstimate(
            flops=total * 16 * BLK**3, bytes_accessed=total * BLK * BLK * 2, transcendentals=0
        ),
    )(table, right, *lefts, *(() if before is None else (before,)))


def tables(order, notes, right_codes, c_code, start, core):
    order = np.array(order, np.int32)
    count = order.shape[0]
    row, other, k, distance, panel = (order[:, n] for n in range(5))
    notes = jnp.stack(notes)[:, :, :32].astype(jnp.int32)
    flat = (notes[:, :, :16] * 64 + notes[:, :, 16:] - 1).reshape(1, 2 * NOTE * 16)
    of = (start + panel + core * (3 - 2 * panel)) % 16
    place = (other * NOTE + k * NQ + distance) * 16 + of
    codes = jnp.sum(jnp.where(place[:, None] == jnp.arange(2 * NOTE * 16)[None, :], flat, 0), axis=1)
    step = panel + core * (2 - 2 * panel)
    right_live = right_codes >= 0
    right_inner = jnp.where(right_live, right_codes // BC, -1)
    owners = jnp.arange(16, dtype=jnp.int32)
    earlier = owners[None, :] < owners[:, None]
    rank = jnp.sum(
        ((right_inner[:, None, :] == right_inner[None, :, :]) & earlier[:, :, None]).astype(jnp.int32),
        axis=1,
    )
    packed = jnp.where(right_live, right_inner * 1024 + rank * 32 + right_codes % BC, -1)
    right_n = jnp.where(
        (step == 0)[:, None],
        packed[None, :, 0],
        jnp.where((step == 1)[:, None], packed[None, :, 1], packed[None, :, 2]),
    )
    match = (right_n >= 0) & (codes >= 0)[:, None] & ((right_n // 1024) == (codes % PANEL)[:, None])
    rows = []
    for rank_number in range(2):
        hit = match & ((right_n // 32) % 32 == rank_number)
        found = jnp.sum(jnp.where(hit, owners[None, :] * 32 + right_n % 32 + 1, 0), axis=1)
        partner = jnp.maximum(found - 1, 0)
        target = (codes // PANEL) * BC + partner % 32
        there = (target[:, None] == c_code[None, :]) & (found > 0)[:, None]
        slot = jnp.sum(jnp.where(there, jnp.arange(KEPT)[None, :] - KEPT, 0), axis=1) + KEPT
        rows += [partner // 32 * HALF + step * BLK, slot]
    return jnp.stack(rows + [jnp.array(row)]).astype(jnp.int32).reshape(5, count)


def moved(array, distance):
    route = []
    for i in range(NQ):
        route.append((2 * i, 2 * ((i + distance) % NQ)))
        route.append((2 * i + 1, 2 * ((i - distance) % NQ) + 1))
    return lax.ppermute(array, COL, route)


def from_other_core(array):
    return lax.ppermute(array, "core", [(0, 1), (1, 0)])


def local(a_own_values, a_own_code, b_own_values, b_own_code, c_code):
    r = lax.axis_index(ROW)
    q = lax.axis_index(("xh", "z"))
    core = lax.axis_index("core")
    start = (r + 2 * q) % 16
    a_own = a_own_values.reshape(16, BLK, BLK)
    b_own = b_own_values.reshape(16, BLK, BLK)

    def note_of(code):
        code = code.reshape(16) + 1
        digits = jnp.concatenate([code // 64, code % 64]).astype(jnp.bfloat16).reshape(1, 32)
        return jnp.pad(digits, ((0, 15), (0, BLK - 32)))

    spans = 2 * q + core + 8 * lax.axis_index("xl") + jnp.arange(SPAN, dtype=jnp.int32)
    b_kept, b_sent = split(jnp.concatenate([spans, spans + 8]) % 16, b_own, note_of(b_own_code))
    b_other = lax.ppermute(b_sent, "xl", [(0, 1), (1, 0)])

    sources, at = [], {}

    def keep(array, names):
        for n, name in enumerate(names):
            at[name] = (len(sources), 2 * n)
        sources.append(array)
        return len(sources) - 1

    def send(array, names, distance):
        return keep(moved(array, distance), [(a, (d + distance) % NQ, k) for a, d, k in names])

    def blocks(names):
        return [(at[name][0], at[name][1] + b) for name in names for b in range(2)]

    def packed(spec, notes=(), after=()):
        return pack(sources, spec, notes, after)

    note = note_of(a_own_code)
    a_other, note_other = from_other_core(a_own), from_other_core(note)
    note = jnp.concatenate([note[:1], note_other[:1], note[2:]])
    a_index = jnp.arange(16, dtype=jnp.int32)
    a_index = (start + jnp.where(core == 0, a_index, 3 - a_index)) % 16

    starts = [
        (items([(3, 0), (4, 0)]), 2),
        (items([(7, 0), (0, 0)]), 14),
        (items([(1, 0), (2, 0)]), 1),
        (items([(5, 0), (6, 0)]), 13),
        ([(4, 0, 0), (5, 0, 0)], 12),
    ]
    orders = tuple(
        tuple((k, 2 * a + b) for a, _, k in names for b in range(2)) for names, _ in starts
    )
    arrays = first_packed(a_index, a_own, a_other, note, orders)
    near = []
    for array, (names, _) in zip(arrays[:4], starts[:4], strict=True):
        own = keep(array, names)
    near.append((own, 8 * BLK, 0, True))
    for array, (names, distance) in zip(arrays[:4], starts[:4], strict=True):
        near.append((send(array, names, distance), 2 * len(names) * BLK, distance, True))

    names = items([(2, 1), (6, 13), (3, 2), (7, 14), (0, 14), (4, 2)])
    (up_in,) = packed([(blocks(names), True)], near, (b_other,))
    sources.append(up_in)
    up3 = send(up_in, names, 1)
    right = lax.all_to_all(right_packed(b_kept, b_other, up_in), "y", 0, 0, tiled=True)
    right = right.reshape(16 * HALF, BLK)
    middle = [(up3 - 1, 24 * BLK, 0, False), (up3, 24 * BLK, 1, False)]

    names = items([(1, 1), (5, 13), (2, 2), (6, 14)])
    (up_in,) = packed([(blocks(names), True)], middle)
    up6 = send(up_in, names, 15)
    across, _ = lax.optimization_barrier((arrays[4], up_in))
    middle.append((send(across, *starts[4]), 4 * BLK, starts[4][1], True))
    far = middle + [(up6, 16 * BLK, 15, False)]

    early = items([(1, 1), (5, 13), (2, 2), (6, 14), (3, 3), (7, 15)]) + [(4, 12, 0)]
    early += items([(2, 1), (6, 13), (3, 2), (7, 14), (0, 15), (4, 3)]) + [(5, 12, 0)]

    def pass_on(names, kept=None, notes=(), after=()):
        entries = [(at[name][0], at[name][1] + b) for name in names for b, _ in passed_on(name)]
        spec = [(entries, bool(notes))]
        if kept:
            spec.append(([(at[name][0], at[name][1] + b) for name in kept for b, _ in wanted(name)], False))
        array, *own_part = packed(spec, notes, after)
        received = from_other_core(array)
        end = len(entries) * BLK
        return received, own_part, (array[end:], received[end:])

    mine = items([(0, 0), (1, 0)]) + early
    early_other, early_own, early_notes = pass_on(early, mine, middle, (up_in,))

    names = items([(1, 16), (5, 4), (2, 17), (6, 5), (0, 15), (4, 3)])
    up_in, notes = packed([(blocks(names), False), ((), True)], far)
    send(up_in, names, 1)
    notes = (notes, from_other_core(notes))

    late = items([(1, 16), (5, 4), (2, 17), (6, 5)])
    late += items([(1, 17), (5, 5), (2, 18), (6, 6), (0, 16), (4, 4)])

    def part_of(names):
        by_source = {}
        for name in names:
            source, place = at[name]
            for b, panel in wanted(name):
                by_source.setdefault(source, []).append(((place + b) * BLK, 0, name[2], name[1], panel))
        return [(sources[source], rows) for source, rows in sorted(by_source.items())]

    def received_of(array, names):
        rows = []
        for name in names:
            for _, panel in passed_on(name):
                rows.append((len(rows) * BLK, 1, name[2], name[1], panel))
        return [(array, rows)]

    panels = (start + core + jnp.arange(STEPS, dtype=jnp.int32)) % 16
    digits = right.reshape(16, HALF, BLK)[:, STEPS * BLK, :32].astype(jnp.int32)
    right_codes = (digits[:, :16] * 64 + digits[:, 16:] - 1)[:, None, :]
    right_codes = jnp.sum(
        jnp.where(panels[:, None] == jnp.arange(16)[None, :], right_codes, 0), axis=2
    )
    c_code = c_code.reshape(KEPT)

    def table_of(parts, notes):
        order = [row for part in parts for _, rows in part for row in rows]
        return tables(order, notes, right_codes, c_code, start, core)

    def product_of(table, part, base, before=None, last=False):
        lefts, counts = [array for array, _ in part], tuple(len(rows) for _, rows in part)
        return product(table, right, lefts, counts, base, before, last), base + sum(counts)

    rows = []
    for name in mine:
        rows += [(len(rows) * BLK + n * BLK, 0, name[2], name[1], w) for n, (_, w) in enumerate(wanted(name))]
    part = [(early_own[0], rows)] + received_of(early_other, early)
    sums, _ = product_of(table_of((part,), early_notes), part, 0)
    parts = [part_of(late), received_of(None, late)]
    table = table_of(parts, notes)
    late_other, _, _ = pass_on(late, None, (), (sums,))
    sums, base = product_of(table, parts[0], 0, sums)
    out, _ = product_of(table, received_of(late_other, late), base, sums, last=True)
    return out[None, None]


def solution(mesh):
    fine = Mesh(mesh.devices.reshape(SIZES), AXES)
    return jax.shard_map(
        local,
        mesh=fine,
        in_specs=(
            P(ROW, COL, None, None, None, None),
            P(ROW, COL, None, None),
            P(ROW, COL, None, None, None, None),
            P(ROW, COL, None, None),
            P(ROW, COL, None),
        ),
        out_specs=P(ROW, COL, None, None, None),
        check_vma=False,
    )
```

```python
import functools

import jax
import jax.numpy as jnp
import numpy as np
from jax import lax
from jax.experimental import pallas as pl
from jax.experimental.pallas import tpu as pltpu
from jax.sharding import Mesh
from jax.sharding import PartitionSpec as P

AXES = ("xl", "y", "xh", "z", "core")
ROW = ("xl", "y")
COL = ("xh", "z", "core")
SIZES = (2, 8, 2, 12, 2)
NQ = 24
NOTE = 2 * NQ
BC = 16
PANEL = 48
STEPS = 3
KEPT = 12
SPAN = 8 + STEPS - 1
HALF = STEPS * 128 + 16
BLK = 128


def items(pairs):
    return [(a, d, k) for a, d in pairs for k in range(2)]


def wanted(name):
    a, d, _ = name
    return [(0, 0), (1, 1)] if (d - a) % 8 == 0 else [(0, 2)]


def passed_on(name):
    a, d, _ = name
    return [(1, 2)] if (d - a) % 8 == 0 else [(0, 1), (1, 0)]


VMEM = pltpu.VMEM
SMEM_SPEC = pl.BlockSpec(memory_space=pltpu.SMEM)
VMEM_SPEC = pl.BlockSpec(memory_space=pltpu.VMEM)
ANY_SPEC = pl.BlockSpec(memory_space=pl.ANY)
LIMIT = pltpu.CompilerParams(vmem_limit_bytes=16 << 20)


def moves(blocks):
    return pl.CostEstimate(flops=0, bytes_accessed=2 * blocks * BLK * BLK * 2, transcendentals=0)


def rows_shape(rows):
    return jax.ShapeDtypeStruct((rows, BLK), jnp.bfloat16)


def blk(n):
    return pl.ds(n * BLK, BLK)


def first_kernel(orders, index_ref, own_ref, other_ref, note_ref, *outs):
    for out, order in zip(outs, orders, strict=True):
        for n, (other, place) in enumerate(order):
            out[blk(n), :] = (other_ref if other else own_ref)[index_ref[place]]
        out[pl.ds(len(order) * BLK, 16), :] = note_ref[...]


def first_packed(index, own, other, note, orders):
    return pl.pallas_call(
        functools.partial(first_kernel, orders),
        out_shape=[rows_shape(len(order) * BLK + 16) for order in orders],
        in_specs=[SMEM_SPEC] + [VMEM_SPEC] * 3,
        out_specs=[VMEM_SPEC for _ in orders],
        compiler_params=LIMIT,
        cost_estimate=moves(sum(len(order) for order in orders)),
    )(index, own, other, note)


def split_kernel(index_ref, src_ref, note_ref, *outs):
    for half, out in enumerate(outs):
        for n in range(SPAN):
            out[blk(n), :] = src_ref[index_ref[SPAN * half + n]]
        out[pl.ds(SPAN * BLK, 16), :] = note_ref[...]


def split(index, src, note):
    return pl.pallas_call(
        split_kernel,
        out_shape=[rows_shape(SPAN * BLK + 16)] * 2,
        in_specs=[SMEM_SPEC, VMEM_SPEC, VMEM_SPEC],
        out_specs=[VMEM_SPEC] * 2,
        compiler_params=LIMIT,
        cost_estimate=moves(2 * SPAN),
    )(index, src, note)


def right_kernel(*refs):
    sources, out = refs[:2], refs[-1]
    for n in range(8):
        for half, source in enumerate(sources):
            out[n, pl.ds(half * HALF, STEPS * BLK), :] = source[pl.ds(n * BLK, STEPS * BLK), :]
            note = source[pl.ds(SPAN * BLK, 16), :]
            out[n, pl.ds(half * HALF + STEPS * BLK, 16), :] = note


def right_packed(kept, other, after):
    return pl.pallas_call(
        right_kernel,
        out_shape=jax.ShapeDtypeStruct((8, 2 * HALF, BLK), jnp.bfloat16),
        in_specs=[VMEM_SPEC, VMEM_SPEC, ANY_SPEC],
        out_specs=VMEM_SPEC,
        compiler_params=LIMIT,
        cost_estimate=moves(48),
    )(kept, other, after)


def turned(note, distance):
    if distance == 0:
        return note
    return jnp.concatenate([pltpu.roll(note[n : n + NQ], distance, 0) for n in (0, NQ)])


def pack_kernel(spec, notes, count, *refs):
    sources, outs = refs[:count], refs[-len(spec) :]
    if notes:
        merged = None
        rows = lax.broadcasted_iota(jnp.int32, (NOTE, BLK), 0)
        for source, row, distance, small in notes:
            if small:
                note = sources[source][pl.ds(row, 16), :].astype(jnp.float32)
                other = jnp.where(rows == NQ + distance, note[1:2], 0.0)
                note = jnp.where(rows == distance, note[0:1], other)
            else:
                note = turned(sources[source][pl.ds(row, NOTE), :].astype(jnp.float32), distance)
            merged = note if merged is None else jnp.maximum(merged, note)
        merged = merged.astype(jnp.bfloat16)
    for out, (entries, noted) in zip(outs, spec, strict=True):
        for n, (source, place) in enumerate(entries):
            out[blk(n), :] = sources[source][blk(place), :]
        if noted:
            out[pl.ds(len(entries) * BLK, NOTE), :] = merged


def pack(sources, spec, notes, after):
    used = sorted({e[0] for entries, _ in spec for e in entries} | {n[0] for n in notes})
    where = {source: n for n, source in enumerate(used)}
    spec = tuple((tuple((where[s], n) for s, n in entries), noted) for entries, noted in spec)
    notes = tuple((where[n[0]],) + tuple(n[1:]) for n in notes)
    return pl.pallas_call(
        functools.partial(pack_kernel, spec, notes, len(used)),
        out_shape=[rows_shape(len(entries) * BLK + NOTE * noted) for entries, noted in spec],
        in_specs=[VMEM_SPEC] * len(used) + [ANY_SPEC] * len(after),
        out_specs=[VMEM_SPEC for _ in spec],
        compiler_params=LIMIT,
        cost_estimate=moves(sum(len(entries) for entries, _ in spec)),
    )(*[sources[source] for source in used], *after)


def product_kernel(counts, base, first, last, table_ref, right_ref, *rest):
    lefts, rest = rest[: len(counts)], rest[len(counts) :]
    if last:
        before, out_ref, acc = rest
        acc[...] = before[...]
    elif first:
        (acc,) = rest
        acc[...] = jnp.zeros_like(acc)
    else:
        before, acc = rest
        acc[...] = before[...]
    for left, count in zip(lefts, counts, strict=True):

        def body(n, carry, left=left, base=base):
            block = left[pl.ds(pl.multiple_of(table_ref[4, base + n], BLK), BLK), :]
            pair = []
            for rank in range(2):
                row = pl.multiple_of(table_ref[2 * rank, base + n], 16)
                pair.append(right_ref[pl.ds(row, BLK), :])
            both = jnp.dot(block, jnp.concatenate(pair, axis=1), preferred_element_type=jnp.float32)
            acc[table_ref[1, base + n]] += both[:, :BLK]
            acc[table_ref[3, base + n]] += both[:, BLK:]
            return carry

        unroll = max(n for n in range(1, 17) if count % n == 0)
        lax.fori_loop(0, count, body, 0, unroll=unroll)
        base += count
    if last:
        out_ref[...] = acc[:KEPT].astype(out_ref.dtype)


def product(table, right, lefts, counts, base, before=None, last=False):
    total = sum(counts)
    sums = jax.ShapeDtypeStruct((KEPT + 1, BLK, BLK), jnp.float32)
    return pl.pallas_call(
        functools.partial(product_kernel, counts, base, before is None, last),
        out_shape=jax.ShapeDtypeStruct((KEPT, BLK, BLK), jnp.bfloat16) if last else sums,
        in_specs=[SMEM_SPEC] + [VMEM_SPEC] * (1 + len(lefts) + (before is not None)),
        out_specs=VMEM_SPEC,
        scratch_shapes=[VMEM(sums.shape, jnp.float32)] if last else [],
        compiler_params=LIMIT,
        cost_estimate=pl.CostEstimate(
            flops=total * 16 * BLK**3, bytes_accessed=total * BLK * BLK * 2, transcendentals=0
        ),
    )(table, right, *lefts, *(() if before is None else (before,)))


def tables(order, notes, right_codes, c_code, start, core):
    order = np.array(order, np.int32)
    count = order.shape[0]
    row, other, k, distance, panel = (order[:, n] for n in range(5))
    notes = jnp.stack(notes)[:, :, :32].astype(jnp.int32)
    flat = (notes[:, :, :16] * 64 + notes[:, :, 16:] - 1).reshape(1, 2 * NOTE * 16)
    of = (start + panel + core * (3 - 2 * panel)) % 16
    place = (other * NOTE + k * NQ + distance) * 16 + of
    codes = jnp.sum(jnp.where(place[:, None] == jnp.arange(2 * NOTE * 16)[None, :], flat, 0), axis=1)
    step = panel + core * (2 - 2 * panel)
    right_live = right_codes >= 0
    right_inner = jnp.where(right_live, right_codes // BC, -1)
    owners = jnp.arange(16, dtype=jnp.int32)
    earlier = owners[None, :] < owners[:, None]
    rank = jnp.sum(
        ((right_inner[:, None, :] == right_inner[None, :, :]) & earlier[:, :, None]).astype(jnp.int32),
        axis=1,
    )
    packed = jnp.where(right_live, right_inner * 1024 + rank * 32 + right_codes % BC, -1)
    right_n = jnp.where(
        (step == 0)[:, None],
        packed[None, :, 0],
        jnp.where((step == 1)[:, None], packed[None, :, 1], packed[None, :, 2]),
    )
    match = (right_n >= 0) & (codes >= 0)[:, None] & ((right_n // 1024) == (codes % PANEL)[:, None])
    rows = []
    for rank_number in range(2):
        hit = match & ((right_n // 32) % 32 == rank_number)
        found = jnp.sum(jnp.where(hit, owners[None, :] * 32 + right_n % 32 + 1, 0), axis=1)
        partner = jnp.maximum(found - 1, 0)
        target = (codes // PANEL) * BC + partner % 32
        there = (target[:, None] == c_code[None, :]) & (found > 0)[:, None]
        slot = jnp.sum(jnp.where(there, jnp.arange(KEPT)[None, :] - KEPT, 0), axis=1) + KEPT
        rows += [partner // 32 * HALF + step * BLK, slot]
    return jnp.stack(rows + [jnp.array(row)]).astype(jnp.int32).reshape(5, count)


def moved(array, distance):
    route = []
    for i in range(NQ):
        route.append((2 * i, 2 * ((i + distance) % NQ)))
        route.append((2 * i + 1, 2 * ((i - distance) % NQ) + 1))
    return lax.ppermute(array, COL, route)


def from_other_core(array):
    return lax.ppermute(array, "core", [(0, 1), (1, 0)])


def local(a_own_values, a_own_code, b_own_values, b_own_code, c_code):
    r = lax.axis_index(ROW)
    q = lax.axis_index(("xh", "z"))
    core = lax.axis_index("core")
    start = (r + 2 * q) % 16
    a_own = a_own_values.reshape(16, BLK, BLK)
    b_own = b_own_values.reshape(16, BLK, BLK)

    def note_of(code):
        code = code.reshape(16) + 1
        digits = jnp.concatenate([code // 64, code % 64]).astype(jnp.bfloat16).reshape(1, 32)
        return jnp.pad(digits, ((0, 15), (0, BLK - 32)))

    spans = 2 * q + core + 8 * lax.axis_index("xl") + jnp.arange(SPAN, dtype=jnp.int32)
    b_kept, b_sent = split(jnp.concatenate([spans, spans + 8]) % 16, b_own, note_of(b_own_code))
    b_other = lax.ppermute(b_sent, "xl", [(0, 1), (1, 0)])

    sources, at = [], {}

    def keep(array, names):
        for n, name in enumerate(names):
            at[name] = (len(sources), 2 * n)
        sources.append(array)
        return len(sources) - 1

    def send(array, names, distance):
        return keep(moved(array, distance), [(a, (d + distance) % NQ, k) for a, d, k in names])

    def blocks(names):
        return [(at[name][0], at[name][1] + b) for name in names for b in range(2)]

    def packed(spec, notes=(), after=()):
        return pack(sources, spec, notes, after)

    note = note_of(a_own_code)
    a_other, note_other = from_other_core(a_own), from_other_core(note)
    note = jnp.concatenate([note[:1], note_other[:1], note[2:]])
    a_index = jnp.arange(16, dtype=jnp.int32)
    a_index = (start + jnp.where(core == 0, a_index, 3 - a_index)) % 16

    starts = [
        (items([(3, 0), (4, 0)]), 2),
        (items([(7, 0), (0, 0)]), 14),
        (items([(1, 0), (2, 0)]), 1),
        (items([(5, 0), (6, 0)]), 13),
        ([(4, 0, 0), (5, 0, 0)], 12),
    ]
    orders = tuple(
        tuple((k, 2 * a + b) for a, _, k in names for b in range(2)) for names, _ in starts
    )
    arrays = first_packed(a_index, a_own, a_other, note, orders)
    near = []
    for array, (names, _) in zip(arrays[:4], starts[:4], strict=True):
        own = keep(array, names)
    near.append((own, 8 * BLK, 0, True))
    for array, (names, distance) in zip(arrays[:4], starts[:4], strict=True):
        near.append((send(array, names, distance), 2 * len(names) * BLK, distance, True))

    names = items([(2, 1), (6, 13), (3, 2), (7, 14), (0, 14), (4, 2)])
    (up_in,) = packed([(blocks(names), True)], near, (b_other,))
    sources.append(up_in)
    up3 = send(up_in, names, 1)
    right = lax.all_to_all(right_packed(b_kept, b_other, up_in), "y", 0, 0, tiled=True)
    right = right.reshape(16 * HALF, BLK)
    middle = [(up3 - 1, 24 * BLK, 0, False), (up3, 24 * BLK, 1, False)]

    names = items([(1, 1), (5, 13), (2, 2), (6, 14)])
    (up_in,) = packed([(blocks(names), True)], middle)
    up6 = send(up_in, names, 15)
    across, _ = lax.optimization_barrier((arrays[4], up_in))
    middle.append((send(across, *starts[4]), 4 * BLK, starts[4][1], True))
    far = middle + [(up6, 16 * BLK, 15, False)]

    early = items([(1, 1), (5, 13), (2, 2), (6, 14), (3, 3), (7, 15)]) + [(4, 12, 0)]
    early += items([(2, 1), (6, 13), (3, 2), (7, 14), (0, 15), (4, 3)]) + [(5, 12, 0)]

    def pass_on(names, pieces, kept=None, notes=(), after=()):
        entries = [(at[name][0], at[name][1] + b) for name in names for b, _ in passed_on(name)]
        size = len(entries) // pieces
        assert size * pieces == len(entries)
        spec = [(entries[n * size : (n + 1) * size], bool(notes) and n == 0) for n in range(pieces)]
        if kept:
            spec.append(([(at[name][0], at[name][1] + b) for name in kept for b, _ in wanted(name)], False))
        arrays = packed(spec, notes, after)
        received = [from_other_core(array) for array in arrays[:pieces]]
        end = size * BLK
        return received, arrays[pieces:], (arrays[0][end:], received[0][end:])

    mine = items([(0, 0), (1, 0)]) + early
    early_other, early_own, early_notes = pass_on(early, 3, mine, middle, (up_in,))

    names = items([(1, 16), (5, 4), (2, 17), (6, 5), (0, 15), (4, 3)])
    up_in, notes = packed([(blocks(names), False), ((), True)], far)
    send(up_in, names, 1)
    notes, _ = lax.optimization_barrier((notes, early_other[2]))
    notes = (notes, from_other_core(notes))

    late = items([(1, 16), (5, 4), (2, 17), (6, 5)])
    late += items([(1, 17), (5, 5), (2, 18), (6, 6), (0, 16), (4, 4)])

    def part_of(names):
        by_source = {}
        for name in names:
            source, place = at[name]
            for b, panel in wanted(name):
                by_source.setdefault(source, []).append(((place + b) * BLK, 0, name[2], name[1], panel))
        return [(sources[source], rows) for source, rows in sorted(by_source.items())]

    def received_of(arrays, names):
        found = [(name, panel) for name in names for _, panel in passed_on(name)]
        size = len(found) // len(arrays)
        return [
            (array, [(m * BLK, 1, name[2], name[1], panel) for m, (name, panel) in enumerate(found[n * size : (n + 1) * size])])
            for n, array in enumerate(arrays)
        ]

    panels = (start + core + jnp.arange(STEPS, dtype=jnp.int32)) % 16
    digits = right.reshape(16, HALF, BLK)[:, STEPS * BLK, :32].astype(jnp.int32)
    right_codes = (digits[:, :16] * 64 + digits[:, 16:] - 1)[:, None, :]
    right_codes = jnp.sum(
        jnp.where(panels[:, None] == jnp.arange(16)[None, :], right_codes, 0), axis=2
    )
    c_code = c_code.reshape(KEPT)

    def table_of(parts, notes):
        order = [row for part in parts for _, rows in part for row in rows]
        return tables(order, notes, right_codes, c_code, start, core)

    def product_of(table, part, base, before=None, last=False):
        lefts, counts = [array for array, _ in part], tuple(len(rows) for _, rows in part)
        return product(table, right, lefts, counts, base, before, last), base + sum(counts)

    rows = []
    for name in mine:
        rows += [(len(rows) * BLK + n * BLK, 0, name[2], name[1], w) for n, (_, w) in enumerate(wanted(name))]
    part = [(early_own[0], rows)] + received_of(early_other, early)
    sums, _ = product_of(table_of((part,), early_notes), part, 0)
    parts = [part_of(late), received_of([None], late)]
    table = table_of(parts, notes)
    late_other, _, _ = pass_on(late, 1, None, (), (sums,))
    sums, base = product_of(table, parts[0], 0, sums)
    out, _ = product_of(table, received_of(late_other, late), base, sums, last=True)
    return out[None, None]


def solution(mesh):
    fine = Mesh(mesh.devices.reshape(SIZES), AXES)
    return jax.shard_map(
        local,
        mesh=fine,
        in_specs=(
            P(ROW, COL, None, None, None, None),
            P(ROW, COL, None, None),
            P(ROW, COL, None, None, None, None),
            P(ROW, COL, None, None),
            P(ROW, COL, None),
        ),
        out_specs=P(ROW, COL, None, None, None),
        check_vma=False,
    )
```

```python
import functools

import jax
import jax.numpy as jnp
import numpy as np
from jax import lax
from jax.experimental import pallas as pl
from jax.experimental.pallas import tpu as pltpu
from jax.sharding import Mesh
from jax.sharding import PartitionSpec as P

AXES = ("xl", "y", "xh", "z", "core")
ROW = ("xl", "y")
COL = ("xh", "z", "core")
SIZES = (2, 8, 2, 12, 2)
NQ = 24
NOTE = 2 * NQ
BC = 16
PANEL = 48
STEPS = 3
KEPT = 12
PIECES = 1
HALF = STEPS * 128 + 16
BLK = 128


def items(pairs):
    return [(a, d, k) for a, d in pairs for k in range(2)]


def wanted(name):
    a, d, _ = name
    return [(0, 0), (1, 1)] if (d - a) % 8 == 0 else [(0, 2)]


def passed_on(name):
    a, d, _ = name
    return [(1, 2)] if (d - a) % 8 == 0 else [(0, 1), (1, 0)]


VMEM = pltpu.VMEM
SMEM_SPEC = pl.BlockSpec(memory_space=pltpu.SMEM)
VMEM_SPEC = pl.BlockSpec(memory_space=pltpu.VMEM)
ANY_SPEC = pl.BlockSpec(memory_space=pl.ANY)
LIMIT = pltpu.CompilerParams(vmem_limit_bytes=16 << 20)


def moves(blocks):
    return pl.CostEstimate(flops=0, bytes_accessed=2 * blocks * BLK * BLK * 2, transcendentals=0)


def rows_shape(rows):
    return jax.ShapeDtypeStruct((rows, BLK), jnp.bfloat16)


def blk(n):
    return pl.ds(n * BLK, BLK)


def first_kernel(orders, index_ref, own_ref, other_ref, note_ref, *outs):
    for out, order in zip(outs, orders, strict=True):
        for n, (other, place) in enumerate(order):
            out[blk(n), :] = (other_ref if other else own_ref)[index_ref[place]]
        out[pl.ds(len(order) * BLK, 16), :] = note_ref[...]


def first_packed(index, own, other, note, orders):
    return pl.pallas_call(
        functools.partial(first_kernel, orders),
        out_shape=[rows_shape(len(order) * BLK + 16) for order in orders],
        in_specs=[SMEM_SPEC] + [VMEM_SPEC] * 3,
        out_specs=[VMEM_SPEC for _ in orders],
        compiler_params=LIMIT,
        cost_estimate=moves(sum(len(order) for order in orders)),
    )(index, own, other, note)


def right_kernel(index_ref, src_ref, code_ref, after_ref, out):
    del after_ref
    for n in range(16):
        for t in range(STEPS):
            out[n, blk(t), :] = src_ref[index_ref[n + t]]
        out[n, pl.ds(STEPS * BLK, 16), :] = code_ref[n]


def right_packed(src, index, codes, after):
    return pl.pallas_call(
        right_kernel,
        out_shape=jax.ShapeDtypeStruct((16, HALF, BLK), jnp.bfloat16),
        in_specs=[SMEM_SPEC, VMEM_SPEC, VMEM_SPEC, ANY_SPEC],
        out_specs=VMEM_SPEC,
        compiler_params=LIMIT,
        cost_estimate=moves(48),
    )(index, src, codes, after)


def turned(note, distance):
    if distance == 0:
        return note
    return jnp.concatenate([pltpu.roll(note[n : n + NQ], distance, 0) for n in (0, NQ)])


def pack_kernel(spec, notes, count, *refs):
    sources, outs = refs[:count], refs[-len(spec) :]
    if notes:
        merged = None
        rows = lax.broadcasted_iota(jnp.int32, (NOTE, BLK), 0)
        for source, row, distance, small in notes:
            if small:
                note = sources[source][pl.ds(row, 16), :].astype(jnp.float32)
                other = jnp.where(rows == NQ + distance, note[1:2], 0.0)
                note = jnp.where(rows == distance, note[0:1], other)
            else:
                note = turned(sources[source][pl.ds(row, NOTE), :].astype(jnp.float32), distance)
            merged = note if merged is None else jnp.maximum(merged, note)
        merged = merged.astype(jnp.bfloat16)
    for out, (entries, noted) in zip(outs, spec, strict=True):
        for n, (source, place) in enumerate(entries):
            out[blk(n), :] = sources[source][blk(place), :]
        if noted:
            out[pl.ds(len(entries) * BLK, NOTE), :] = merged


def pack(sources, spec, notes, after):
    used = sorted({e[0] for entries, _ in spec for e in entries} | {n[0] for n in notes})
    where = {source: n for n, source in enumerate(used)}
    spec = tuple((tuple((where[s], n) for s, n in entries), noted) for entries, noted in spec)
    notes = tuple((where[n[0]],) + tuple(n[1:]) for n in notes)
    return pl.pallas_call(
        functools.partial(pack_kernel, spec, notes, len(used)),
        out_shape=[rows_shape(len(entries) * BLK + NOTE * noted) for entries, noted in spec],
        in_specs=[VMEM_SPEC] * len(used) + [ANY_SPEC] * len(after),
        out_specs=[VMEM_SPEC for _ in spec],
        compiler_params=LIMIT,
        cost_estimate=moves(sum(len(entries) for entries, _ in spec)),
    )(*[sources[source] for source in used], *after)


def product_kernel(counts, base, first, last, table_ref, right_ref, *rest):
    lefts, rest = rest[: len(counts)], rest[len(counts) :]
    if last:
        before, out_ref, acc = rest
        acc[...] = before[...]
    elif first:
        (acc,) = rest
        acc[...] = jnp.zeros_like(acc)
    else:
        before, acc = rest
        acc[...] = before[...]
    for left, count in zip(lefts, counts, strict=True):

        def body(n, carry, left=left, base=base):
            block = left[pl.ds(pl.multiple_of(table_ref[4, base + n], BLK), BLK), :]
            pair = []
            for rank in range(2):
                row = pl.multiple_of(table_ref[2 * rank, base + n], 16)
                pair.append(right_ref[pl.ds(row, BLK), :])
            both = jnp.dot(block, jnp.concatenate(pair, axis=1), preferred_element_type=jnp.float32)
            acc[table_ref[1, base + n]] += both[:, :BLK]
            acc[table_ref[3, base + n]] += both[:, BLK:]
            return carry

        unroll = max(n for n in range(1, 17) if count % n == 0)
        lax.fori_loop(0, count, body, 0, unroll=unroll)
        base += count
    if last:
        out_ref[...] = acc[:KEPT].astype(out_ref.dtype)


def product(table, right, lefts, counts, base, before=None, last=False):
    total = sum(counts)
    sums = jax.ShapeDtypeStruct((KEPT + 1, BLK, BLK), jnp.float32)
    return pl.pallas_call(
        functools.partial(product_kernel, counts, base, before is None, last),
        out_shape=jax.ShapeDtypeStruct((KEPT, BLK, BLK), jnp.bfloat16) if last else sums,
        in_specs=[SMEM_SPEC] + [VMEM_SPEC] * (1 + len(lefts) + (before is not None)),
        out_specs=VMEM_SPEC,
        scratch_shapes=[VMEM(sums.shape, jnp.float32)] if last else [],
        compiler_params=LIMIT,
        cost_estimate=pl.CostEstimate(
            flops=total * 16 * BLK**3, bytes_accessed=total * BLK * BLK * 2, transcendentals=0
        ),
    )(table, right, *lefts, *(() if before is None else (before,)))


def tables(order, notes, right_codes, c_code, start, core):
    half = NQ // 4
    order = [
        (row, 1 - other, 1 - k, half, panel) if d == 3 * half else (row, other, k, d, panel)
        for row, other, k, d, panel in order
    ]
    order = np.array(order, np.int32)
    count = order.shape[0]
    row, other, k, distance, panel = (order[:, n] for n in range(5))
    notes = jnp.stack(notes)[:, :, :32].astype(jnp.int32)
    flat = (notes[:, :, :16] * 64 + notes[:, :, 16:] - 1).reshape(1, 2 * NOTE * 16)
    of = (start + panel + core * (3 - 2 * panel)) % 16
    place = (other * NOTE + k * NQ + distance) * 16 + of
    codes = jnp.sum(jnp.where(place[:, None] == jnp.arange(2 * NOTE * 16)[None, :], flat, 0), axis=1)
    step = panel + core * (2 - 2 * panel)
    right_live = right_codes >= 0
    right_inner = jnp.where(right_live, right_codes // BC, -1)
    owners = jnp.arange(16, dtype=jnp.int32)
    earlier = owners[None, :] < owners[:, None]
    rank = jnp.sum(
        ((right_inner[:, None, :] == right_inner[None, :, :]) & earlier[:, :, None]).astype(jnp.int32),
        axis=1,
    )
    packed = jnp.where(right_live, right_inner * 1024 + rank * 32 + right_codes % BC, -1)
    right_n = jnp.where(
        (step == 0)[:, None],
        packed[None, :, 0],
        jnp.where((step == 1)[:, None], packed[None, :, 1], packed[None, :, 2]),
    )
    match = (right_n >= 0) & (codes >= 0)[:, None] & ((right_n // 1024) == (codes % PANEL)[:, None])
    rows = []
    for rank_number in range(2):
        hit = match & ((right_n // 32) % 32 == rank_number)
        found = jnp.sum(jnp.where(hit, owners[None, :] * 32 + right_n % 32 + 1, 0), axis=1)
        partner = jnp.maximum(found - 1, 0)
        target = (codes // PANEL) * BC + partner % 32
        there = (target[:, None] == c_code[None, :]) & (found > 0)[:, None]
        slot = jnp.sum(jnp.where(there, jnp.arange(KEPT)[None, :] - KEPT, 0), axis=1) + KEPT
        rows += [partner // 32 * HALF + step * BLK, slot]
    return jnp.stack(rows + [jnp.array(row)]).astype(jnp.int32).reshape(5, count)


def moved(array, distance):
    route = []
    for i in range(NQ):
        route.append((2 * i, 2 * ((i + distance) % NQ)))
        route.append((2 * i + 1, 2 * ((i - distance) % NQ) + 1))
    return lax.ppermute(array, COL, route)


def from_other_core(array):
    return lax.ppermute(array, "core", [(0, 1), (1, 0)])


def local(a_own_values, a_own_code, b_own_values, b_own_code, c_code):
    r = lax.axis_index(ROW)
    q = lax.axis_index(("xh", "z"))
    core = lax.axis_index("core")
    start = (r + 2 * q) % 16
    a_own = a_own_values.reshape(16, BLK, BLK)
    b_own = b_own_values.reshape(16, BLK, BLK)

    def note_of(code):
        code = code.reshape(16) + 1
        digits = jnp.concatenate([code // 64, code % 64]).astype(jnp.bfloat16).reshape(1, 32)
        return jnp.pad(digits, ((0, 15), (0, BLK - 32)))

    sources, at = [], {}

    def keep(array, names):
        for n, name in enumerate(names):
            at[name] = (len(sources), 2 * n)
        sources.append(array)
        return len(sources) - 1

    def send(array, names, distance):
        return keep(moved(array, distance), [(a, (d + distance) % NQ, k) for a, d, k in names])

    def blocks(names):
        return [(at[name][0], at[name][1] + b) for name in names for b in range(2)]

    def packed(spec, notes=(), after=()):
        return pack(sources, spec, notes, after)

    note = note_of(a_own_code)
    a_other, note_other = from_other_core(a_own), from_other_core(note)

    shift = (2 * q + core + jnp.arange(18, dtype=jnp.int32)) % 16
    b_code = b_own_code.reshape(16) + 1
    b_code = jnp.sum(jnp.where(shift[:, None] == jnp.arange(16)[None, :], b_code[None, :], 0), axis=1)
    b_code = jnp.stack([b_code[t : t + 16] for t in range(STEPS)], axis=1)
    b_code = jnp.concatenate([b_code // 16, b_code % 16], axis=1).astype(jnp.bfloat16)
    b_code = jnp.broadcast_to(jnp.pad(b_code, ((0, 0), (0, BLK - 6)))[:, None, :], (16, 16, BLK))
    right = right_packed(b_own, shift, b_code, note_other)
    right = lax.all_to_all(right, ROW, 0, 0, tiled=True).reshape(16 * HALF, BLK)
    note = jnp.concatenate([note[:1], note_other[:1], note[2:]])
    a_index = jnp.arange(16, dtype=jnp.int32)
    a_index = (start + jnp.where(core == 0, a_index, 3 - a_index)) % 16

    starts = [
        (items([(2, 0), (3, 0), (4, 0)]), 2),
        (items([(6, 0), (7, 0), (0, 0)]), 14),
        (items([(1, 0), (2, 0)]), 1),
        (items([(5, 0), (6, 0)]), 13),
        ([(4, 0, 0), (5, 0, 0)], 12),
    ]
    orders = tuple(
        tuple((k, 2 * a + b) for a, _, k in names for b in range(2)) for names, _ in starts
    )
    arrays = first_packed(a_index, a_own, a_other, note, orders)
    near = []
    for array, (names, _) in zip(arrays[:4], starts[:4], strict=True):
        own = keep(array, names)
    near.append((own, 8 * BLK, 0, True))
    for array, (names, distance) in zip(arrays[:4], starts[:4], strict=True):
        near.append((send(array, names, distance), 2 * len(names) * BLK, distance, True))

    sources.append(moved(note, NQ // 4))
    opposite = len(sources) - 1
    long_names = items([(1, 1), (5, 13), (2, 2), (6, 14)])
    names = items([(3, 2), (7, 14), (0, 14), (4, 2)])
    long_in, up_in = packed([(blocks(long_names), True), (blocks(names), True)], near, (sources[opposite],))
    far = [(len(sources), 16 * BLK, 0, False)]
    sources.append(long_in)
    far.append((send(long_in, long_names, 15), 16 * BLK, 15, False))
    far.append((send(up_in, names, 1), 16 * BLK, 1, False))
    across, _ = lax.optimization_barrier((arrays[4], long_in))
    far.append((send(across, *starts[4]), 4 * BLK, starts[4][1], True))
    far.append((opposite, 0, NQ // 4, True))

    early = items([(1, 1), (5, 13), (2, 2), (6, 14), (2, 1), (6, 13), (3, 2), (7, 14)])

    def pass_on(names, pieces, kept=None, notes=(), after=()):
        entries = [(at[name][0], at[name][1] + b) for name in names for b, _ in passed_on(name)]
        size = -(-len(entries) // pieces)
        spec = [(entries[n * size : (n + 1) * size], bool(notes) and n == pieces - 1) for n in range(pieces)]
        if kept:
            spec.append(([(at[name][0], at[name][1] + b) for name in kept for b, _ in wanted(name)], False))
        arrays = packed(spec, notes, after)
        received = [from_other_core(array) for array in arrays[:pieces]]
        end = (len(entries) - size * (pieces - 1)) * BLK
        return received, arrays[pieces:], (arrays[pieces - 1][end:], received[-1][end:])

    mine = items([(0, 0), (1, 0)]) + early
    early_other, early_own, early_notes = pass_on(early, PIECES, mine, near, (long_in,))

    names = items([(1, 16), (5, 4), (2, 17), (6, 5), (0, 15), (4, 3)])
    (up_in,) = packed([(blocks(names), False)])
    send(up_in, names, 1)

    late = [(4, 12, 0), (5, 12, 0)] + items([(3, 3), (7, 15)]) + names
    last = items([(1, 17), (5, 5), (2, 18), (6, 6), (0, 16), (4, 4)])
    late_other, late_own, late_notes = pass_on(late, 3, late, far, (up_in,))

    def kept_of(array, names):
        found = [(name, panel) for name in names for _, panel in wanted(name)]
        return [(array, [(m * BLK, 0, n[2], n[1], panel) for m, (n, panel) in enumerate(found)])]

    def part_of(names):
        by_source = {}
        for name in names:
            source, place = at[name]
            for b, panel in wanted(name):
                by_source.setdefault(source, []).append(((place + b) * BLK, 0, name[2], name[1], panel))
        return [(sources[source], rows) for source, rows in sorted(by_source.items())]

    def received_of(arrays, names):
        found = [(name, panel) for name in names for _, panel in passed_on(name)]
        size = -(-len(found) // len(arrays))
        return [
            (array, [(m * BLK, 1, name[2], name[1], panel) for m, (name, panel) in enumerate(found[n * size : (n + 1) * size])])
            for n, array in enumerate(arrays)
        ]

    right_codes = right.reshape(16, HALF, BLK)[:, STEPS * BLK, :6].astype(jnp.int32)
    right_codes = right_codes[:, :3] * 16 + right_codes[:, 3:] - 1
    c_code = c_code.reshape(KEPT)

    def table_of(parts, notes):
        order = [row for part in parts for _, rows in part for row in rows]
        return tables(order, notes, right_codes, c_code, start, core)

    def product_of(table, part, base, before=None, last=False):
        lefts, counts = [array for array, _ in part], tuple(len(rows) for _, rows in part)
        return product(table, right, lefts, counts, base, before, last), base + sum(counts)

    part = kept_of(early_own[0], mine) + received_of(early_other, early)
    sums, _ = product_of(table_of((part,), early_notes), part, 0)
    part = kept_of(late_own[0], late) + received_of(late_other, late)
    parts = [part, part_of(last), received_of([None], last)]
    table = table_of(parts, late_notes)
    sums, base = product_of(table, part, 0, sums)
    last_other, _, _ = pass_on(last, 1, None, (), (sums,))
    sums, base = product_of(table, parts[1], base, sums)
    out, _ = product_of(table, received_of(last_other, last), base, sums, last=True)
    return out[None, None]


def solution(mesh):
    fine = Mesh(mesh.devices.reshape(SIZES), AXES)
    return jax.shard_map(
        local,
        mesh=fine,
        in_specs=(
            P(ROW, COL, None, None, None, None),
            P(ROW, COL, None, None),
            P(ROW, COL, None, None, None, None),
            P(ROW, COL, None, None),
            P(ROW, COL, None),
        ),
        out_specs=P(ROW, COL, None, None, None),
        check_vma=False,
    )
```

```python
import functools

import jax
import jax.numpy as jnp
import numpy as np
from jax import lax
from jax.experimental import pallas as pl
from jax.experimental.pallas import tpu as pltpu
from jax.sharding import Mesh
from jax.sharding import PartitionSpec as P

AXES = ("xl", "y", "xh", "z", "core")
ROW = ("xl", "y")
COL = ("xh", "z", "core")
SIZES = (2, 8, 2, 12, 2)
NQ = 24
NOTE = 2 * NQ
BC = 16
PANEL = 48
STEPS = 3
KEPT = 12
PIECES = 1
HALF = STEPS * 128 + 16
BLK = 128


def items(pairs):
    return [(a, d, k) for a, d in pairs for k in range(2)]


def wanted(name):
    a, d, _ = name
    return [(0, 0), (1, 1)] if (d - a) % 8 == 0 else [(0, 2)]


def passed_on(name):
    a, d, _ = name
    return [(1, 2)] if (d - a) % 8 == 0 else [(0, 1), (1, 0)]


VMEM = pltpu.VMEM
SMEM_SPEC = pl.BlockSpec(memory_space=pltpu.SMEM)
VMEM_SPEC = pl.BlockSpec(memory_space=pltpu.VMEM)
ANY_SPEC = pl.BlockSpec(memory_space=pl.ANY)
LIMIT = pltpu.CompilerParams(vmem_limit_bytes=16 << 20)


def moves(blocks):
    return pl.CostEstimate(flops=0, bytes_accessed=2 * blocks * BLK * BLK * 2, transcendentals=0)


def rows_shape(rows):
    return jax.ShapeDtypeStruct((rows, BLK), jnp.bfloat16)


def blk(n):
    return pl.ds(n * BLK, BLK)


def first_kernel(orders, index_ref, own_ref, other_ref, note_ref, *outs):
    for out, order in zip(outs, orders, strict=True):
        for n, (other, place) in enumerate(order):
            out[blk(n), :] = (other_ref if other else own_ref)[index_ref[place]]
        out[pl.ds(len(order) * BLK, 16), :] = note_ref[...]


def first_packed(index, own, other, note, orders):
    return pl.pallas_call(
        functools.partial(first_kernel, orders),
        out_shape=[rows_shape(len(order) * BLK + 16) for order in orders],
        in_specs=[SMEM_SPEC] + [VMEM_SPEC] * 3,
        out_specs=[VMEM_SPEC for _ in orders],
        compiler_params=LIMIT,
        cost_estimate=moves(sum(len(order) for order in orders)),
    )(index, own, other, note)


def right_kernel(index_ref, src_ref, code_ref, *rest):
    out = rest[-1]
    for n in range(16):
        for t in range(STEPS):
            out[n, blk(t), :] = src_ref[index_ref[n + t]]
        out[n, pl.ds(STEPS * BLK, 16), :] = code_ref[n]


def right_packed(src, index, codes, after):
    return pl.pallas_call(
        right_kernel,
        out_shape=jax.ShapeDtypeStruct((16, HALF, BLK), jnp.bfloat16),
        in_specs=[SMEM_SPEC, VMEM_SPEC, VMEM_SPEC] + [ANY_SPEC] * len(after),
        out_specs=VMEM_SPEC,
        compiler_params=LIMIT,
        cost_estimate=moves(48),
    )(index, src, codes, *after)


def turned(note, distance):
    if distance == 0:
        return note
    return jnp.concatenate([pltpu.roll(note[n : n + NQ], distance, 0) for n in (0, NQ)])


def pack_kernel(spec, notes, count, *refs):
    sources, outs = refs[:count], refs[-len(spec) :]
    if notes:
        merged = None
        rows = lax.broadcasted_iota(jnp.int32, (NOTE, BLK), 0)
        for source, row, distance, small in notes:
            if small:
                note = sources[source][pl.ds(row, 16), :].astype(jnp.float32)
                other = jnp.where(rows == NQ + distance, note[1:2], 0.0)
                note = jnp.where(rows == distance, note[0:1], other)
            else:
                note = turned(sources[source][pl.ds(row, NOTE), :].astype(jnp.float32), distance)
            merged = note if merged is None else jnp.maximum(merged, note)
        merged = merged.astype(jnp.bfloat16)
    for out, (entries, noted) in zip(outs, spec, strict=True):
        for n, (source, place) in enumerate(entries):
            out[blk(n), :] = sources[source][blk(place), :]
        if noted:
            out[pl.ds(len(entries) * BLK, NOTE), :] = merged


def pack(sources, spec, notes, after):
    used = sorted({e[0] for entries, _ in spec for e in entries} | {n[0] for n in notes})
    where = {source: n for n, source in enumerate(used)}
    spec = tuple((tuple((where[s], n) for s, n in entries), noted) for entries, noted in spec)
    notes = tuple((where[n[0]],) + tuple(n[1:]) for n in notes)
    return pl.pallas_call(
        functools.partial(pack_kernel, spec, notes, len(used)),
        out_shape=[rows_shape(len(entries) * BLK + NOTE * noted) for entries, noted in spec],
        in_specs=[VMEM_SPEC] * len(used) + [ANY_SPEC] * len(after),
        out_specs=[VMEM_SPEC for _ in spec],
        compiler_params=LIMIT,
        cost_estimate=moves(sum(len(entries) for entries, _ in spec)),
    )(*[sources[source] for source in used], *after)


def product_kernel(counts, base, first, last, table_ref, right_ref, *rest):
    lefts, rest = rest[: len(counts)], rest[len(counts) :]
    if last:
        before, out_ref, acc = rest
        acc[...] = before[...]
    elif first:
        (acc,) = rest
        acc[...] = jnp.zeros_like(acc)
    else:
        before, acc = rest
        acc[...] = before[...]
    for left, count in zip(lefts, counts, strict=True):

        def body(n, carry, left=left, base=base):
            block = left[pl.ds(pl.multiple_of(table_ref[base + n, 4], BLK), BLK), :]
            pair = []
            for rank in range(2):
                row = pl.multiple_of(table_ref[base + n, 2 * rank], 16)
                pair.append(right_ref[pl.ds(row, BLK), :])
            both = jnp.dot(block, jnp.concatenate(pair, axis=1), preferred_element_type=jnp.float32)
            acc[table_ref[base + n, 1]] += both[:, :BLK]
            acc[table_ref[base + n, 3]] += both[:, BLK:]
            return carry

        unroll = count if count <= 24 else max(n for n in range(1, 17) if count % n == 0)
        lax.fori_loop(0, count, body, 0, unroll=unroll)
        base += count
    if last:
        out_ref[...] = acc[:KEPT].astype(out_ref.dtype)


def product(table, right, lefts, counts, base, before=None, last=False):
    total = sum(counts)
    sums = jax.ShapeDtypeStruct((KEPT + 1, BLK, BLK), jnp.float32)
    return pl.pallas_call(
        functools.partial(product_kernel, counts, base, before is None, last),
        out_shape=jax.ShapeDtypeStruct((KEPT, BLK, BLK), jnp.bfloat16) if last else sums,
        in_specs=[SMEM_SPEC] + [VMEM_SPEC] * (1 + len(lefts) + (before is not None)),
        out_specs=VMEM_SPEC,
        scratch_shapes=[VMEM(sums.shape, jnp.float32)] if last else [],
        compiler_params=LIMIT,
        cost_estimate=pl.CostEstimate(
            flops=total * 16 * BLK**3, bytes_accessed=total * BLK * BLK * 2, transcendentals=0
        ),
    )(table, right, *lefts, *(() if before is None else (before,)))


def total(mask, value, axis):
    return jnp.sum(jnp.where(mask, value, 0.0), axis=axis, keepdims=True)


def table_kernel(note_rows, scalars, pick_ref, meta_ref, slots_ref, own, other, right, out, notes, tails, sems):
    copies = [
        pltpu.make_async_copy(
            ref.at[pl.ds(row, NOTE)], notes.at[pl.ds(n * NOTE, NOTE)], sems.at[n]
        )
        for n, (ref, row) in enumerate(zip((own, other), note_rows, strict=True))
    ]
    copies += [
        pltpu.make_async_copy(
            right.at[pl.ds(n * HALF + STEPS * BLK, 16)], tails.at[pl.ds(n * 16, 16)], sems.at[2 + n]
        )
        for n in range(16)
    ]
    for copy in copies:
        copy.start()
    for copy in copies:
        copy.wait()
    start, core = scalars[0], scalars[1]
    count = out.shape[0]
    lane = lax.broadcasted_iota(jnp.int32, (count, BLK), 1)
    panel = meta_ref[:, 0:1]
    picked = jnp.dot(pick_ref[...], notes[...], preferred_element_type=jnp.float32)
    at = (start + panel + core * (3 - 2 * panel)) & 15
    code = total(lane == at, picked, 1) * 64.0 + total(lane == at + 16, picked, 1)
    code = code.astype(jnp.int32) - 1
    left_row = (jnp.maximum(code, 0) * 43691) >> 21
    left_key = code - left_row * PANEL + (panel + core * (2 - 2 * panel)) * 64
    left_key = jnp.where(code >= 0, left_key, -2)
    rows = lax.broadcasted_iota(jnp.int32, (16, 256), 0)
    firsts = (rows * 16 == lax.broadcasted_iota(jnp.int32, (16, 256), 1)).astype(jnp.bfloat16)
    digits = jnp.dot(firsts, tails[...], preferred_element_type=jnp.float32).astype(jnp.bfloat16)
    rows = lax.broadcasted_iota(jnp.int32, (BLK, BLK), 0)
    cols = lax.broadcasted_iota(jnp.int32, (BLK, BLK), 1)
    owner = lax.broadcasted_iota(jnp.int32, (16, BLK), 0) == (cols[:16] & 15)
    values = []
    for digit in range(2):
        spread = (rows == (cols >> 4) + STEPS * digit).astype(jnp.bfloat16)
        spread = jnp.dot(digits, spread, preferred_element_type=jnp.float32)
        values.append(total(owner, spread, 0))
    right_code = (values[0] * 16.0 + values[1]).astype(jnp.int32) - 1
    line = cols[:1]
    live = (right_code >= 0) & (line < 16 * STEPS)
    key = jnp.where(live, (right_code >> 4) + (line >> 4) * 64, -1)
    column = (right_code & 15).astype(jnp.float32)
    keys = jnp.broadcast_to(key, (BLK, BLK)).astype(jnp.float32)
    turned_keys = total(rows == cols, keys, 1)
    rank = total((turned_keys == keys) & (rows < cols), 1.0, 0)
    place = ((line & 15) * HALF + (line >> 4) * BLK + 1).astype(jnp.float32)
    match = left_key == key
    table = jnp.where(lane == 4, meta_ref[:, 1:2], 0)
    for rank_number in range(2):
        hit = match & (rank == rank_number)
        found = total(hit, place, 1).astype(jnp.int32)
        target = left_row * BC + total(hit, column, 1).astype(jnp.int32)
        there = (slots_ref[...] == target) & (found > 0)
        slot = total(there, (lane - KEPT).astype(jnp.float32), 1).astype(jnp.int32) + KEPT
        table = jnp.where(lane == 2 * rank_number, jnp.maximum(found - 1, 0), table)
        table = jnp.where(lane == 2 * rank_number + 1, slot, table)
    out[...] = table


def tables(order, notes, right, slots, scalars):
    half = NQ // 4
    order = [
        (row, 1 - other, 1 - k, half, panel) if d == 3 * half else (row, other, k, d, panel)
        for row, other, k, d, panel in order
    ]
    order = np.array(order, np.int32)
    count = -(-order.shape[0] // 8) * 8
    pick = np.zeros((count, 2 * NOTE), np.float32)
    pick[np.arange(order.shape[0]), order[:, 1] * NOTE + order[:, 2] * NQ + order[:, 3]] = 1
    meta = np.zeros((count, BLK), np.int32)
    meta[: order.shape[0], 0] = order[:, 4]
    meta[: order.shape[0], 1] = order[:, 0]
    arrays, rows = zip(*notes, strict=True)
    return pl.pallas_call(
        functools.partial(table_kernel, rows),
        out_shape=jax.ShapeDtypeStruct((count, BLK), jnp.int32),
        in_specs=[SMEM_SPEC] + [VMEM_SPEC] * 3 + [ANY_SPEC] * 3,
        out_specs=VMEM_SPEC,
        scratch_shapes=[
            VMEM((2 * NOTE, BLK), jnp.bfloat16),
            VMEM((256, BLK), jnp.bfloat16),
            pltpu.SemaphoreType.DMA((18,)),
        ],
        compiler_params=LIMIT,
        cost_estimate=pl.CostEstimate(
            flops=count * BLK * 200, bytes_accessed=count * BLK * 8, transcendentals=0
        ),
    )(scalars, jnp.asarray(pick, jnp.bfloat16), jnp.asarray(meta), slots, *arrays, right)


def moved(array, distance):
    route = []
    for i in range(NQ):
        route.append((2 * i, 2 * ((i + distance) % NQ)))
        route.append((2 * i + 1, 2 * ((i - distance) % NQ) + 1))
    return lax.ppermute(array, COL, route)


def from_other_core(array):
    return lax.ppermute(array, "core", [(0, 1), (1, 0)])


def local(a_own_values, a_own_code, b_own_values, b_own_code, c_code):
    r = lax.axis_index(ROW)
    q = lax.axis_index(("xh", "z"))
    core = lax.axis_index("core")
    start = (r + 2 * q) % 16
    a_own = a_own_values.reshape(16, BLK, BLK)
    b_own = b_own_values.reshape(16, BLK, BLK)

    def note_of(code):
        code = code.reshape(16) + 1
        digits = jnp.concatenate([code // 64, code % 64]).astype(jnp.bfloat16).reshape(1, 32)
        return jnp.pad(digits, ((0, 15), (0, BLK - 32)))

    sources, at = [], {}

    def keep(array, names):
        for n, name in enumerate(names):
            at[name] = (len(sources), 2 * n)
        sources.append(array)
        return len(sources) - 1

    def send(array, names, distance):
        return keep(moved(array, distance), [(a, (d + distance) % NQ, k) for a, d, k in names])

    def blocks(names):
        return [(at[name][0], at[name][1] + b) for name in names for b in range(2)]

    def packed(spec, notes=(), after=()):
        return pack(sources, spec, notes, after)

    note = note_of(a_own_code)
    a_other, note_other = from_other_core(a_own), from_other_core(note)

    shift = (2 * q + core + jnp.arange(18, dtype=jnp.int32)) % 16
    b_code = b_own_code.reshape(16) + 1
    b_code = jnp.sum(jnp.where(shift[:, None] == jnp.arange(16)[None, :], b_code[None, :], 0), axis=1)
    b_code = jnp.stack([b_code[t : t + 16] for t in range(STEPS)], axis=1)
    b_code = jnp.concatenate([b_code // 16, b_code % 16], axis=1).astype(jnp.bfloat16)
    b_code = jnp.broadcast_to(jnp.pad(b_code, ((0, 0), (0, BLK - 6)))[:, None, :], (16, 16, BLK))
    right = right_packed(b_own, shift, b_code, (note_other, a_other))
    right = lax.all_to_all(right, ROW, 0, 0, tiled=True).reshape(16 * HALF, BLK)
    note = jnp.concatenate([note[:1], note_other[:1], note[2:]])
    a_index = jnp.arange(16, dtype=jnp.int32)
    a_index = (start + jnp.where(core == 0, a_index, 3 - a_index)) % 16

    starts = [
        (items([(2, 0), (3, 0), (4, 0)]), 2),
        (items([(6, 0), (7, 0), (0, 0)]), 14),
        (items([(1, 0), (2, 0)]), 1),
        (items([(5, 0), (6, 0)]), 13),
        ([(4, 0, 0), (5, 0, 0)], 12),
    ]
    orders = tuple(
        tuple((k, 2 * a + b) for a, _, k in names for b in range(2)) for names, _ in starts
    )
    arrays = first_packed(a_index, a_own, a_other, note, orders)
    near = []
    for array, (names, _) in zip(arrays[:4], starts[:4], strict=True):
        own = keep(array, names)
    near.append((own, 8 * BLK, 0, True))
    for array, (names, distance) in zip(arrays[:4], starts[:4], strict=True):
        near.append((send(array, names, distance), 2 * len(names) * BLK, distance, True))

    long_names = items([(1, 1), (5, 13), (2, 2), (6, 14)])
    names = items([(3, 2), (7, 14), (0, 14), (4, 2)])
    long_in, up_in = packed([(blocks(long_names), True), (blocks(names), True)], near)
    far = [(len(sources), 16 * BLK, 0, False)]
    sources.append(long_in)
    far.append((send(long_in, long_names, 15), 16 * BLK, 15, False))
    far.append((send(up_in, names, 1), 16 * BLK, 1, False))
    across, opposite, _ = lax.optimization_barrier((arrays[4], note, long_in))
    far.append((send(across, *starts[4]), 4 * BLK, starts[4][1], True))
    sources.append(moved(opposite, NQ // 4))
    far.append((len(sources) - 1, 0, NQ // 4, True))

    early = items([(1, 1), (5, 13), (2, 2), (6, 14), (2, 1), (6, 13), (3, 2), (7, 14)])

    def pass_on(names, pieces, kept=None, notes=(), after=()):
        entries = [(at[name][0], at[name][1] + b) for name in names for b, _ in passed_on(name)]
        size = -(-len(entries) // pieces)
        spec = [(entries[n * size : (n + 1) * size], bool(notes) and n == pieces - 1) for n in range(pieces)]
        if kept:
            spec.append(([(at[name][0], at[name][1] + b) for name in kept for b, _ in wanted(name)], False))
        arrays = packed(spec, notes, after)
        received = [from_other_core(array) for array in arrays[:pieces]]
        end = (len(entries) - size * (pieces - 1)) * BLK
        return received, arrays[pieces:], ((arrays[pieces - 1], end), (received[-1], end))

    mine = items([(0, 0), (1, 0)]) + early
    early_other, early_own, early_notes = pass_on(early, PIECES, mine, near, (long_in,))

    names = items([(1, 16), (5, 4), (2, 17), (6, 5), (0, 15), (4, 3)])
    (up_in,) = packed([(blocks(names), False)], (), [sources[note[0]] for note in far[-2:]])
    send(up_in, names, 1)

    late = [(4, 12, 0), (5, 12, 0)] + items([(3, 3), (7, 15)]) + names
    last = items([(1, 17), (5, 5), (2, 18), (6, 6), (0, 16), (4, 4)])
    late_other, late_own, late_notes = pass_on(late, 3, late, far, (up_in,))

    def kept_of(array, names):
        found = [(name, panel) for name in names for _, panel in wanted(name)]
        return [(array, [(m * BLK, 0, n[2], n[1], panel) for m, (n, panel) in enumerate(found)])]

    def part_of(names):
        by_source = {}
        for name in names:
            source, place = at[name]
            for b, panel in wanted(name):
                by_source.setdefault(source, []).append(((place + b) * BLK, 0, name[2], name[1], panel))
        return [(sources[source], rows) for source, rows in sorted(by_source.items())]

    def received_of(arrays, names):
        found = [(name, panel) for name in names for _, panel in passed_on(name)]
        size = -(-len(found) // len(arrays))
        return [
            (array, [(m * BLK, 1, name[2], name[1], panel) for m, (name, panel) in enumerate(found[n * size : (n + 1) * size])])
            for n, array in enumerate(arrays)
        ]

    slots = jnp.pad(c_code.reshape(1, KEPT), ((0, 0), (0, BLK - KEPT)), constant_values=-1)
    scalars = jnp.stack([start, core]).astype(jnp.int32)

    def table_of(parts, notes):
        order = [row for part in parts for _, rows in part for row in rows]
        return tables(order, notes, right, slots, scalars)

    def product_of(table, part, base, before=None, last=False):
        lefts, counts = [array for array, _ in part], tuple(len(rows) for _, rows in part)
        return product(table, right, lefts, counts, base, before, last), base + sum(counts)

    part = kept_of(early_own[0], mine) + received_of(early_other, early)
    sums, _ = product_of(table_of((part,), early_notes), part, 0)
    part = kept_of(late_own[0], late) + received_of(late_other, late)
    parts = [part, part_of(last), received_of([None], last)]
    table = table_of(parts, late_notes)
    sums, base = product_of(table, part, 0, sums)
    last_other, _, _ = pass_on(last, 1, None, (), (sums,))
    sums, base = product_of(table, parts[1], base, sums)
    out, _ = product_of(table, received_of(last_other, last), base, sums, last=True)
    return out[None, None]


def solution(mesh):
    fine = Mesh(mesh.devices.reshape(SIZES), AXES)
    return jax.shard_map(
        local,
        mesh=fine,
        in_specs=(
            P(ROW, COL, None, None, None, None),
            P(ROW, COL, None, None),
            P(ROW, COL, None, None, None, None),
            P(ROW, COL, None, None),
            P(ROW, COL, None),
        ),
        out_specs=P(ROW, COL, None, None, None),
        check_vma=False,
    )
```

```python
import functools

import jax
import jax.numpy as jnp
import numpy as np
from jax import lax
from jax.experimental import pallas as pl
from jax.experimental.pallas import tpu as pltpu
from jax.sharding import Mesh
from jax.sharding import PartitionSpec as P

AXES = ("xl", "y", "xh", "z", "core")
ROW = ("xl", "y")
COL = ("xh", "z", "core")
SIZES = (2, 8, 2, 12, 2)
NQ = 24
NOTE = 2 * NQ
BC = 16
PANEL = 48
STEPS = 3
KEPT = 12
SPAN = 8 + STEPS - 1
HALF = STEPS * 128 + 16
BLK = 128


def items(pairs):
    return [(a, d, k) for a, d in pairs for k in range(2)]


def wanted(name):
    a, d, _ = name
    return [(0, 0), (1, 1)] if (d - a) % 8 == 0 else [(0, 2)]


def passed_on(name):
    a, d, _ = name
    return [(1, 2)] if (d - a) % 8 == 0 else [(0, 1), (1, 0)]


VMEM = pltpu.VMEM
SMEM_SPEC = pl.BlockSpec(memory_space=pltpu.SMEM)
VMEM_SPEC = pl.BlockSpec(memory_space=pltpu.VMEM)
ANY_SPEC = pl.BlockSpec(memory_space=pl.ANY)
LIMIT = pltpu.CompilerParams(vmem_limit_bytes=16 << 20)


def moves(blocks):
    return pl.CostEstimate(flops=0, bytes_accessed=2 * blocks * BLK * BLK * 2, transcendentals=0)


def rows_shape(rows):
    return jax.ShapeDtypeStruct((rows, BLK), jnp.bfloat16)


def blk(n):
    return pl.ds(n * BLK, BLK)


def first_kernel(orders, index_ref, own_ref, other_ref, note_ref, *outs):
    for out, order in zip(outs, orders, strict=True):
        for n, (other, place) in enumerate(order):
            out[blk(n), :] = (other_ref if other else own_ref)[index_ref[place]]
        out[pl.ds(len(order) * BLK, 16), :] = note_ref[...]


def first_packed(index, own, other, note, orders):
    return pl.pallas_call(
        functools.partial(first_kernel, orders),
        out_shape=[rows_shape(len(order) * BLK + 16) for order in orders],
        in_specs=[SMEM_SPEC] + [VMEM_SPEC] * 3,
        out_specs=[VMEM_SPEC for _ in orders],
        compiler_params=LIMIT,
        cost_estimate=moves(sum(len(order) for order in orders)),
    )(index, own, other, note)


def split_kernel(index_ref, src_ref, note_ref, *outs):
    for half, out in enumerate(outs):
        for n in range(SPAN):
            out[blk(n), :] = src_ref[index_ref[SPAN * half + n]]
        out[pl.ds(SPAN * BLK, 16), :] = note_ref[...]


def split(index, src, note):
    return pl.pallas_call(
        split_kernel,
        out_shape=[rows_shape(SPAN * BLK + 16)] * 2,
        in_specs=[SMEM_SPEC, VMEM_SPEC, VMEM_SPEC],
        out_specs=[VMEM_SPEC] * 2,
        compiler_params=LIMIT,
        cost_estimate=moves(2 * SPAN),
    )(index, src, note)


def right_kernel(*refs):
    sources, out = refs[:2], refs[-1]
    for n in range(8):
        for half, source in enumerate(sources):
            out[n, pl.ds(half * HALF, STEPS * BLK), :] = source[pl.ds(n * BLK, STEPS * BLK), :]
            note = source[pl.ds(SPAN * BLK, 16), :]
            out[n, pl.ds(half * HALF + STEPS * BLK, 16), :] = note


def right_packed(kept, other, after):
    return pl.pallas_call(
        right_kernel,
        out_shape=jax.ShapeDtypeStruct((8, 2 * HALF, BLK), jnp.bfloat16),
        in_specs=[VMEM_SPEC, VMEM_SPEC, ANY_SPEC],
        out_specs=VMEM_SPEC,
        compiler_params=LIMIT,
        cost_estimate=moves(48),
    )(kept, other, after)


def turned(note, distance):
    if distance == 0:
        return note
    return jnp.concatenate([pltpu.roll(note[n : n + NQ], distance, 0) for n in (0, NQ)])


def pack_kernel(spec, notes, count, *refs):
    sources, outs = refs[:count], refs[-len(spec) :]
    if notes:
        merged = None
        rows = lax.broadcasted_iota(jnp.int32, (NOTE, BLK), 0)
        for source, row, distance, small in notes:
            if small:
                note = sources[source][pl.ds(row, 16), :].astype(jnp.float32)
                other = jnp.where(rows == NQ + distance, note[1:2], 0.0)
                note = jnp.where(rows == distance, note[0:1], other)
            else:
                note = turned(sources[source][pl.ds(row, NOTE), :].astype(jnp.float32), distance)
            merged = note if merged is None else jnp.maximum(merged, note)
        merged = merged.astype(jnp.bfloat16)
    for out, (entries, noted) in zip(outs, spec, strict=True):
        for n, (source, place) in enumerate(entries):
            out[blk(n), :] = sources[source][blk(place), :]
        if noted:
            out[pl.ds(len(entries) * BLK, NOTE), :] = merged


def pack(sources, spec, notes, after):
    used = sorted({e[0] for entries, _ in spec for e in entries} | {n[0] for n in notes})
    where = {source: n for n, source in enumerate(used)}
    spec = tuple((tuple((where[s], n) for s, n in entries), noted) for entries, noted in spec)
    notes = tuple((where[n[0]],) + tuple(n[1:]) for n in notes)
    return pl.pallas_call(
        functools.partial(pack_kernel, spec, notes, len(used)),
        out_shape=[rows_shape(len(entries) * BLK + NOTE * noted) for entries, noted in spec],
        in_specs=[VMEM_SPEC] * len(used) + [ANY_SPEC] * len(after),
        out_specs=[VMEM_SPEC for _ in spec],
        compiler_params=LIMIT,
        cost_estimate=moves(sum(len(entries) for entries, _ in spec)),
    )(*[sources[source] for source in used], *after)


def product_kernel(counts, base, first, last, table_ref, right_ref, *rest):
    lefts, rest = rest[: len(counts)], rest[len(counts) :]
    if last:
        before, out_ref, acc = rest
        acc[...] = before[...]
    elif first:
        (acc,) = rest
        acc[...] = jnp.zeros_like(acc)
    else:
        before, acc = rest
        acc[...] = before[...]
    for left, count in zip(lefts, counts, strict=True):

        def body(n, carry, left=left, base=base):
            block = left[pl.ds(pl.multiple_of(table_ref[4, base + n], BLK), BLK), :]
            pair = []
            for rank in range(2):
                row = pl.multiple_of(table_ref[2 * rank, base + n], 16)
                pair.append(right_ref[pl.ds(row, BLK), :])
            both = jnp.dot(block, jnp.concatenate(pair, axis=1), preferred_element_type=jnp.float32)
            acc[table_ref[1, base + n]] += both[:, :BLK]
            acc[table_ref[3, base + n]] += both[:, BLK:]
            return carry

        unroll = count if count <= 24 else max(n for n in range(1, 17) if count % n == 0)
        lax.fori_loop(0, count, body, 0, unroll=unroll)
        base += count
    if last:
        out_ref[...] = acc[:KEPT].astype(out_ref.dtype)


def product(table, right, lefts, counts, base, before=None, last=False):
    total = sum(counts)
    sums = jax.ShapeDtypeStruct((KEPT + 1, BLK, BLK), jnp.float32)
    return pl.pallas_call(
        functools.partial(product_kernel, counts, base, before is None, last),
        out_shape=jax.ShapeDtypeStruct((KEPT, BLK, BLK), jnp.bfloat16) if last else sums,
        in_specs=[SMEM_SPEC] + [VMEM_SPEC] * (1 + len(lefts) + (before is not None)),
        out_specs=VMEM_SPEC,
        scratch_shapes=[VMEM(sums.shape, jnp.float32)] if last else [],
        compiler_params=LIMIT,
        cost_estimate=pl.CostEstimate(
            flops=total * 16 * BLK**3, bytes_accessed=total * BLK * BLK * 2, transcendentals=0
        ),
    )(table, right, *lefts, *(() if before is None else (before,)))


def tables(order, notes, right_codes, c_code, start, core):
    order = np.array(order, np.int32)
    count = order.shape[0]
    row, other, k, distance, panel = (order[:, n] for n in range(5))
    notes = jnp.stack(notes)[:, :, :32].astype(jnp.int32)
    flat = (notes[:, :, :16] * 64 + notes[:, :, 16:] - 1).reshape(1, 2 * NOTE * 16)
    of = (start + panel + core * (3 - 2 * panel)) % 16
    place = (other * NOTE + k * NQ + distance) * 16 + of
    codes = jnp.sum(jnp.where(place[:, None] == jnp.arange(2 * NOTE * 16)[None, :], flat, 0), axis=1)
    step = panel + core * (2 - 2 * panel)
    right_live = right_codes >= 0
    right_inner = jnp.where(right_live, right_codes // BC, -1)
    owners = jnp.arange(16, dtype=jnp.int32)
    earlier = owners[None, :] < owners[:, None]
    rank = jnp.sum(
        ((right_inner[:, None, :] == right_inner[None, :, :]) & earlier[:, :, None]).astype(jnp.int32),
        axis=1,
    )
    packed = jnp.where(right_live, right_inner * 1024 + rank * 32 + right_codes % BC, -1)
    right_n = jnp.where(
        (step == 0)[:, None],
        packed[None, :, 0],
        jnp.where((step == 1)[:, None], packed[None, :, 1], packed[None, :, 2]),
    )
    match = (right_n >= 0) & (codes >= 0)[:, None] & ((right_n // 1024) == (codes % PANEL)[:, None])
    rows = []
    for rank_number in range(2):
        hit = match & ((right_n // 32) % 32 == rank_number)
        found = jnp.sum(jnp.where(hit, owners[None, :] * 32 + right_n % 32 + 1, 0), axis=1)
        partner = jnp.maximum(found - 1, 0)
        target = (codes // PANEL) * BC + partner % 32
        there = (target[:, None] == c_code[None, :]) & (found > 0)[:, None]
        slot = jnp.sum(jnp.where(there, jnp.arange(KEPT)[None, :] - KEPT, 0), axis=1) + KEPT
        rows += [partner // 32 * HALF + step * BLK, slot]
    return jnp.stack(rows + [jnp.array(row)]).astype(jnp.int32).reshape(5, count)


def moved(array, distance):
    route = []
    for i in range(NQ):
        route.append((2 * i, 2 * ((i + distance) % NQ)))
        route.append((2 * i + 1, 2 * ((i - distance) % NQ) + 1))
    return lax.ppermute(array, COL, route)


def from_other_core(array):
    return lax.ppermute(array, "core", [(0, 1), (1, 0)])


def local(a_own_values, a_own_code, b_own_values, b_own_code, c_code):
    r = lax.axis_index(ROW)
    q = lax.axis_index(("xh", "z"))
    core = lax.axis_index("core")
    start = (r + 2 * q) % 16
    a_own = a_own_values.reshape(16, BLK, BLK)
    b_own = b_own_values.reshape(16, BLK, BLK)

    def note_of(code):
        code = code.reshape(16) + 1
        digits = jnp.concatenate([code // 64, code % 64]).astype(jnp.bfloat16).reshape(1, 32)
        return jnp.pad(digits, ((0, 15), (0, BLK - 32)))

    spans = 2 * q + core + 8 * lax.axis_index("xl") + jnp.arange(SPAN, dtype=jnp.int32)
    b_kept, b_sent = split(jnp.concatenate([spans, spans + 8]) % 16, b_own, note_of(b_own_code))
    b_other = lax.ppermute(b_sent, "xl", [(0, 1), (1, 0)])

    sources, at = [], {}

    def keep(array, names):
        for n, name in enumerate(names):
            at[name] = (len(sources), 2 * n)
        sources.append(array)
        return len(sources) - 1

    def send(array, names, distance):
        return keep(moved(array, distance), [(a, (d + distance) % NQ, k) for a, d, k in names])

    def blocks(names):
        return [(at[name][0], at[name][1] + b) for name in names for b in range(2)]

    def packed(spec, notes=(), after=()):
        return pack(sources, spec, notes, after)

    note = note_of(a_own_code)
    a_other, note_other = from_other_core(a_own), from_other_core(note)
    note = jnp.concatenate([note[:1], note_other[:1], note[2:]])
    a_index = jnp.arange(16, dtype=jnp.int32)
    a_index = (start + jnp.where(core == 0, a_index, 3 - a_index)) % 16

    starts = [
        (items([(3, 0), (4, 0)]), 2),
        (items([(7, 0), (0, 0)]), 14),
        (items([(1, 0), (2, 0)]), 1),
        (items([(5, 0), (6, 0)]), 13),
        ([(4, 0, 0), (5, 0, 0)], 12),
    ]
    orders = tuple(
        tuple((k, 2 * a + b) for a, _, k in names for b in range(2)) for names, _ in starts
    )
    arrays = first_packed(a_index, a_own, a_other, note, orders)
    near = []
    for array, (names, _) in zip(arrays[:4], starts[:4], strict=True):
        own = keep(array, names)
    near.append((own, 8 * BLK, 0, True))
    for array, (names, distance) in zip(arrays[:4], starts[:4], strict=True):
        near.append((send(array, names, distance), 2 * len(names) * BLK, distance, True))

    names = items([(2, 1), (6, 13), (3, 2), (7, 14), (0, 14), (4, 2)])
    (up_in,) = packed([(blocks(names), True)], near, (b_other,))
    sources.append(up_in)
    up3 = send(up_in, names, 1)
    right = lax.all_to_all(right_packed(b_kept, b_other, up_in), "y", 0, 0, tiled=True)
    right = right.reshape(16 * HALF, BLK)
    middle = [(up3 - 1, 24 * BLK, 0, False), (up3, 24 * BLK, 1, False)]

    names = items([(1, 1), (5, 13), (2, 2), (6, 14)])
    (up_in,) = packed([(blocks(names), True)], middle)
    up6 = send(up_in, names, 15)
    across, _ = lax.optimization_barrier((arrays[4], up_in))
    middle.append((send(across, *starts[4]), 4 * BLK, starts[4][1], True))
    far = middle + [(up6, 16 * BLK, 15, False)]

    early = items([(1, 1), (5, 13), (2, 2), (6, 14), (3, 3), (7, 15)]) + [(4, 12, 0)]
    early += items([(2, 1), (6, 13), (3, 2), (7, 14), (0, 15), (4, 3)]) + [(5, 12, 0)]

    def pass_on(names, kept=None, notes=(), after=()):
        entries = [(at[name][0], at[name][1] + b) for name in names for b, _ in passed_on(name)]
        spec = [(entries, bool(notes))]
        if kept:
            spec.append(([(at[name][0], at[name][1] + b) for name in kept for b, _ in wanted(name)], False))
        array, *own_part = packed(spec, notes, after)
        received = from_other_core(array)
        end = len(entries) * BLK
        return received, own_part, (array[end:], received[end:])

    mine = items([(0, 0), (1, 0)]) + early
    early_other, early_own, early_notes = pass_on(early, mine, middle, (up_in,))

    names = items([(1, 16), (5, 4), (2, 17), (6, 5), (0, 15), (4, 3)])
    up_in, notes = packed([(blocks(names), False), ((), True)], far)
    send(up_in, names, 1)
    notes = (notes, from_other_core(notes))

    middle = items([(1, 16), (5, 4), (2, 17), (6, 5)])
    last = items([(1, 17), (5, 5), (2, 18), (6, 6), (0, 16), (4, 4)])

    def part_of(names):
        by_source = {}
        for name in names:
            source, place = at[name]
            for b, panel in wanted(name):
                by_source.setdefault(source, []).append(((place + b) * BLK, 0, name[2], name[1], panel))
        return [(sources[source], rows) for source, rows in sorted(by_source.items())]

    def received_of(array, names):
        rows = []
        for name in names:
            for _, panel in passed_on(name):
                rows.append((len(rows) * BLK, 1, name[2], name[1], panel))
        return [(array, rows)]

    panels = (start + core + jnp.arange(STEPS, dtype=jnp.int32)) % 16
    digits = right.reshape(16, HALF, BLK)[:, STEPS * BLK, :32].astype(jnp.int32)
    right_codes = (digits[:, :16] * 64 + digits[:, 16:] - 1)[:, None, :]
    right_codes = jnp.sum(
        jnp.where(panels[:, None] == jnp.arange(16)[None, :], right_codes, 0), axis=2
    )
    c_code = c_code.reshape(KEPT)

    def table_of(parts, notes):
        order = [row for part in parts for _, rows in part for row in rows]
        return tables(order, notes, right_codes, c_code, start, core)

    def product_of(table, part, base, before=None, last=False):
        lefts, counts = [array for array, _ in part], tuple(len(rows) for _, rows in part)
        return product(table, right, lefts, counts, base, before, last), base + sum(counts)

    rows = []
    for name in mine:
        rows += [(len(rows) * BLK + n * BLK, 0, name[2], name[1], w) for n, (_, w) in enumerate(wanted(name))]
    part = [(early_own[0], rows)] + received_of(early_other, early)
    sums, _ = product_of(table_of((part,), early_notes), part, 0)
    parts = [part_of(middle + last) + received_of(None, middle), received_of(None, last)]
    table = table_of(parts, notes)
    middle_other, _, _ = pass_on(middle, None, (), (sums,))
    last_other, _, _ = pass_on(last, None, (), (sums,))
    parts[0] = part_of(middle + last) + received_of(middle_other, middle)
    sums, base = product_of(table, parts[0], 0, sums)
    out, _ = product_of(table, received_of(last_other, last), base, sums, last=True)
    return out[None, None]


def solution(mesh):
    fine = Mesh(mesh.devices.reshape(SIZES), AXES)
    return jax.shard_map(
        local,
        mesh=fine,
        in_specs=(
            P(ROW, COL, None, None, None, None),
            P(ROW, COL, None, None),
            P(ROW, COL, None, None, None, None),
            P(ROW, COL, None, None),
            P(ROW, COL, None),
        ),
        out_specs=P(ROW, COL, None, None, None),
        check_vma=False,
    )
```

```python
import functools

import jax
import jax.numpy as jnp
import numpy as np
from jax import lax
from jax.experimental import pallas as pl
from jax.experimental.pallas import tpu as pltpu
from jax.sharding import Mesh
from jax.sharding import PartitionSpec as P

AXES = ("xl", "y", "xh", "z", "core")
ROW = ("xl", "y")
COL = ("xh", "z", "core")
SIZES = (2, 8, 2, 12, 2)
NQ = 24
NOTE = 2 * NQ
BC = 16
PANEL = 48
STEPS = 3
KEPT = 12
SPAN = 8 + STEPS - 1
HALF = STEPS * 128 + 16
BLK = 128


def items(pairs):
    return [(a, d, k) for a, d in pairs for k in range(2)]


def wanted(name):
    a, d, _ = name
    return [(0, 0), (1, 1)] if (d - a) % 8 == 0 else [(0, 2)]


def passed_on(name):
    a, d, _ = name
    return [(1, 2)] if (d - a) % 8 == 0 else [(0, 1), (1, 0)]


VMEM = pltpu.VMEM
SMEM_SPEC = pl.BlockSpec(memory_space=pltpu.SMEM)
VMEM_SPEC = pl.BlockSpec(memory_space=pltpu.VMEM)
ANY_SPEC = pl.BlockSpec(memory_space=pl.ANY)
LIMIT = pltpu.CompilerParams(vmem_limit_bytes=16 << 20)


def moves(blocks):
    return pl.CostEstimate(flops=0, bytes_accessed=2 * blocks * BLK * BLK * 2, transcendentals=0)


def rows_shape(rows):
    return jax.ShapeDtypeStruct((rows, BLK), jnp.bfloat16)


def blk(n):
    return pl.ds(n * BLK, BLK)


def first_kernel(orders, index_ref, own_ref, other_ref, note_ref, *outs):
    for out, order in zip(outs, orders, strict=True):
        for n, (other, place) in enumerate(order):
            out[blk(n), :] = (other_ref if other else own_ref)[index_ref[place]]
        out[pl.ds(len(order) * BLK, 16), :] = note_ref[...]


def first_packed(index, own, other, note, orders):
    return pl.pallas_call(
        functools.partial(first_kernel, orders),
        out_shape=[rows_shape(len(order) * BLK + 16) for order in orders],
        in_specs=[SMEM_SPEC] + [VMEM_SPEC] * 3,
        out_specs=[VMEM_SPEC for _ in orders],
        compiler_params=LIMIT,
        cost_estimate=moves(sum(len(order) for order in orders)),
    )(index, own, other, note)


def split_kernel(index_ref, src_ref, note_ref, *outs):
    for half, out in enumerate(outs):
        for n in range(SPAN):
            out[blk(n), :] = src_ref[index_ref[SPAN * half + n]]
        out[pl.ds(SPAN * BLK, 16), :] = note_ref[...]


def split(index, src, note):
    return pl.pallas_call(
        split_kernel,
        out_shape=[rows_shape(SPAN * BLK + 16)] * 2,
        in_specs=[SMEM_SPEC, VMEM_SPEC, VMEM_SPEC],
        out_specs=[VMEM_SPEC] * 2,
        compiler_params=LIMIT,
        cost_estimate=moves(2 * SPAN),
    )(index, src, note)


def right_kernel(*refs):
    sources, out = refs[:2], refs[-1]
    for n in range(8):
        for half, source in enumerate(sources):
            out[n, pl.ds(half * HALF, STEPS * BLK), :] = source[pl.ds(n * BLK, STEPS * BLK), :]
            note = source[pl.ds(SPAN * BLK, 16), :]
            out[n, pl.ds(half * HALF + STEPS * BLK, 16), :] = note


def right_packed(kept, other, after):
    return pl.pallas_call(
        right_kernel,
        out_shape=jax.ShapeDtypeStruct((8, 2 * HALF, BLK), jnp.bfloat16),
        in_specs=[VMEM_SPEC, VMEM_SPEC, ANY_SPEC],
        out_specs=VMEM_SPEC,
        compiler_params=LIMIT,
        cost_estimate=moves(48),
    )(kept, other, after)


def turned(note, distance):
    if distance == 0:
        return note
    return jnp.concatenate([pltpu.roll(note[n : n + NQ], distance, 0) for n in (0, NQ)])


def pack_kernel(spec, notes, count, *refs):
    sources, outs = refs[:count], refs[-len(spec) :]
    if notes:
        merged = None
        rows = lax.broadcasted_iota(jnp.int32, (NOTE, BLK), 0)
        for source, row, distance, small in notes:
            if small:
                note = sources[source][pl.ds(row, 16), :].astype(jnp.float32)
                other = jnp.where(rows == NQ + distance, note[1:2], 0.0)
                note = jnp.where(rows == distance, note[0:1], other)
            else:
                note = turned(sources[source][pl.ds(row, NOTE), :].astype(jnp.float32), distance)
            merged = note if merged is None else jnp.maximum(merged, note)
        merged = merged.astype(jnp.bfloat16)
    for out, (entries, noted) in zip(outs, spec, strict=True):
        for n, (source, place) in enumerate(entries):
            out[blk(n), :] = sources[source][blk(place), :]
        if noted:
            out[pl.ds(len(entries) * BLK, NOTE), :] = merged


def pack(sources, spec, notes, after):
    used = sorted({e[0] for entries, _ in spec for e in entries} | {n[0] for n in notes})
    where = {source: n for n, source in enumerate(used)}
    spec = tuple((tuple((where[s], n) for s, n in entries), noted) for entries, noted in spec)
    notes = tuple((where[n[0]],) + tuple(n[1:]) for n in notes)
    return pl.pallas_call(
        functools.partial(pack_kernel, spec, notes, len(used)),
        out_shape=[rows_shape(len(entries) * BLK + NOTE * noted) for entries, noted in spec],
        in_specs=[VMEM_SPEC] * len(used) + [ANY_SPEC] * len(after),
        out_specs=[VMEM_SPEC for _ in spec],
        compiler_params=LIMIT,
        cost_estimate=moves(sum(len(entries) for entries, _ in spec)),
    )(*[sources[source] for source in used], *after)


def product_kernel(counts, base, first, last, table_ref, right_ref, *rest):
    lefts, rest = rest[: len(counts)], rest[len(counts) :]
    if last:
        before, out_ref, acc = rest
        acc[...] = before[...]
    elif first:
        (acc,) = rest
        acc[...] = jnp.zeros_like(acc)
    else:
        before, acc = rest
        acc[...] = before[...]
    for left, count in zip(lefts, counts, strict=True):

        def body(n, carry, left=left, base=base):
            block = left[pl.ds(pl.multiple_of(table_ref[4, base + n], BLK), BLK), :]
            pair = []
            for rank in range(2):
                row = pl.multiple_of(table_ref[2 * rank, base + n], 16)
                pair.append(right_ref[pl.ds(row, BLK), :])
            both = jnp.dot(block, jnp.concatenate(pair, axis=1), preferred_element_type=jnp.float32)
            acc[table_ref[1, base + n]] += both[:, :BLK]
            acc[table_ref[3, base + n]] += both[:, BLK:]
            return carry

        unroll = count if count <= 24 else max(n for n in range(1, 17) if count % n == 0)
        lax.fori_loop(0, count, body, 0, unroll=unroll)
        base += count
    if last:
        out_ref[...] = acc[:KEPT].astype(out_ref.dtype)


def product(table, right, lefts, counts, base, before=None, last=False):
    total = sum(counts)
    sums = jax.ShapeDtypeStruct((KEPT + 1, BLK, BLK), jnp.float32)
    return pl.pallas_call(
        functools.partial(product_kernel, counts, base, before is None, last),
        out_shape=jax.ShapeDtypeStruct((KEPT, BLK, BLK), jnp.bfloat16) if last else sums,
        in_specs=[SMEM_SPEC] + [VMEM_SPEC] * (1 + len(lefts) + (before is not None)),
        out_specs=VMEM_SPEC,
        scratch_shapes=[VMEM(sums.shape, jnp.float32)] if last else [],
        compiler_params=LIMIT,
        cost_estimate=pl.CostEstimate(
            flops=total * 16 * BLK**3, bytes_accessed=total * BLK * BLK * 2, transcendentals=0
        ),
    )(table, right, *lefts, *(() if before is None else (before,)))


def tables(order, notes, right_codes, c_code, start, core):
    order = np.array(order, np.int32)
    count = order.shape[0]
    row, other, k, distance, panel = (order[:, n] for n in range(5))
    notes = jnp.stack(notes)[:, :, :32].astype(jnp.int32)
    flat = (notes[:, :, :16] * 64 + notes[:, :, 16:] - 1).reshape(1, 2 * NOTE * 16)
    of = (start + panel + core * (3 - 2 * panel)) % 16
    place = (other * NOTE + k * NQ + distance) * 16 + of
    codes = jnp.sum(jnp.where(place[:, None] == jnp.arange(2 * NOTE * 16)[None, :], flat, 0), axis=1)
    step = panel + core * (2 - 2 * panel)
    right_live = right_codes >= 0
    right_inner = jnp.where(right_live, right_codes // BC, -1)
    owners = jnp.arange(16, dtype=jnp.int32)
    earlier = owners[None, :] < owners[:, None]
    rank = jnp.sum(
        ((right_inner[:, None, :] == right_inner[None, :, :]) & earlier[:, :, None]).astype(jnp.int32),
        axis=1,
    )
    packed = jnp.where(right_live, right_inner * 1024 + rank * 32 + right_codes % BC, -1)
    right_n = jnp.where(
        (step == 0)[:, None],
        packed[None, :, 0],
        jnp.where((step == 1)[:, None], packed[None, :, 1], packed[None, :, 2]),
    )
    match = (right_n >= 0) & (codes >= 0)[:, None] & ((right_n // 1024) == (codes % PANEL)[:, None])
    rows = []
    for rank_number in range(2):
        hit = match & ((right_n // 32) % 32 == rank_number)
        found = jnp.sum(jnp.where(hit, owners[None, :] * 32 + right_n % 32 + 1, 0), axis=1)
        partner = jnp.maximum(found - 1, 0)
        target = (codes // PANEL) * BC + partner % 32
        there = (target[:, None] == c_code[None, :]) & (found > 0)[:, None]
        slot = jnp.sum(jnp.where(there, jnp.arange(KEPT)[None, :] - KEPT, 0), axis=1) + KEPT
        rows += [partner // 32 * HALF + step * BLK, slot]
    return jnp.stack(rows + [jnp.array(row)]).astype(jnp.int32).reshape(5, count)


def moved(array, distance):
    route = []
    for i in range(NQ):
        route.append((2 * i, 2 * ((i + distance) % NQ)))
        route.append((2 * i + 1, 2 * ((i - distance) % NQ) + 1))
    return lax.ppermute(array, COL, route)


def from_other_core(array):
    return lax.ppermute(array, "core", [(0, 1), (1, 0)])


def local(a_own_values, a_own_code, b_own_values, b_own_code, c_code):
    r = lax.axis_index(ROW)
    q = lax.axis_index(("xh", "z"))
    core = lax.axis_index("core")
    start = (r + 2 * q) % 16
    a_own = a_own_values.reshape(16, BLK, BLK)
    b_own = b_own_values.reshape(16, BLK, BLK)

    def note_of(code):
        code = code.reshape(16) + 1
        digits = jnp.concatenate([code // 64, code % 64]).astype(jnp.bfloat16).reshape(1, 32)
        return jnp.pad(digits, ((0, 15), (0, BLK - 32)))

    spans = 2 * q + core + 8 * lax.axis_index("xl") + jnp.arange(SPAN, dtype=jnp.int32)
    b_kept, b_sent = split(jnp.concatenate([spans, spans + 8]) % 16, b_own, note_of(b_own_code))
    b_other = lax.ppermute(b_sent, "xl", [(0, 1), (1, 0)])

    sources, at = [], {}

    def keep(array, names):
        for n, name in enumerate(names):
            at[name] = (len(sources), 2 * n)
        sources.append(array)
        return len(sources) - 1

    def send(array, names, distance):
        return keep(moved(array, distance), [(a, (d + distance) % NQ, k) for a, d, k in names])

    def blocks(names):
        return [(at[name][0], at[name][1] + b) for name in names for b in range(2)]

    def packed(spec, notes=(), after=()):
        return pack(sources, spec, notes, after)

    note = note_of(a_own_code)
    a_other, note_other = from_other_core(a_own), from_other_core(note)
    note = jnp.concatenate([note[:1], note_other[:1], note[2:]])
    a_index = jnp.arange(16, dtype=jnp.int32)
    a_index = (start + jnp.where(core == 0, a_index, 3 - a_index)) % 16

    starts = [
        (items([(3, 0), (4, 0)]), 2),
        (items([(7, 0), (0, 0)]), 14),
        (items([(1, 0), (2, 0)]), 1),
        (items([(5, 0), (6, 0)]), 13),
        ([(4, 0, 0), (5, 0, 0)], 12),
    ]
    orders = tuple(
        tuple((k, 2 * a + b) for a, _, k in names for b in range(2)) for names, _ in starts
    )
    arrays = first_packed(a_index, a_own, a_other, note, orders)
    near = []
    for array, (names, _) in zip(arrays[:4], starts[:4], strict=True):
        own = keep(array, names)
    near.append((own, 8 * BLK, 0, True))
    for array, (names, distance) in zip(arrays[:4], starts[:4], strict=True):
        near.append((send(array, names, distance), 2 * len(names) * BLK, distance, True))

    names = items([(2, 1), (6, 13), (3, 2), (7, 14), (0, 14), (4, 2)])
    right_out = right_packed(b_kept, b_other, arrays[0])
    (up_in,) = packed([(blocks(names), True)], near, (right_out,))
    sources.append(up_in)
    up3 = send(up_in, names, 1)
    right = lax.all_to_all(right_out, "y", 0, 0, tiled=True)
    right = right.reshape(16 * HALF, BLK)
    middle = [(up3 - 1, 24 * BLK, 0, False), (up3, 24 * BLK, 1, False)]

    names = items([(1, 1), (5, 13), (2, 2), (6, 14)])
    (up_in,) = packed([(blocks(names), True)], middle)
    up6 = send(up_in, names, 15)
    across, _ = lax.optimization_barrier((arrays[4], up_in))
    middle.append((send(across, *starts[4]), 4 * BLK, starts[4][1], True))
    far = middle + [(up6, 16 * BLK, 15, False)]

    early = items([(1, 1), (5, 13), (2, 2), (6, 14), (3, 3), (7, 15)]) + [(4, 12, 0)]
    early += items([(2, 1), (6, 13), (3, 2), (7, 14), (0, 15), (4, 3)]) + [(5, 12, 0)]

    def pass_on(names, kept=None, notes=(), after=()):
        entries = [(at[name][0], at[name][1] + b) for name in names for b, _ in passed_on(name)]
        spec = [(entries, bool(notes))]
        if kept:
            spec.append(([(at[name][0], at[name][1] + b) for name in kept for b, _ in wanted(name)], False))
        array, *own_part = packed(spec, notes, after)
        received = from_other_core(array)
        end = len(entries) * BLK
        return received, own_part, (array[end:], received[end:])

    mine = items([(0, 0), (1, 0)]) + early
    early_other, early_own, early_notes = pass_on(early, mine, middle, (up_in,))

    names = items([(1, 16), (5, 4), (2, 17), (6, 5), (0, 15), (4, 3)])
    up_in, notes = packed([(blocks(names), False), ((), True)], far)
    send(up_in, names, 1)
    notes = (notes, from_other_core(notes))

    middle = items([(1, 16), (5, 4), (2, 17), (6, 5)])
    last = items([(1, 17), (5, 5), (2, 18), (6, 6), (0, 16), (4, 4)])

    def part_of(names):
        by_source = {}
        for name in names:
            source, place = at[name]
            for b, panel in wanted(name):
                by_source.setdefault(source, []).append(((place + b) * BLK, 0, name[2], name[1], panel))
        return [(sources[source], rows) for source, rows in sorted(by_source.items())]

    def received_of(array, names):
        rows = []
        for name in names:
            for _, panel in passed_on(name):
                rows.append((len(rows) * BLK, 1, name[2], name[1], panel))
        return [(array, rows)]

    panels = (start + core + jnp.arange(STEPS, dtype=jnp.int32)) % 16
    digits = right.reshape(16, HALF, BLK)[:, STEPS * BLK, :32].astype(jnp.int32)
    right_codes = (digits[:, :16] * 64 + digits[:, 16:] - 1)[:, None, :]
    right_codes = jnp.sum(
        jnp.where(panels[:, None] == jnp.arange(16)[None, :], right_codes, 0), axis=2
    )
    c_code = c_code.reshape(KEPT)

    def table_of(parts, notes):
        order = [row for part in parts for _, rows in part for row in rows]
        return tables(order, notes, right_codes, c_code, start, core)

    def product_of(table, part, base, before=None, last=False):
        lefts, counts = [array for array, _ in part], tuple(len(rows) for _, rows in part)
        return product(table, right, lefts, counts, base, before, last), base + sum(counts)

    rows = []
    for name in mine:
        rows += [(len(rows) * BLK + n * BLK, 0, name[2], name[1], w) for n, (_, w) in enumerate(wanted(name))]
    part = [(early_own[0], rows)] + received_of(early_other, early)
    sums, _ = product_of(table_of((part,), early_notes), part, 0)
    middle_other, _, _ = pass_on(middle, None, (), (early_other,))
    parts = [part_of(middle) + received_of(middle_other, middle), part_of(last), received_of(None, last)]
    table = table_of(parts, notes)
    sums, base = product_of(table, parts[0], 0, sums)
    last_other, _, _ = pass_on(last, None, (), (sums,))
    sums, base = product_of(table, parts[1], base, sums)
    out, _ = product_of(table, received_of(last_other, last), base, sums, last=True)
    return out[None, None]


def solution(mesh):
    fine = Mesh(mesh.devices.reshape(SIZES), AXES)
    return jax.shard_map(
        local,
        mesh=fine,
        in_specs=(
            P(ROW, COL, None, None, None, None),
            P(ROW, COL, None, None),
            P(ROW, COL, None, None, None, None),
            P(ROW, COL, None, None),
            P(ROW, COL, None),
        ),
        out_specs=P(ROW, COL, None, None, None),
        check_vma=False,
    )
```

```python
import functools

import jax
import jax.numpy as jnp
import numpy as np
from jax import lax
from jax.experimental import pallas as pl
from jax.experimental.pallas import tpu as pltpu
from jax.sharding import Mesh
from jax.sharding import PartitionSpec as P

AXES = ("xl", "y", "xh", "z", "core")
ROW = ("xl", "y")
COL = ("xh", "z", "core")
SIZES = (2, 8, 2, 12, 2)
NQ = 24
NOTE = 2 * NQ
BC = 16
PANEL = 48
STEPS = 3
KEPT = 12
SPAN = 8 + STEPS - 1
HALF = STEPS * 128 + 16
BLK = 128


def items(pairs):
    return [(a, d, k) for a, d in pairs for k in range(2)]


def wanted(name):
    a, d, _ = name
    return [(0, 0), (1, 1)] if (d - a) % 8 == 0 else [(0, 2)]


def passed_on(name):
    a, d, _ = name
    return [(1, 2)] if (d - a) % 8 == 0 else [(0, 1), (1, 0)]


VMEM = pltpu.VMEM
SMEM_SPEC = pl.BlockSpec(memory_space=pltpu.SMEM)
VMEM_SPEC = pl.BlockSpec(memory_space=pltpu.VMEM)
ANY_SPEC = pl.BlockSpec(memory_space=pl.ANY)
LIMIT = pltpu.CompilerParams(vmem_limit_bytes=16 << 20)


def moves(blocks):
    return pl.CostEstimate(flops=0, bytes_accessed=2 * blocks * BLK * BLK * 2, transcendentals=0)


def rows_shape(rows):
    return jax.ShapeDtypeStruct((rows, BLK), jnp.bfloat16)


def blk(n):
    return pl.ds(n * BLK, BLK)


def first_kernel(orders, index_ref, own_ref, other_ref, note_ref, *rest):
    outs, sems = rest[:-1], rest[-1]
    copies = []
    for out, order in zip(outs, orders, strict=True):
        for n, (other, place) in enumerate(order):
            if not other:
                source = own_ref.at[index_ref[place]]
                copies.append(pltpu.make_async_copy(source, out.at[blk(n)], sems.at[len(copies)]))
    for copy in copies:
        copy.start()
    for out, order in zip(outs, orders, strict=True):
        for n, (other, place) in enumerate(order):
            if other:
                out[blk(n), :] = other_ref[index_ref[place]]
        out[pl.ds(len(order) * BLK, 16), :] = note_ref[...]
    for copy in copies:
        copy.wait()


def first_packed(index, own, other, note, orders):
    count = sum(not k for order in orders for k, _ in order)
    return pl.pallas_call(
        functools.partial(first_kernel, orders),
        out_shape=[rows_shape(len(order) * BLK + 16) for order in orders],
        in_specs=[SMEM_SPEC, ANY_SPEC, VMEM_SPEC, VMEM_SPEC],
        out_specs=[VMEM_SPEC for _ in orders],
        scratch_shapes=[pltpu.SemaphoreType.DMA((count,))],
        compiler_params=LIMIT,
        cost_estimate=moves(sum(len(order) for order in orders)),
    )(index, own, other, note)


def split_kernel(index_ref, src_ref, note_ref, *rest):
    outs, sems = rest[:2], rest[2]
    copies = []
    for half, out in enumerate(outs):
        for n in range(SPAN):
            source = src_ref.at[index_ref[SPAN * half + n]]
            copies.append(pltpu.make_async_copy(source, out.at[blk(n)], sems.at[len(copies)]))
    for copy in copies:
        copy.start()
    for out in outs:
        out[pl.ds(SPAN * BLK, 16), :] = note_ref[...]
    for copy in copies:
        copy.wait()


def split(index, src, note):
    return pl.pallas_call(
        split_kernel,
        out_shape=[rows_shape(SPAN * BLK + 16)] * 2,
        in_specs=[SMEM_SPEC, ANY_SPEC, VMEM_SPEC],
        out_specs=[VMEM_SPEC] * 2,
        scratch_shapes=[pltpu.SemaphoreType.DMA((2 * SPAN,))],
        compiler_params=LIMIT,
        cost_estimate=moves(2 * SPAN),
    )(index, src, note)


def right_kernel(*refs):
    sources, out = refs[:2], refs[-1]
    for n in range(8):
        for half, source in enumerate(sources):
            out[n, pl.ds(half * HALF, STEPS * BLK), :] = source[pl.ds(n * BLK, STEPS * BLK), :]
            note = source[pl.ds(SPAN * BLK, 16), :]
            out[n, pl.ds(half * HALF + STEPS * BLK, 16), :] = note


def right_packed(kept, other, after):
    return pl.pallas_call(
        right_kernel,
        out_shape=jax.ShapeDtypeStruct((8, 2 * HALF, BLK), jnp.bfloat16),
        in_specs=[VMEM_SPEC, VMEM_SPEC, ANY_SPEC],
        out_specs=VMEM_SPEC,
        compiler_params=LIMIT,
        cost_estimate=moves(48),
    )(kept, other, after)


def turned(note, distance):
    if distance == 0:
        return note
    return jnp.concatenate([pltpu.roll(note[n : n + NQ], distance, 0) for n in (0, NQ)])


def pack_kernel(spec, notes, count, *refs):
    sources, outs = refs[:count], refs[-len(spec) :]
    if notes:
        merged = None
        rows = lax.broadcasted_iota(jnp.int32, (NOTE, BLK), 0)
        for source, row, distance, small in notes:
            if small:
                note = sources[source][pl.ds(row, 16), :].astype(jnp.float32)
                other = jnp.where(rows == NQ + distance, note[1:2], 0.0)
                note = jnp.where(rows == distance, note[0:1], other)
            else:
                note = turned(sources[source][pl.ds(row, NOTE), :].astype(jnp.float32), distance)
            merged = note if merged is None else jnp.maximum(merged, note)
        merged = merged.astype(jnp.bfloat16)
    for out, (entries, noted) in zip(outs, spec, strict=True):
        for n, (source, place) in enumerate(entries):
            out[blk(n), :] = sources[source][blk(place), :]
        if noted:
            out[pl.ds(len(entries) * BLK, NOTE), :] = merged


def pack(sources, spec, notes, after):
    used = sorted({e[0] for entries, _ in spec for e in entries} | {n[0] for n in notes})
    where = {source: n for n, source in enumerate(used)}
    spec = tuple((tuple((where[s], n) for s, n in entries), noted) for entries, noted in spec)
    notes = tuple((where[n[0]],) + tuple(n[1:]) for n in notes)
    return pl.pallas_call(
        functools.partial(pack_kernel, spec, notes, len(used)),
        out_shape=[rows_shape(len(entries) * BLK + NOTE * noted) for entries, noted in spec],
        in_specs=[VMEM_SPEC] * len(used) + [ANY_SPEC] * len(after),
        out_specs=[VMEM_SPEC for _ in spec],
        compiler_params=LIMIT,
        cost_estimate=moves(sum(len(entries) for entries, _ in spec)),
    )(*[sources[source] for source in used], *after)


def product_kernel(counts, base, first, last, table_ref, right_ref, *rest):
    lefts, rest = rest[: len(counts)], rest[len(counts) :]
    if last:
        before, out_ref, acc = rest
        acc[...] = before[...]
    elif first:
        (acc,) = rest
        acc[...] = jnp.zeros_like(acc)
    else:
        before, acc = rest
        acc[...] = before[...]
    for left, count in zip(lefts, counts, strict=True):

        def body(n, carry, left=left, base=base):
            block = left[pl.ds(pl.multiple_of(table_ref[4, base + n], BLK), BLK), :]
            pair = []
            for rank in range(2):
                row = pl.multiple_of(table_ref[2 * rank, base + n], 16)
                pair.append(right_ref[pl.ds(row, BLK), :])
            both = jnp.dot(block, jnp.concatenate(pair, axis=1), preferred_element_type=jnp.float32)
            acc[table_ref[1, base + n]] += both[:, :BLK]
            acc[table_ref[3, base + n]] += both[:, BLK:]
            return carry

        unroll = count if count <= 24 else max(n for n in range(1, 17) if count % n == 0)
        lax.fori_loop(0, count, body, 0, unroll=unroll)
        base += count
    if last:
        out_ref[...] = acc[:KEPT].astype(out_ref.dtype)


def product(table, right, lefts, counts, base, before=None, last=False):
    total = sum(counts)
    sums = jax.ShapeDtypeStruct((KEPT + 1, BLK, BLK), jnp.float32)
    return pl.pallas_call(
        functools.partial(product_kernel, counts, base, before is None, last),
        out_shape=jax.ShapeDtypeStruct((KEPT, BLK, BLK), jnp.bfloat16) if last else sums,
        in_specs=[SMEM_SPEC] + [VMEM_SPEC] * (1 + len(lefts) + (before is not None)),
        out_specs=VMEM_SPEC,
        scratch_shapes=[VMEM(sums.shape, jnp.float32)] if last else [],
        compiler_params=LIMIT,
        cost_estimate=pl.CostEstimate(
            flops=total * 16 * BLK**3, bytes_accessed=total * BLK * BLK * 2, transcendentals=0
        ),
    )(table, right, *lefts, *(() if before is None else (before,)))


def tables(order, notes, right_codes, c_code, start, core):
    order = np.array(order, np.int32)
    count = order.shape[0]
    row, other, k, distance, panel = (order[:, n] for n in range(5))
    notes = jnp.stack(notes)[:, :, :32].astype(jnp.int32)
    flat = (notes[:, :, :16] * 64 + notes[:, :, 16:] - 1).reshape(1, 2 * NOTE * 16)
    of = (start + panel + core * (3 - 2 * panel)) % 16
    place = (other * NOTE + k * NQ + distance) * 16 + of
    codes = jnp.sum(jnp.where(place[:, None] == jnp.arange(2 * NOTE * 16)[None, :], flat, 0), axis=1)
    step = panel + core * (2 - 2 * panel)
    right_live = right_codes >= 0
    right_inner = jnp.where(right_live, right_codes // BC, -1)
    owners = jnp.arange(16, dtype=jnp.int32)
    earlier = owners[None, :] < owners[:, None]
    rank = jnp.sum(
        ((right_inner[:, None, :] == right_inner[None, :, :]) & earlier[:, :, None]).astype(jnp.int32),
        axis=1,
    )
    packed = jnp.where(right_live, right_inner * 1024 + rank * 32 + right_codes % BC, -1)
    right_n = jnp.where(
        (step == 0)[:, None],
        packed[None, :, 0],
        jnp.where((step == 1)[:, None], packed[None, :, 1], packed[None, :, 2]),
    )
    match = (right_n >= 0) & (codes >= 0)[:, None] & ((right_n // 1024) == (codes % PANEL)[:, None])
    rows = []
    for rank_number in range(2):
        hit = match & ((right_n // 32) % 32 == rank_number)
        found = jnp.sum(jnp.where(hit, owners[None, :] * 32 + right_n % 32 + 1, 0), axis=1)
        partner = jnp.maximum(found - 1, 0)
        target = (codes // PANEL) * BC + partner % 32
        there = (target[:, None] == c_code[None, :]) & (found > 0)[:, None]
        slot = jnp.sum(jnp.where(there, jnp.arange(KEPT)[None, :] - KEPT, 0), axis=1) + KEPT
        rows += [partner // 32 * HALF + step * BLK, slot]
    return jnp.stack(rows + [jnp.array(row)]).astype(jnp.int32).reshape(5, count)


def moved(array, distance):
    route = []
    for i in range(NQ):
        route.append((2 * i, 2 * ((i + distance) % NQ)))
        route.append((2 * i + 1, 2 * ((i - distance) % NQ) + 1))
    return lax.ppermute(array, COL, route)


def from_other_core(array):
    return lax.ppermute(array, "core", [(0, 1), (1, 0)])


def local(a_own_values, a_own_code, b_own_values, b_own_code, c_code):
    r = lax.axis_index(ROW)
    q = lax.axis_index(("xh", "z"))
    core = lax.axis_index("core")
    start = (r + 2 * q) % 16
    a_own = a_own_values.reshape(16, BLK, BLK)
    b_own = b_own_values.reshape(16, BLK, BLK)

    def note_of(code):
        code = code.reshape(16) + 1
        digits = jnp.concatenate([code // 64, code % 64]).astype(jnp.bfloat16).reshape(1, 32)
        return jnp.pad(digits, ((0, 15), (0, BLK - 32)))

    spans = 2 * q + core + 8 * lax.axis_index("xl") + jnp.arange(SPAN, dtype=jnp.int32)
    b_kept, b_sent = split(jnp.concatenate([spans, spans + 8]) % 16, b_own, note_of(b_own_code))
    b_other = lax.ppermute(b_sent, "xl", [(0, 1), (1, 0)])

    sources, at = [], {}

    def keep(array, names):
        for n, name in enumerate(names):
            at[name] = (len(sources), 2 * n)
        sources.append(array)
        return len(sources) - 1

    def send(array, names, distance):
        return keep(moved(array, distance), [(a, (d + distance) % NQ, k) for a, d, k in names])

    def blocks(names):
        return [(at[name][0], at[name][1] + b) for name in names for b in range(2)]

    def packed(spec, notes=(), after=()):
        return pack(sources, spec, notes, after)

    note = note_of(a_own_code)
    a_other, note_other = from_other_core(a_own), from_other_core(note)
    note = jnp.concatenate([note[:1], note_other[:1], note[2:]])
    a_index = jnp.arange(16, dtype=jnp.int32)
    a_index = (start + jnp.where(core == 0, a_index, 3 - a_index)) % 16

    starts = [
        (items([(3, 0), (4, 0)]), 2),
        (items([(7, 0), (0, 0)]), 14),
        (items([(1, 0), (2, 0)]), 1),
        (items([(5, 0), (6, 0)]), 13),
        ([(4, 0, 0), (5, 0, 0)], 12),
    ]
    orders = tuple(
        tuple((k, 2 * a + b) for a, _, k in names for b in range(2)) for names, _ in starts
    )
    arrays = first_packed(a_index, a_own, a_other, note, orders)
    near = []
    for array, (names, _) in zip(arrays[:4], starts[:4], strict=True):
        own = keep(array, names)
    near.append((own, 8 * BLK, 0, True))
    for array, (names, distance) in zip(arrays[:4], starts[:4], strict=True):
        near.append((send(array, names, distance), 2 * len(names) * BLK, distance, True))

    names = items([(2, 1), (6, 13), (3, 2), (7, 14), (0, 14), (4, 2)])
    right_out = right_packed(b_kept, b_other, arrays[0])
    (up_in,) = packed([(blocks(names), True)], near, (right_out,))
    sources.append(up_in)
    up3 = send(up_in, names, 1)
    right = lax.all_to_all(right_out, "y", 0, 0, tiled=True)
    right = right.reshape(16 * HALF, BLK)
    middle = [(up3 - 1, 24 * BLK, 0, False), (up3, 24 * BLK, 1, False)]

    names = items([(1, 1), (5, 13), (2, 2), (6, 14)])
    (up_in,) = packed([(blocks(names), True)], middle)
    up6 = send(up_in, names, 15)
    across, _ = lax.optimization_barrier((arrays[4], up_in))
    middle.append((send(across, *starts[4]), 4 * BLK, starts[4][1], True))
    far = middle + [(up6, 16 * BLK, 15, False)]

    early = items([(1, 1), (5, 13), (2, 2), (6, 14), (3, 3), (7, 15)]) + [(4, 12, 0)]
    early += items([(2, 1), (6, 13), (3, 2), (7, 14), (0, 15), (4, 3)]) + [(5, 12, 0)]

    def pass_on(names, kept=None, notes=(), after=()):
        entries = [(at[name][0], at[name][1] + b) for name in names for b, _ in passed_on(name)]
        spec = [(entries, bool(notes))]
        if kept:
            spec.append(([(at[name][0], at[name][1] + b) for name in kept for b, _ in wanted(name)], False))
        array, *own_part = packed(spec, notes, after)
        received = from_other_core(array)
        end = len(entries) * BLK
        return received, own_part, (array[end:], received[end:])

    mine = items([(0, 0), (1, 0)]) + early
    early_other, early_own, early_notes = pass_on(early, mine, middle, (up_in,))

    names = items([(1, 16), (5, 4), (2, 17), (6, 5), (0, 15), (4, 3)])
    up_in, notes = packed([(blocks(names), False), ((), True)], far)
    send(up_in, names, 1)
    notes = (notes, from_other_core(notes))

    middle = items([(1, 16), (5, 4), (2, 17), (6, 5)])
    last = items([(1, 17), (5, 5), (2, 18), (6, 6), (0, 16), (4, 4)])

    def part_of(names):
        by_source = {}
        for name in names:
            source, place = at[name]
            for b, panel in wanted(name):
                by_source.setdefault(source, []).append(((place + b) * BLK, 0, name[2], name[1], panel))
        return [(sources[source], rows) for source, rows in sorted(by_source.items())]

    def received_of(array, names):
        rows = []
        for name in names:
            for _, panel in passed_on(name):
                rows.append((len(rows) * BLK, 1, name[2], name[1], panel))
        return [(array, rows)]

    panels = (start + core + jnp.arange(STEPS, dtype=jnp.int32)) % 16
    digits = right.reshape(16, HALF, BLK)[:, STEPS * BLK, :32].astype(jnp.int32)
    right_codes = (digits[:, :16] * 64 + digits[:, 16:] - 1)[:, None, :]
    right_codes = jnp.sum(
        jnp.where(panels[:, None] == jnp.arange(16)[None, :], right_codes, 0), axis=2
    )
    c_code = c_code.reshape(KEPT)

    def table_of(parts, notes):
        order = [row for part in parts for _, rows in part for row in rows]
        return tables(order, notes, right_codes, c_code, start, core)

    def product_of(table, part, base, before=None, last=False):
        lefts, counts = [array for array, _ in part], tuple(len(rows) for _, rows in part)
        return product(table, right, lefts, counts, base, before, last), base + sum(counts)

    rows = []
    for name in mine:
        rows += [(len(rows) * BLK + n * BLK, 0, name[2], name[1], w) for n, (_, w) in enumerate(wanted(name))]
    part = [(early_own[0], rows)] + received_of(early_other, early)
    sums, _ = product_of(table_of((part,), early_notes), part, 0)
    middle_other, _, _ = pass_on(middle, None, (), (early_other,))
    parts = [part_of(middle) + received_of(middle_other, middle), part_of(last), received_of(None, last)]
    table = table_of(parts, notes)
    sums, base = product_of(table, parts[0], 0, sums)
    last_other, _, _ = pass_on(last, None, (), (sums,))
    sums, base = product_of(table, parts[1], base, sums)
    out, _ = product_of(table, received_of(last_other, last), base, sums, last=True)
    return out[None, None]


def solution(mesh):
    fine = Mesh(mesh.devices.reshape(SIZES), AXES)
    return jax.shard_map(
        local,
        mesh=fine,
        in_specs=(
            P(ROW, COL, None, None, None, None),
            P(ROW, COL, None, None),
            P(ROW, COL, None, None, None, None),
            P(ROW, COL, None, None),
            P(ROW, COL, None),
        ),
        out_specs=P(ROW, COL, None, None, None),
        check_vma=False,
    )
```

```python
import functools

import jax
import jax.numpy as jnp
import numpy as np
from jax import lax
from jax.experimental import pallas as pl
from jax.experimental.pallas import tpu as pltpu
from jax.sharding import Mesh
from jax.sharding import PartitionSpec as P

AXES = ("xl", "y", "xh", "z", "core")
ROW = ("xl", "y")
COL = ("xh", "z", "core")
SIZES = (2, 8, 2, 12, 2)
NQ = 24
NOTE = 2 * NQ
BC = 16
PANEL = 48
STEPS = 3
KEPT = 12
SPAN = 8 + STEPS - 1
HALF = STEPS * 128 + 16
BLK = 128


def items(pairs):
    return [(a, d, k) for a, d in pairs for k in range(2)]


def wanted(name):
    a, d, _ = name
    return [(0, 0), (1, 1)] if (d - a) % 8 == 0 else [(0, 2)]


def passed_on(name):
    a, d, _ = name
    return [(1, 2)] if (d - a) % 8 == 0 else [(0, 1), (1, 0)]


VMEM = pltpu.VMEM
SMEM_SPEC = pl.BlockSpec(memory_space=pltpu.SMEM)
VMEM_SPEC = pl.BlockSpec(memory_space=pltpu.VMEM)
ANY_SPEC = pl.BlockSpec(memory_space=pl.ANY)
LIMIT = pltpu.CompilerParams(vmem_limit_bytes=16 << 20)


def moves(blocks):
    return pl.CostEstimate(flops=0, bytes_accessed=2 * blocks * BLK * BLK * 2, transcendentals=0)


def rows_shape(rows):
    return jax.ShapeDtypeStruct((rows, BLK), jnp.bfloat16)


def blk(n):
    return pl.ds(n * BLK, BLK)


def first_kernel(orders, index_ref, own_ref, other_ref, note_ref, *outs):
    for out, order in zip(outs, orders, strict=True):
        for n, (other, place) in enumerate(order):
            out[blk(n), :] = (other_ref if other else own_ref)[index_ref[place]]
        out[pl.ds(len(order) * BLK, 16), :] = note_ref[...]


def first_packed(index, own, other, note, orders):
    return pl.pallas_call(
        functools.partial(first_kernel, orders),
        out_shape=[rows_shape(len(order) * BLK + 16) for order in orders],
        in_specs=[SMEM_SPEC] + [VMEM_SPEC] * 3,
        out_specs=[VMEM_SPEC for _ in orders],
        compiler_params=LIMIT,
        cost_estimate=moves(sum(len(order) for order in orders)),
    )(index, own, other, note)


def split_kernel(index_ref, src_ref, note_ref, *outs):
    for half, out in enumerate(outs):
        for n in range(SPAN):
            out[blk(n), :] = src_ref[index_ref[SPAN * half + n]]
        out[pl.ds(SPAN * BLK, 16), :] = note_ref[...]


def split(index, src, note):
    return pl.pallas_call(
        split_kernel,
        out_shape=[rows_shape(SPAN * BLK + 16)] * 2,
        in_specs=[SMEM_SPEC, VMEM_SPEC, VMEM_SPEC],
        out_specs=[VMEM_SPEC] * 2,
        compiler_params=LIMIT,
        cost_estimate=moves(2 * SPAN),
    )(index, src, note)


def right_kernel(*refs):
    sources, out = refs[:2], refs[-1]
    for n in range(8):
        for half, source in enumerate(sources):
            out[n, pl.ds(half * HALF, STEPS * BLK), :] = source[pl.ds(n * BLK, STEPS * BLK), :]
            note = source[pl.ds(SPAN * BLK, 16), :]
            out[n, pl.ds(half * HALF + STEPS * BLK, 16), :] = note


def right_packed(kept, other, after):
    return pl.pallas_call(
        right_kernel,
        out_shape=jax.ShapeDtypeStruct((8, 2 * HALF, BLK), jnp.bfloat16),
        in_specs=[VMEM_SPEC, VMEM_SPEC, ANY_SPEC],
        out_specs=VMEM_SPEC,
        compiler_params=LIMIT,
        cost_estimate=moves(48),
    )(kept, other, after)


def turned(note, distance):
    if distance == 0:
        return note
    return jnp.concatenate([pltpu.roll(note[n : n + NQ], distance, 0) for n in (0, NQ)])


def pack_kernel(spec, notes, count, *refs):
    sources, outs = refs[:count], refs[-len(spec) :]
    if notes:
        merged = None
        rows = lax.broadcasted_iota(jnp.int32, (NOTE, BLK), 0)
        for source, row, distance, small in notes:
            if small:
                note = sources[source][pl.ds(row, 16), :].astype(jnp.float32)
                other = jnp.where(rows == NQ + distance, note[1:2], 0.0)
                note = jnp.where(rows == distance, note[0:1], other)
            else:
                note = turned(sources[source][pl.ds(row, NOTE), :].astype(jnp.float32), distance)
            merged = note if merged is None else jnp.maximum(merged, note)
        merged = merged.astype(jnp.bfloat16)
    for out, (entries, noted) in zip(outs, spec, strict=True):
        for n, (source, place) in enumerate(entries):
            out[blk(n), :] = sources[source][blk(place), :]
        if noted:
            out[pl.ds(len(entries) * BLK, NOTE), :] = merged


def pack(sources, spec, notes, after):
    used = sorted({e[0] for entries, _ in spec for e in entries} | {n[0] for n in notes})
    where = {source: n for n, source in enumerate(used)}
    spec = tuple((tuple((where[s], n) for s, n in entries), noted) for entries, noted in spec)
    notes = tuple((where[n[0]],) + tuple(n[1:]) for n in notes)
    return pl.pallas_call(
        functools.partial(pack_kernel, spec, notes, len(used)),
        out_shape=[rows_shape(len(entries) * BLK + NOTE * noted) for entries, noted in spec],
        in_specs=[VMEM_SPEC] * len(used) + [ANY_SPEC] * len(after),
        out_specs=[VMEM_SPEC for _ in spec],
        compiler_params=LIMIT,
        cost_estimate=moves(sum(len(entries) for entries, _ in spec)),
    )(*[sources[source] for source in used], *after)


def product_kernel(counts, base, first, last, table_ref, right_ref, *rest):
    lefts, rest = rest[: len(counts)], rest[len(counts) :]
    if last:
        before, out_ref, acc = rest
        acc[...] = before[...]
    elif first:
        (acc,) = rest
        acc[...] = jnp.zeros_like(acc)
    else:
        before, acc = rest
        acc[...] = before[...]
    for left, count in zip(lefts, counts, strict=True):

        def body(n, carry, left=left, base=base):
            block = left[pl.ds(pl.multiple_of(table_ref[4, base + n], BLK), BLK), :]
            pair = []
            for rank in range(2):
                row = pl.multiple_of(table_ref[2 * rank, base + n], 16)
                pair.append(right_ref[pl.ds(row, BLK), :])
            both = jnp.dot(block, jnp.concatenate(pair, axis=1), preferred_element_type=jnp.float32)
            acc[table_ref[1, base + n]] += both[:, :BLK]
            acc[table_ref[3, base + n]] += both[:, BLK:]
            return carry

        unroll = count if count <= 24 else max(n for n in range(1, 17) if count % n == 0)
        lax.fori_loop(0, count, body, 0, unroll=unroll)
        base += count
    if last:
        out_ref[...] = acc[:KEPT].astype(out_ref.dtype)


def product(table, right, lefts, counts, base, before=None, last=False):
    total = sum(counts)
    sums = jax.ShapeDtypeStruct((KEPT + 1, BLK, BLK), jnp.float32)
    return pl.pallas_call(
        functools.partial(product_kernel, counts, base, before is None, last),
        out_shape=jax.ShapeDtypeStruct((KEPT, BLK, BLK), jnp.bfloat16) if last else sums,
        in_specs=[SMEM_SPEC] + [VMEM_SPEC] * (1 + len(lefts) + (before is not None)),
        out_specs=VMEM_SPEC,
        scratch_shapes=[VMEM(sums.shape, jnp.float32)] if last else [],
        compiler_params=LIMIT,
        cost_estimate=pl.CostEstimate(
            flops=total * 16 * BLK**3, bytes_accessed=total * BLK * BLK * 2, transcendentals=0
        ),
    )(table, right, *lefts, *(() if before is None else (before,)))


def tables(order, notes, right_codes, c_code, start, core):
    order = np.array(order, np.int32)
    count = order.shape[0]
    row, other, k, distance, panel = (order[:, n] for n in range(5))
    notes = jnp.stack(notes)[:, :, :32].astype(jnp.int32)
    flat = (notes[:, :, :16] * 64 + notes[:, :, 16:] - 1).reshape(1, 2 * NOTE * 16)
    of = (start + panel + core * (3 - 2 * panel)) % 16
    place = (other * NOTE + k * NQ + distance) * 16 + of
    codes = jnp.sum(jnp.where(place[:, None] == jnp.arange(2 * NOTE * 16)[None, :], flat, 0), axis=1)
    step = panel + core * (2 - 2 * panel)
    right_live = right_codes >= 0
    right_inner = jnp.where(right_live, right_codes // BC, -1)
    owners = jnp.arange(16, dtype=jnp.int32)
    earlier = owners[None, :] < owners[:, None]
    rank = jnp.sum(
        ((right_inner[:, None, :] == right_inner[None, :, :]) & earlier[:, :, None]).astype(jnp.int32),
        axis=1,
    )
    packed = jnp.where(right_live, right_inner * 1024 + rank * 32 + right_codes % BC, -1)
    right_n = jnp.where(
        (step == 0)[:, None],
        packed[None, :, 0],
        jnp.where((step == 1)[:, None], packed[None, :, 1], packed[None, :, 2]),
    )
    match = (right_n >= 0) & (codes >= 0)[:, None] & ((right_n // 1024) == (codes % PANEL)[:, None])
    rows = []
    for rank_number in range(2):
        hit = match & ((right_n // 32) % 32 == rank_number)
        found = jnp.sum(jnp.where(hit, owners[None, :] * 32 + right_n % 32 + 1, 0), axis=1)
        partner = jnp.maximum(found - 1, 0)
        target = (codes // PANEL) * BC + partner % 32
        there = (target[:, None] == c_code[None, :]) & (found > 0)[:, None]
        slot = jnp.sum(jnp.where(there, jnp.arange(KEPT)[None, :] - KEPT, 0), axis=1) + KEPT
        rows += [partner // 32 * HALF + step * BLK, slot]
    return jnp.stack(rows + [jnp.array(row)]).astype(jnp.int32).reshape(5, count)


def moved(array, distance):
    route = []
    for i in range(NQ):
        route.append((2 * i, 2 * ((i + distance) % NQ)))
        route.append((2 * i + 1, 2 * ((i - distance) % NQ) + 1))
    return lax.ppermute(array, COL, route)


def from_other_core(array):
    return lax.ppermute(array, "core", [(0, 1), (1, 0)])


def local(a_own_values, a_own_code, b_own_values, b_own_code, c_code):
    r = lax.axis_index(ROW)
    q = lax.axis_index(("xh", "z"))
    core = lax.axis_index("core")
    start = (r + 2 * q) % 16
    a_own = a_own_values.reshape(16, BLK, BLK)
    b_own = b_own_values.reshape(16, BLK, BLK)

    def note_of(code):
        code = code.reshape(16) + 1
        digits = jnp.concatenate([code // 64, code % 64]).astype(jnp.bfloat16).reshape(1, 32)
        return jnp.pad(digits, ((0, 15), (0, BLK - 32)))

    spans = 2 * q + core + 8 * lax.axis_index("xl") + jnp.arange(SPAN, dtype=jnp.int32)
    b_kept, b_sent = split(jnp.concatenate([spans, spans + 8]) % 16, b_own, note_of(b_own_code))
    b_other = lax.ppermute(b_sent, "xl", [(0, 1), (1, 0)])

    sources, at = [], {}

    def keep(array, names):
        for n, name in enumerate(names):
            at[name] = (len(sources), 2 * n)
        sources.append(array)
        return len(sources) - 1

    def send(array, names, distance):
        return keep(moved(array, distance), [(a, (d + distance) % NQ, k) for a, d, k in names])

    def blocks(names):
        return [(at[name][0], at[name][1] + b) for name in names for b in range(2)]

    def packed(spec, notes=(), after=()):
        return pack(sources, spec, notes, after)

    note = note_of(a_own_code)
    a_other, note_other = from_other_core(a_own), from_other_core(note)
    note = jnp.concatenate([note[:1], note_other[:1], note[2:]])
    a_index = jnp.arange(16, dtype=jnp.int32)
    a_index = (start + jnp.where(core == 0, a_index, 3 - a_index)) % 16

    starts = [
        (items([(3, 0), (4, 0)]), 2),
        (items([(7, 0), (0, 0)]), 14),
        (items([(1, 0), (2, 0)]), 1),
        (items([(5, 0), (6, 0)]), 13),
        ([(4, 0, 0), (5, 0, 0)], 12),
    ]
    orders = tuple(
        tuple((k, 2 * a + b) for a, _, k in names for b in range(2)) for names, _ in starts
    )
    arrays = first_packed(a_index, a_own, a_other, note, orders)
    near = []
    for array, (names, _) in zip(arrays[:4], starts[:4], strict=True):
        own = keep(array, names)
    near.append((own, 8 * BLK, 0, True))
    for array, (names, distance) in zip(arrays[:4], starts[:4], strict=True):
        near.append((send(array, names, distance), 2 * len(names) * BLK, distance, True))

    names = items([(2, 1), (6, 13), (3, 2), (7, 14), (0, 14), (4, 2)])
    (up_in,) = packed([(blocks(names), True)], near, (b_other,))
    sources.append(up_in)
    up3 = send(up_in, names, 1)
    right = lax.all_to_all(right_packed(b_kept, b_other, up_in), "y", 0, 0, tiled=True)
    right = right.reshape(16 * HALF, BLK)
    middle = [(up3 - 1, 24 * BLK, 0, False), (up3, 24 * BLK, 1, False)]

    names = items([(1, 1), (5, 13), (2, 2), (6, 14)])
    (up_in,) = packed([(blocks(names), True)], middle)
    up6 = send(up_in, names, 15)
    across, _ = lax.optimization_barrier((arrays[4], up_in))
    middle.append((send(across, *starts[4]), 4 * BLK, starts[4][1], True))
    far = middle + [(up6, 16 * BLK, 15, False)]

    early = items([(1, 1), (5, 13), (2, 2), (6, 14), (3, 3), (7, 15)]) + [(4, 12, 0)]
    early += items([(2, 1), (6, 13), (3, 2), (7, 14), (0, 15), (4, 3)]) + [(5, 12, 0)]

    def pass_on(names, kept=None, notes=(), after=()):
        entries = [(at[name][0], at[name][1] + b) for name in names for b, _ in passed_on(name)]
        spec = [(entries, bool(notes))]
        if kept:
            spec.append(([(at[name][0], at[name][1] + b) for name in kept for b, _ in wanted(name)], False))
        array, *own_part = packed(spec, notes, after)
        received = from_other_core(array)
        end = len(entries) * BLK
        return received, own_part, (array[end:], received[end:])

    mine = items([(0, 0), (1, 0)]) + early
    early_other, early_own, early_notes = pass_on(early, mine, middle, (up_in,))

    names = items([(1, 16), (5, 4), (2, 17), (6, 5), (0, 15), (4, 3)])
    up_in, notes = packed([(blocks(names), False), ((), True)], far)
    send(up_in, names, 1)
    notes = (notes, from_other_core(notes))

    middle = items([(1, 16), (5, 4), (2, 17), (6, 5)])
    last = items([(1, 17), (5, 5), (2, 18), (6, 6), (0, 16), (4, 4)])

    def part_of(names):
        by_source = {}
        for name in names:
            source, place = at[name]
            for b, panel in wanted(name):
                by_source.setdefault(source, []).append(((place + b) * BLK, 0, name[2], name[1], panel))
        return [(sources[source], rows) for source, rows in sorted(by_source.items())]

    def received_of(array, names):
        rows = []
        for name in names:
            for _, panel in passed_on(name):
                rows.append((len(rows) * BLK, 1, name[2], name[1], panel))
        return [(array, rows)]

    panels = (start + core + jnp.arange(STEPS, dtype=jnp.int32)) % 16
    digits = right.reshape(16, HALF, BLK)[:, STEPS * BLK, :32].astype(jnp.int32)
    right_codes = (digits[:, :16] * 64 + digits[:, 16:] - 1)[:, None, :]
    right_codes = jnp.sum(
        jnp.where(panels[:, None] == jnp.arange(16)[None, :], right_codes, 0), axis=2
    )
    c_code = c_code.reshape(KEPT)

    def table_of(parts, notes):
        order = [row for part in parts for _, rows in part for row in rows]
        return tables(order, notes, right_codes, c_code, start, core)

    def product_of(table, part, base, before=None, last=False):
        lefts, counts = [array for array, _ in part], tuple(len(rows) for _, rows in part)
        return product(table, right, lefts, counts, base, before, last), base + sum(counts)

    rows = []
    for name in mine:
        rows += [(len(rows) * BLK + n * BLK, 0, name[2], name[1], w) for n, (_, w) in enumerate(wanted(name))]
    part = [(early_own[0], rows)] + received_of(early_other, early)
    sums, _ = product_of(table_of((part,), early_notes), part, 0)
    middle_other, _, _ = pass_on(middle, None, (), (early_other,))
    parts = [part_of(middle) + received_of(middle_other, middle), part_of(last), received_of(None, last)]
    table = table_of(parts, notes)
    sums, base = product_of(table, parts[0], 0, sums)
    last_other, _, _ = pass_on(last, None, (), (sums,))
    sums, base = product_of(table, parts[1], base, sums)
    out, _ = product_of(table, received_of(last_other, last), base, sums, last=True)
    return out[None, None]


def solution(mesh):
    fine = Mesh(mesh.devices.reshape(SIZES), AXES)
    return jax.shard_map(
        local,
        mesh=fine,
        in_specs=(
            P(ROW, COL, None, None, None, None),
            P(ROW, COL, None, None),
            P(ROW, COL, None, None, None, None),
            P(ROW, COL, None, None),
            P(ROW, COL, None),
        ),
        out_specs=P(ROW, COL, None, None, None),
        check_vma=False,
    )
```
